32 devices in a mesh: seq: 2 (over y), sp: 16 (over z, x, core).
Axes of the slice: x: 2, y: 2, z: 4, core: 2. Of those that a mesh axis runs over, the one named last changes fastest.
Arguments:
- video: bfloat16 [4, 16, 128, 1152], P('seq', None, 'sp'), may hold values from -6 to 6
- segment_ids: int32 [4, 16], P('seq'), may hold values from 0 to 1, never falling along the last dimension, each value on 1 to 12 neighbouring positions
- timesteps: int32 [4, 2], P('seq'), may hold values from 0 to 999
- drop_mask: int32 [4, 2], P('seq'), may hold values 0 or 1
- captions: bfloat16 [4, 2, 120, 4096], P('seq', None, None, 'sp'), may hold values from -6 to 6
- null_caption: bfloat16 [120, 4096], P(None, 'sp'), may hold values from -6 to 6
- caption_weight: bfloat16 [4096, 1152], P('sp'), may hold values from -0.09375 to 0.09375
- spatial_qkv: bfloat16 [1152, 3456], P('sp'), may hold values from -0.1875 to 0.1875
- spatial_out: bfloat16 [1152, 1152], P('sp'), may hold values from -0.5 to 0.5
- spatial_expand: bfloat16 [1152, 4608], P('sp'), may hold values from -0.1875 to 0.1875
- spatial_shrink: bfloat16 [4608, 1152], P('sp'), may hold values from -0.09375 to 0.09375
- spatial_vectors: bfloat16 [14, 1152], P(None, 'sp'), may hold values from -2.5 to 2.5
- temporal_qkv: bfloat16 [1152, 3456], P('sp'), may hold values from -0.1875 to 0.1875
- temporal_out: bfloat16 [1152, 1152], P('sp'), may hold values from -0.25 to 0.25
- temporal_expand: bfloat16 [1152, 4608], P('sp'), may hold values from -0.1875 to 0.1875
- temporal_shrink: bfloat16 [4608, 1152], P('sp'), may hold values from -0.09375 to 0.09375
- cross_query: bfloat16 [1152, 1152], P('sp'), may hold values from -0.1875 to 0.1875
- cross_keyval: bfloat16 [1152, 2304], P('sp'), may hold values from -0.1875 to 0.1875
- cross_out: bfloat16 [1152, 1152], P('sp'), may hold values from -0.375 to 0.375
- temporal_vectors: bfloat16 [18, 1152], P(None, 'sp'), may hold values from -2.5 to 2.5
- cotangent: bfloat16 [4, 16, 128, 1152], P('seq', None, 'sp'), may hold values from -6 to 6
Outputs:
- layer_output: bfloat16 [4, 16, 128, 1152], P('seq', None, 'sp')
- video_grad: bfloat16 [4, 16, 128, 1152], P('seq', None, 'sp')
- null_caption_grad: float32 [120, 4096], P(None, 'sp')
- caption_weight_grad: float32 [4096, 1152], P('sp')
- spatial_qkv_grad: float32 [1152, 3456], P('sp')
- spatial_out_grad: float32 [1152, 1152], P('sp')
- spatial_expand_grad: float32 [1152, 4608], P('sp')
- spatial_shrink_grad: float32 [4608, 1152], P('sp')
- spatial_vectors_grad: float32 [14, 1152], P(None, 'sp')
- temporal_qkv_grad: float32 [1152, 3456], P('sp')
- temporal_out_grad: float32 [1152, 1152], P('sp')
- temporal_expand_grad: float32 [1152, 4608], P('sp')
- temporal_shrink_grad: float32 [4608, 1152], P('sp')
- cross_query_grad: float32 [1152, 1152], P('sp')
- cross_keyval_grad: float32 [1152, 2304], P('sp')
- cross_out_grad: float32 [1152, 1152], P('sp')
- temporal_vectors_grad: float32 [18, 1152], P(None, 'sp')
The draws below stay inside these ranges and needn't reach their ends.
Inputs may be any that keep to these rules, and one draw needn't show every extreme that they name: `segment_ids`: within a sequence clip numbers never fall along the frames; each of the 2 clips has 1 to 12 frames.
All inputs are finite; a program needn't handle non-finite values. No bound on the sum of `drop_mask` on one device may be relied on, other than what follows from the above.
Results may differ from the reference program's by a relative error of at most 0.03.
Values may be sent and summed in bfloat16 or wider, within the bound.
A program may use at most 384 MiB of HBM per device.

```python
import math
from functools import partial
import jax
import jax.numpy as jnp
import numpy as np
from jax import lax

D = 1152
HEADS = 16
HEAD_DIM = 72
FF = 4608
TEXT = 4096
CAP = 120
FRAMES = 16
CLIPS = 2
MOST = 12
SEQS = 4
PATCHES = 128


def touch_ends(values, key, smallest, largest):
    shape = values.shape
    spot = [jax.random.randint(jax.random.fold_in(key, axis), (), 0, shape[axis]) for axis in range(len(shape))]
    values = values.at[tuple(spot)].set(smallest)
    longest = shape.index(max(shape))
    spot[longest] = (spot[longest] + 1) % shape[longest]
    return values.at[tuple(spot)].set(largest)


def levels(key, dims, shards, low, top_value):
    loudness, own = 1.0, jax.random.fold_in(key, 6)
    for position, shards_of in shards:
        heights = jnp.exp(jax.random.uniform(jax.random.fold_in(own, position), (shards_of,), jnp.float32, low / len(shards), top_value / len(shards)))
        loudness = loudness * jnp.repeat(heights, dims[position] // shards_of).reshape([-1 if axis == position else 1 for axis in range(len(dims))])
    return loudness


def profile(number_of, total, most, slope):
    loads = [(1 << 20) // math.isqrt(rank ** slope) + 1 for rank in range(2, number_of + 1)]
    surplus, holding = total - most - (number_of - 1), [1] * (number_of - 1)
    while surplus > 0:
        candidates = [i for i in range(number_of - 1) if holding[i] < most]
        mass, left = sum([loads[i] for i in candidates]), surplus
        for i in candidates:
            more = min(most - holding[i], max(1, left * loads[i] // mass), surplus)
            holding[i] = holding[i] + more
            surplus = surplus - more
    return np.array([most] + holding)


def ragged(key, count, total, reach, slope):
    if count == 2:
        one = jax.random.randint(key, (), max(1, total - reach), min(reach, total - 1) + 1)
        return jnp.stack([one, total - one])
    tallies = jnp.asarray(profile(count, total, reach, slope), jnp.int32)
    pairs = (count - 1) // 2
    source_of, receiver = tallies[1:1 + 2 * pairs:2], tallies[2:2 + 2 * pairs:2]
    room = jnp.minimum(source_of - 1, reach - receiver)
    passed = jax.random.randint(jax.random.fold_in(key, 1), (pairs,), 0, 1 << 20) % (room + 1)
    tallies = tallies.at[1:1 + 2 * pairs:2].set(source_of - passed).at[2:2 + 2 * pairs:2].set(receiver + passed)
    return tallies[jax.random.permutation(jax.random.fold_in(key, 2), count)]


def scatter_about(rng, dims, spread, most, split=(), held_as=jnp.bfloat16):
    loudness = levels(rng, dims, split, -0.22, 0.18) if split else 1.0
    drawn = jax.random.normal(rng, dims, jnp.float32) * spread * loudness
    return jnp.minimum(jnp.maximum(drawn, -most), most).astype(held_as)


def setup_inputs(seed: int = 0) -> dict:
    streams_of = jax.random.split(jax.random.key(seed), 22)
    video = scatter_about(streams_of[0], (SEQS, FRAMES, PATCHES, D), 1.0, 6.0, ((0, 2), (2, 16)))
    segment_ids = jax.vmap(lambda own: jnp.searchsorted(jnp.cumsum(ragged(own, CLIPS, FRAMES, MOST, 1)), jnp.arange(FRAMES), side="right"))(jax.random.split(streams_of[1], SEQS)).reshape((SEQS, FRAMES)).astype(jnp.int32)
    timesteps = touch_ends(jax.random.randint(streams_of[2], (SEQS, CLIPS), 0, 1000), jax.random.fold_in(streams_of[2], 1), 0, 999).astype(jnp.int32)
    drop_mask = touch_ends((jax.random.randint(streams_of[3], (SEQS, CLIPS), 0, 3) < 1).astype(jnp.int32), jax.random.fold_in(streams_of[3], 1), 0, 1)
    captions = scatter_about(streams_of[4], (SEQS, CLIPS, CAP, TEXT), 1.0, 6.0, ((0, 2), (3, 16)))
    null_caption = scatter_about(streams_of[5], (CAP, TEXT), 1.0, 6.0, ((1, 16),))
    caption_weight = scatter_about(streams_of[6], (TEXT, D), TEXT ** -0.5, 0.09375, ((0, 16),))
    spatial_qkv = scatter_about(streams_of[7], (D, 3 * D), D ** -0.5, 0.1875, ((0, 16),))
    spatial_out = scatter_about(streams_of[8], (D, D), (D // 8) ** -0.5, 0.5, ((0, 16),))
    spatial_expand = scatter_about(streams_of[9], (D, FF), D ** -0.5, 0.1875, ((0, 16),))
    spatial_shrink = scatter_about(streams_of[10], (FF, D), FF ** -0.5, 0.09375, ((0, 16),))
    spatial_vectors = scatter_about(streams_of[11], (14, D), 0.3, 2.5, ((1, 16),))
    temporal_qkv = scatter_about(streams_of[12], (D, 3 * D), D ** -0.5, 0.1875, ((0, 16),))
    temporal_out = scatter_about(streams_of[13], (D, D), (D // 2) ** -0.5, 0.25, ((0, 16),))
    temporal_expand = scatter_about(streams_of[14], (D, FF), D ** -0.5, 0.1875, ((0, 16),))
    temporal_shrink = scatter_about(streams_of[15], (FF, D), FF ** -0.5, 0.09375, ((0, 16),))
    cross_query = scatter_about(streams_of[16], (D, D), D ** -0.5, 0.1875, ((0, 16),))
    cross_keyval = scatter_about(streams_of[17], (D, 2 * D), D ** -0.5, 0.1875, ((0, 16),))
    cross_out = scatter_about(streams_of[18], (D, D), (D // 4) ** -0.5, 0.375, ((0, 16),))
    temporal_vectors = scatter_about(streams_of[19], (18, D), 0.3, 2.5, ((1, 16),))
    cotangent = scatter_about(streams_of[20], (SEQS, FRAMES, PATCHES, D), 1.0, 6.0, ((0, 2), (2, 16)))
    return {"video": video, "segment_ids": segment_ids, "timesteps": timesteps, "drop_mask": drop_mask, "captions": captions, "null_caption": null_caption, "caption_weight": caption_weight, "spatial_qkv": spatial_qkv, "spatial_out": spatial_out, "spatial_expand": spatial_expand, "spatial_shrink": spatial_shrink, "spatial_vectors": spatial_vectors, "temporal_qkv": temporal_qkv, "temporal_out": temporal_out, "temporal_expand": temporal_expand, "temporal_shrink": temporal_shrink, "cross_query": cross_query, "cross_keyval": cross_keyval, "cross_out": cross_out, "temporal_vectors": temporal_vectors, "cotangent": cotangent}


@jax.custom_vjp
def low(v):
    return lax.optimization_barrier(v.astype(jnp.bfloat16)).astype(jnp.float32)

@jax.custom_vjp
def low_back(v):
    return v

def low_keep(v):
    return (low(v), None)

def low_pass(kept, grad):
    return (grad,)

def back_keep(v):
    return (v, None)

def back_low(kept, grad):
    return (low(grad),)
low.defvjp(low_keep, low_pass)
low_back.defvjp(back_keep, back_low)
highest = lax.Precision.HIGHEST
norm_eps = 1e-06
masked_score = -1e+30

def time_features(timestep):
    half_width = 3 * D
    frequency = jnp.exp(jnp.arange(half_width, dtype=jnp.float32) * (-math.log(10000.0) / half_width))
    angles = timestep.astype(jnp.float32)[..., None] * frequency
    return 0.5 * jnp.concatenate([jnp.cos(angles), jnp.sin(angles)], axis=-1)

def layer_norm(residual):
    center = residual - lax.optimization_barrier(jnp.mean(residual, axis=-1, keepdims=True))
    return center * lax.rsqrt(lax.optimization_barrier(jnp.mean(center * center, axis=-1, keepdims=True)) + norm_eps)

def modulate(residual, offset, scaling):
    return layer_norm(residual) * (1.0 + scaling) + offset

def matmul(operand, matrix):
    return jnp.dot(operand, matrix, precision=highest)

def triple_bias(query_bias, value_bias):
    head_query = query_bias.reshape(HEADS, 1, HEAD_DIM)
    head_value = value_bias.reshape(HEADS, 1, HEAD_DIM)
    return jnp.concatenate([head_query, jnp.zeros_like(head_query), head_value], axis=1).reshape(3 * D)

def pair_bias(value_bias):
    head_value = value_bias.reshape(HEADS, 1, HEAD_DIM)
    return jnp.concatenate([jnp.zeros_like(head_value), head_value], axis=1).reshape(2 * D)

def frame_attention(pieces):
    queries, key_rows, value_rows = pieces
    scores = low_back(jnp.einsum('qhe,khe->hqk', queries, key_rows, precision=highest) * HEAD_DIM ** (-0.5))
    attention = low(jax.nn.softmax(scores, axis=-1))
    return jnp.einsum('hqk,khe->qhe', attention, value_rows, precision=highest)

def caption_attention(keyval, pieces):
    queries, allowed = pieces
    scores = low_back(jnp.einsum('phe,rhe->phr', queries, keyval[:, :, 0], precision=highest) * HEAD_DIM ** (-0.5))
    scores = jnp.where(allowed[None, None, :], scores, masked_score)
    attention = low(jax.nn.softmax(scores, axis=-1))
    return jnp.einsum('phr,rhe->phe', attention, keyval[:, :, 1], precision=highest)

def feed_forward(residual, offset, scaling, expand, shrink, vectors, start_row):
    hidden = low(modulate(residual, offset, scaling))
    inner_sum = low_back(matmul(hidden, expand) + vectors[start_row:start_row + 4].reshape(FF))
    active = low(jax.nn.gelu(inner_sum, approximate=True))
    return low_back(matmul(active, shrink) + vectors[3])

def spatial_block(residual, weights, frame_mod):
    qkv_weight, out_weight, expand, shrink, vectors = weights
    modulation = vectors[4:10][None] + frame_mod
    pieces = [modulation[:, number][:, None, :] for number in range(6)]
    hidden = low(modulate(residual, pieces[0], pieces[1]))
    triple = low_back(low(matmul(hidden, qkv_weight) + triple_bias(vectors[0], vectors[1])))
    triple = triple.reshape(FRAMES, PATCHES, HEADS, 3, HEAD_DIM)
    mixture = lax.map(jax.checkpoint(frame_attention), (triple[:, :, :, 0], triple[:, :, :, 1], triple[:, :, :, 2]))
    mixture = low_back(low(mixture)).reshape(FRAMES, PATCHES, D)
    branch = low_back(matmul(mixture, out_weight) + vectors[2])
    residual = residual + pieces[2] * branch
    return residual + pieces[5] * feed_forward(residual, pieces[3], pieces[4], expand, shrink, vectors, 10)

def temporal_block(residual, weights, frame_mod, same_clip, allowed, context):
    qkv_weight, out_weight, expand, shrink, query_weight, keyval_weight, cross_weight, vectors = weights
    modulation = vectors[8:14][None] + frame_mod
    pieces = [modulation[:, number][:, None, :] for number in range(6)]
    hidden = low(modulate(residual, pieces[0], pieces[1]))
    triple = low_back(low(matmul(hidden, qkv_weight) + triple_bias(vectors[0], vectors[1])))
    triple = triple.reshape(FRAMES, PATCHES, HEADS, 3, HEAD_DIM)
    scores = low_back(jnp.einsum('fphe,gphe->phfg', triple[:, :, :, 0], triple[:, :, :, 1], precision=highest) * HEAD_DIM ** (-0.5))
    scores = jnp.where(same_clip[None, None], scores, masked_score)
    attention = low(jax.nn.softmax(scores, axis=-1))
    mixture = jnp.einsum('phfg,gphe->fphe', attention, triple[:, :, :, 2], precision=highest)
    mixture = low_back(low(mixture)).reshape(FRAMES, PATCHES, D)
    branch = low_back(matmul(mixture, out_weight) + vectors[2])
    residual = residual + pieces[2] * branch
    queries = low_back(low(matmul(low(residual), query_weight) + vectors[4])).reshape(FRAMES, PATCHES, HEADS, HEAD_DIM)
    keyval = low_back(low(matmul(context, keyval_weight) + pair_bias(vectors[5]))).reshape(CLIPS * CAP, HEADS, 2, HEAD_DIM)
    crossed = lax.map(jax.checkpoint(partial(caption_attention, keyval)), (queries, allowed))
    crossed = low_back(low(crossed)).reshape(FRAMES, PATCHES, D)
    residual = residual + low_back(matmul(crossed, cross_weight) + vectors[6])
    return residual + pieces[5] * feed_forward(residual, pieces[3], pieces[4], expand, shrink, vectors, 14)

def forward_one(residual, captions_one, dropped, weights, frame_mod, same_clip, allowed):
    text = jnp.where(dropped[:, None, None], weights[0][None], captions_one).reshape(CLIPS * CAP, TEXT)
    context = low_back(low(matmul(text, weights[1]) + weights[14][7]))
    residual = spatial_block(residual, weights[2:7], frame_mod)
    return temporal_block(residual, weights[7:15], frame_mod, same_clip, allowed, context)

def reference(video, segment_ids, timesteps, drop_mask, captions, null_caption, caption_weight, spatial_qkv, spatial_out, spatial_expand, spatial_shrink, spatial_vectors, temporal_qkv, temporal_out, temporal_expand, temporal_shrink, cross_query, cross_keyval, cross_out, temporal_vectors, cotangent):
    params = tuple((member.astype(jnp.float32) for member in (null_caption, caption_weight, spatial_qkv, spatial_out, spatial_expand, spatial_shrink, spatial_vectors, temporal_qkv, temporal_out, temporal_expand, temporal_shrink, cross_query, cross_keyval, cross_out, temporal_vectors)))
    row_clip = jnp.arange(CLIPS * CAP) // CAP

    def one_sequence(totals, inputs):
        residual, segments, stamps, dropped, captions_one, tangent = inputs
        onehot = (segments[:, None] == jnp.arange(CLIPS)[None, :]).astype(jnp.float32)
        frame_mod = matmul(onehot, time_features(stamps)).reshape(FRAMES, 6, D)
        same_clip = segments[:, None] == segments[None, :]
        allowed = segments[:, None] == row_clip[None, :]

        def run_layer(residual_in, weights):
            return forward_one(residual_in, captions_one.astype(jnp.float32), dropped > 0, weights, frame_mod, same_clip, allowed)
        result, pullback = jax.vjp(run_layer, residual.astype(jnp.float32), params)
        residual_grad, weight_grads = pullback(tangent.astype(jnp.float32))
        totals = tuple((total + member for total, member in zip(totals, weight_grads)))
        return (totals, (result.astype(jnp.bfloat16), residual_grad.astype(jnp.bfloat16)))
    initial = tuple((jnp.zeros(member.shape, jnp.float32) for member in params))
    totals, (outputs, gradients) = lax.scan(one_sequence, initial, (video, segment_ids, timesteps, drop_mask, captions, cotangent))
    return (outputs, gradients, totals[0], totals[1], totals[2], totals[3], totals[4], totals[5], totals[6], totals[7], totals[8], totals[9], totals[10], totals[11], totals[12], totals[13], totals[14])
```

```python
import functools
import math

import jax
import jax.numpy as jnp
from jax import lax
from jax.experimental import pallas as pl
from jax.experimental.pallas import tpu as pltpu
from jax.sharding import PartitionSpec as P

D = 1152
HEADS = 16
HEAD_DIM = 72
FF = 4608
CAP = 120
CLIPS = 2


norm_eps = 1e-06
masked_score = -1e30


def time_features(timestep):
    half_width = 3 * D
    frequency = jnp.exp(
        jnp.arange(half_width, dtype=jnp.float32) * (-math.log(10000.0) / half_width)
    )
    angles = timestep.astype(jnp.float32)[..., None] * frequency
    return 0.5 * jnp.concatenate([jnp.cos(angles), jnp.sin(angles)], axis=-1)


def layer_norm(residual):
    center = residual - jnp.mean(residual, axis=-1, keepdims=True)
    return center * lax.rsqrt(jnp.mean(center * center, axis=-1, keepdims=True) + norm_eps)


def modulate(residual, offset, scaling):
    return layer_norm(residual) * (1.0 + scaling) + offset


def gelu_tanh(inner_sum):
    return jax.nn.gelu(inner_sum, approximate=True)


def as_float(member):
    return member.astype(jnp.float32)


def project(inputs, weight):
    return jnp.dot(inputs, weight, preferred_element_type=jnp.float32)


def weight_grad(inputs, gradients):
    left_rows = inputs.reshape(-1, inputs.shape[-1])
    right_rows = gradients.reshape(-1, gradients.shape[-1])
    return lax.dot_general(
        left_rows, right_rows, (((0,), (0,)), ((), ())), preferred_element_type=jnp.float32
    )


def input_grad(gradients, weight):
    return lax.dot_general(
        gradients,
        weight,
        (((gradients.ndim - 1,), (1,)), ((), ())),
        preferred_element_type=jnp.float32,
    )


def column_sum(gradients):
    return jnp.sum(gradients.astype(jnp.float32).reshape(-1, gradients.shape[-1]), axis=0)


def index_bits():
    return lax.axis_size("sp").bit_length() - 1


def swap_sp(values, bit):
    size = lax.axis_size("sp")
    return lax.ppermute(values, "sp", [(i, i ^ (1 << bit)) for i in range(size)])


def swap_seq(values):
    return lax.ppermute(values, "seq", [(0, 1), (1, 0)])


def far_bits():
    return list(range(index_bits() - 1, 1, -1))


def gather_chip_rows(half, seq_first):
    blocks = half[None]
    for bit in far_bits():
        blocks = jnp.concatenate([blocks, swap_sp(blocks, bit)], axis=0)
    if seq_first:
        other = swap_seq(blocks)
        other = jnp.concatenate([other, swap_sp(other, 1)], axis=0)
        blocks = jnp.concatenate([blocks, swap_sp(blocks, 1)], axis=0)
    else:
        blocks = jnp.concatenate([blocks, swap_sp(blocks, 1)], axis=0)
        other = swap_seq(blocks)
    return blocks, other


def place_kernel(bits, moves, n_in, n_out, *refs):
    sources, outs, sems = refs[:n_in], refs[n_in : n_in + n_out], refs[n_in + n_out :]
    local_sem, send_sem, recv_sem = sems
    me = lax.axis_index("sp")
    plane = lax.axis_index("seq")
    sibling = me + 1 - 2 * (me % 2)
    barrier = pltpu.get_barrier_semaphore()
    pl.semaphore_signal(
        barrier, inc=1, device_id=(plane, sibling), device_id_type=pl.DeviceIdType.MESH
    )
    pl.semaphore_wait(barrier, 1)
    count = sources[0].shape[0]

    def block_at(p):
        block = me
        for i, bit in enumerate(bits):
            mine = (me // (1 << bit)) % 2
            block = block + ((p // (1 << i)) % 2) * ((1 << bit) * (1 - 2 * mine))
        return block

    for own_half in (0, 1):

        @pl.when(plane == own_half)
        def _():
            def copies(p):
                block = block_at(p)
                result = []
                for side in (0, 1):
                    half = own_half if side == 0 else 1 - own_half
                    for pair, first, width, out, place in moves[half]:
                        source = sources[2 * pair + side]
                        target = outs[out]
                        if first is None:
                            src, dst = source.at[p], target.at[block, place]
                        else:
                            src = source.at[p, :, pl.ds(first, width)]
                            dst = target.at[block, :, pl.ds(place, width)]
                        k = len(result)
                        result.append(
                            (
                                pltpu.make_async_copy(src, dst, local_sem.at[p, k]),
                                pltpu.make_async_remote_copy(
                                    src_ref=src,
                                    dst_ref=dst,
                                    send_sem=send_sem.at[p, k],
                                    recv_sem=recv_sem.at[p, k],
                                    device_id=(plane, sibling),
                                    device_id_type=pl.DeviceIdType.MESH,
                                ),
                            )
                        )
                return result

            def begin(p, carry):
                for local, remote in copies(p):
                    remote.start()
                    local.start()
                return carry

            def finish(p, carry):
                for local, remote in copies(p):
                    local.wait()
                    remote.wait()
                return carry

            lax.fori_loop(0, count, begin, 0)
            lax.fori_loop(0, count, finish, 0)


def place_blocks(pairs, moves, shapes, collective_id):
    arrays = [member for pair in pairs for member in pair]
    bits = far_bits() + [1]
    count = arrays[0].shape[0]
    copies = len(moves[0]) + len(moves[1])
    any_space = pl.BlockSpec(memory_space=pl.ANY)
    total = sum(2 * math.prod(shape) for shape in shapes)
    return pl.pallas_call(
        functools.partial(place_kernel, bits, moves, len(arrays), len(shapes)),
        out_shape=[jax.ShapeDtypeStruct(shape, jnp.bfloat16) for shape in shapes],
        in_specs=[pl.BlockSpec(memory_space=pltpu.VMEM)] * len(arrays),
        out_specs=[any_space] * len(shapes),
        scratch_shapes=[pltpu.SemaphoreType.DMA((count, copies))] * 3,
        compiler_params=pltpu.CompilerParams(
            collective_id=collective_id, has_side_effects=True, vmem_limit_bytes=32 << 20
        ),
        cost_estimate=pl.CostEstimate(flops=0, bytes_accessed=2 * total, transcendentals=0),
    )(*arrays)


def pick_half(first, second):
    return jnp.where(lax.axis_index("seq") == 0, first, second)


def gather_full(shard):
    return lax.all_gather(shard, "sp", axis=0, tiled=True)


def gather_columns(members, parts, orders, collective_id):
    rows = members[0].shape[0]
    size = lax.axis_size("sp")
    if rows % 8 or lax.axis_size("seq") != 2:
        return [gather_full(member) for member in members]
    pairs, moves = [], ([], [])
    for number, (halves, seq_first) in enumerate(zip(parts, orders)):
        picked = []
        for half, pieces in enumerate(halves):
            columns = [members[w][:, first : first + width] for w, first, width in pieces]
            picked.append(columns[0] if len(columns) == 1 else jnp.concatenate(columns, axis=1))
            place = 0
            for w, first, width in pieces:
                moves[half].append((number, place, width, w, first))
                place += width
        pairs.append(gather_chip_rows(pick_half(*picked), seq_first))
    shapes = [(size, rows, member.shape[1]) for member in members]
    placed = place_blocks(pairs, moves, shapes, collective_id)
    return [full.reshape(size * rows, -1) for full in placed]


def gather_tall(shard, seq_first, collective_id):
    rows, columns = shard.shape
    size = lax.axis_size("sp")
    if rows % 32 or lax.axis_size("seq") != 2:
        return gather_full(shard)
    pair = gather_chip_rows(pick_half(shard[: rows // 2], shard[rows // 2 :]), seq_first)
    moves = ([(0, None, None, 0, 0)], [(0, None, None, 0, 1)])
    shape = (size, 2, rows // 2, columns)
    (full,) = place_blocks([pair], moves, [shape], collective_id)
    return full.reshape(size * rows, columns)


def low_sum(*members):
    total = members[0].astype(jnp.float32)
    for member in members[1:]:
        total = total + member.astype(jnp.float32)
    return total.astype(jnp.bfloat16)


def pick(values, index, axis):
    return lax.dynamic_index_in_dim(values, index, axis, keepdims=False)


def split_blocks(values, bit_value):
    paired = values.reshape(values.shape[0] // 2, 2, *values.shape[1:])
    return pick(paired, 1 - bit_value, 1), pick(paired, bit_value, 1)


def scatter_grad(inputs, gradients, by_rows, seq_first):
    size = lax.axis_size("sp")
    me = lax.axis_index("sp")
    plane = lax.axis_index("seq")
    bits = [(me // (1 << b)) % 2 for b in range(index_bits())]
    left = inputs.reshape(-1, inputs.shape[-1])
    right = gradients.reshape(-1, gradients.shape[-1])
    tokens, depth = left.shape
    columns = right.shape[1]
    rows = depth // size
    half = (rows if by_rows else columns) // 2
    grouped = left.reshape(tokens, size // 2, 2, rows)
    sides = [pick_core(grouped, 1 - bits[0]), pick_core(grouped, bits[0])]
    if by_rows:
        sides = [
            jnp.stack(
                [
                    pick_half(side[:, :, :half], side[:, :, half:]),
                    pick_half(side[:, :, half:], side[:, :, :half]),
                ],
                axis=1,
            )
            for side in sides
        ]
    else:
        padded = -(-half // 128) * 128
        fill = ((0, 0), (0, padded - half))
        right = jnp.concatenate(
            [
                jnp.pad(pick_half(right[:, :half], right[:, half:]), fill),
                jnp.pad(pick_half(right[:, half:], right[:, :half]), fill),
            ],
            axis=1,
        )

    def product(side):
        flat = side.reshape(tokens, depth // 2)
        total = lax.dot_general(
            flat, right, (((0,), (0,)), ((), ())), preferred_element_type=jnp.float32
        ).astype(jnp.bfloat16)
        if by_rows:
            total = total.reshape(2, size // 2, half, columns)
            return total[0], total[1]
        total = total.reshape(size // 2, rows, -1)
        return total

    sent = product(sides[0])
    kept = product(sides[1])
    if by_rows:
        came = [swap_sp(member, 0) for member in sent]
        own, other = (kept[0], came[0]), (kept[1], came[1])
    else:
        came = swap_sp(sent, 0)
        own = (kept[:, :, :padded], came[:, :, :padded])
        other = (kept[:, :, padded:], came[:, :, padded:])
    if seq_first:
        current = (*own, swap_seq(low_sum(*other)))
        current = halve(current, bits[1], 1)
    else:
        own = halve(own, bits[1], 1)
        other = halve(other, bits[1], 1)
        current = (*own, swap_seq(low_sum(*other)))
    for bit in range(2, index_bits()):
        current = halve(current, bits[bit], bit)
    mine = low_sum(*current)[0]
    theirs = swap_seq(mine)
    if not by_rows:
        mine, theirs = mine[:, :half], theirs[:, :half]
    axis = 0 if by_rows else 1
    return pick_half(
        jnp.concatenate([mine, theirs], axis=axis), jnp.concatenate([theirs, mine], axis=axis)
    ).astype(jnp.float32)


def pick_core(grouped, which):
    return jnp.where(which == 0, grouped[:, :, 0], grouped[:, :, 1])


def halve(members, bit_value, bit):
    parts = [split_blocks(member, bit_value) for member in members]
    sent = low_sum(*[part[0] for part in parts])
    return (low_sum(*[part[1] for part in parts]), swap_sp(sent, bit))


def sum_seq(values):
    mine = values.astype(jnp.bfloat16)
    return mine.astype(jnp.float32) + swap_seq(mine).astype(jnp.float32)


def triple_bias(query_bias, value_bias):
    head_query = query_bias.reshape(HEADS, 1, HEAD_DIM)
    head_value = value_bias.reshape(HEADS, 1, HEAD_DIM)
    return jnp.concatenate([head_query, jnp.zeros_like(head_query), head_value], axis=1).reshape(
        3 * D
    )


def pair_bias(value_bias):
    head_value = value_bias.reshape(HEADS, 1, HEAD_DIM)
    return jnp.concatenate([jnp.zeros_like(head_value), head_value], axis=1).reshape(2 * D)


def triple_bias_grad(totals):
    split_rows = totals.reshape(HEADS, 3, HEAD_DIM)
    return (split_rows[:, 0].reshape(D), split_rows[:, 2].reshape(D))


def frame_modulation(segment_ids, timesteps):
    onehot = (segment_ids[:, :, None] == jnp.arange(CLIPS)[None, None, :]).astype(jnp.float32)
    features = time_features(timesteps)
    return jnp.einsum("sfc,scz->sfz", onehot, features, precision=lax.Precision.HIGHEST)


def block_pieces(table_rows, frame_mod):
    modulation = table_rows[None, None] + frame_mod
    return [modulation[:, :, number][:, :, None, :] for number in range(6)]


def gated_back(grad_out, gating, branch):
    branch_grad = (gating * grad_out).astype(jnp.bfloat16)
    gate_grad = jnp.sum(grad_out * branch, axis=2, keepdims=True)
    return (branch_grad, gate_grad)


def to_pairs(values):
    groups, frames, patches, head_count, columns = values.shape
    reordered = jnp.transpose(values, (0, 1, 3, 2, 4))
    return reordered.reshape(lax.axis_size("sp"), -1, patches, columns)


def from_pairs(values, groups, frames):
    devices, pair_count, patches, columns = values.shape
    reordered = values.reshape(groups, frames, -1, patches, columns)
    return jnp.transpose(reordered, (0, 1, 3, 2, 4))


def pair_scores(triple):
    queries = triple[..., :HEAD_DIM]
    key_rows = triple[..., HEAD_DIM : 2 * HEAD_DIM]
    scores = jnp.einsum(
        "zkqe,zkre->zkqr", queries, key_rows, preferred_element_type=jnp.float32
    ) * HEAD_DIM ** (-0.5)
    return jax.nn.softmax(scores, axis=-1)


def attend_pairs(triple):
    attention = pair_scores(triple).astype(jnp.bfloat16)
    mixture = jnp.einsum(
        "zkqr,zkre->zkqe",
        attention,
        triple[..., 2 * HEAD_DIM :],
        preferred_element_type=jnp.float32,
    ).astype(jnp.bfloat16)
    return lax.all_to_all(mixture, "sp", split_axis=2, concat_axis=0, tiled=True)


def pair_backward(members):
    triple, out_grad = members
    queries = triple[..., :HEAD_DIM]
    key_rows = triple[..., HEAD_DIM : 2 * HEAD_DIM]
    value_rows = triple[..., 2 * HEAD_DIM :]
    attention = pair_scores(triple)
    rounded = attention.astype(jnp.bfloat16)
    prob_grad = jnp.einsum(
        "zkqe,zkre->zkqr", out_grad, value_rows, preferred_element_type=jnp.float32
    )
    centre = jnp.sum(prob_grad * attention, axis=-1, keepdims=True)
    score_grad = (attention * (prob_grad - centre)).astype(jnp.bfloat16)
    scaling = HEAD_DIM ** (-0.5)
    query_grad = (
        jnp.einsum("zkqr,zkre->zkqe", score_grad, key_rows, preferred_element_type=jnp.float32)
        * scaling
    )
    key_grad = (
        jnp.einsum("zkqr,zkqe->zkre", score_grad, queries, preferred_element_type=jnp.float32)
        * scaling
    )
    value_grad = jnp.einsum(
        "zkqr,zkqe->zkre", rounded, out_grad, preferred_element_type=jnp.float32
    )
    gradients = jnp.concatenate([query_grad, key_grad, value_grad], axis=-1).astype(jnp.bfloat16)
    return lax.all_to_all(gradients, "sp", split_axis=2, concat_axis=0, tiled=True)


def pair_attention(triple):
    groups, frames, patches = triple.shape[:3]
    shaped = triple.reshape(groups, frames, patches, HEADS, 3 * HEAD_DIM)
    pairs = lax.all_to_all(to_pairs(shaped), "sp", split_axis=0, concat_axis=2, tiled=True)
    exchanged = attend_pairs(pairs)
    return from_pairs(exchanged, groups, frames).reshape(groups, frames, patches, D), pairs


def pair_attention_back(pairs, mixture_grad):
    groups, frames, patches = mixture_grad.shape[:3]
    grad_shaped = mixture_grad.reshape(groups, frames, patches, HEADS, HEAD_DIM)
    returned = pair_backward(
        (
            pairs,
            lax.all_to_all(to_pairs(grad_shaped), "sp", split_axis=0, concat_axis=2, tiled=True),
        )
    )
    return from_pairs(returned, groups, frames).reshape(groups, frames, patches, 3 * D)


def feed_forward(residual, offset, scaling, gating, expand, shrink, vectors, start_row):
    hidden = modulate(residual, offset, scaling).astype(jnp.bfloat16)
    inner_sum = project(hidden, expand) + vectors[start_row : start_row + 4].reshape(FF)
    active = gelu_tanh(inner_sum).astype(jnp.bfloat16)
    branch = project(active, shrink) + vectors[3]
    return ((hidden, inner_sum, active, branch), residual + gating * branch)


def feed_backward(grad_out, residual, offset, scaling, gating, stored, expand, shrink):
    hidden, inner_sum, active, branch = stored
    branch_grad, gate_grad = gated_back(grad_out, gating, branch)
    shrink_grad = scatter_grad(active, branch_grad, True, True)
    active_grad = input_grad(branch_grad, shrink)
    gelu_value, gelu_back = jax.vjp(gelu_tanh, inner_sum)
    inner_grad = gelu_back(active_grad)[0].astype(jnp.bfloat16)
    expand_grad = scatter_grad(hidden, inner_grad, False, False)
    hidden_grad = input_grad(inner_grad, expand)
    norm_value, norm_back = jax.vjp(modulate, residual, offset, scaling)
    residual_grad, offset_grad, scaling_grad = norm_back(hidden_grad)
    return (
        grad_out + residual_grad,
        [offset_grad, scaling_grad, gate_grad],
        (expand_grad, shrink_grad, column_sum(inner_grad), column_sum(branch_grad)),
    )


def table_sums(members):
    return jnp.stack([jnp.sum(member, axis=(0, 1, 2)) for member in members])


def spatial_forward(residual, weights, frame_mod):
    qkv_weight, out_weight, expand, shrink, vectors = weights
    vectors_f = as_float(vectors)
    pieces = block_pieces(vectors_f[4:10], frame_mod)
    hidden = modulate(residual, pieces[0], pieces[1]).astype(jnp.bfloat16)
    triple = (project(hidden, qkv_weight) + triple_bias(vectors_f[0], vectors_f[1])).astype(
        jnp.bfloat16
    )
    mixture, pairs = pair_attention(triple)
    branch = project(mixture, out_weight) + vectors_f[2]
    middle = residual + pieces[2] * branch
    stored_ffn, result = feed_forward(
        middle, pieces[3], pieces[4], pieces[5], expand, shrink, vectors_f, 10
    )
    return (result, (hidden, pairs, mixture, branch, middle, stored_ffn))


def spatial_backward(grad_out, residual, weights, frame_mod, stored):
    qkv_weight, out_weight, expand, shrink, vectors = weights
    pieces = block_pieces(as_float(vectors)[4:10], frame_mod)
    hidden, pairs, mixture, branch, middle, stored_ffn = stored
    middle_grad, ffn_table, ffn_grads = feed_backward(
        grad_out, middle, pieces[3], pieces[4], pieces[5], stored_ffn, expand, shrink
    )
    branch_grad, gate_grad = gated_back(middle_grad, pieces[2], branch)
    out_weight_grad = scatter_grad(mixture, branch_grad, False, True)
    out_bias = column_sum(branch_grad)
    mixture_grad = input_grad(branch_grad, out_weight).astype(jnp.bfloat16)
    triple_grad = pair_attention_back(pairs, mixture_grad)
    qkv_grad = jnp.concatenate(
        [
            scatter_grad(hidden, triple_grad[..., : 3 * D // 2], False, True),
            scatter_grad(hidden, triple_grad[..., 3 * D // 2 :], False, False),
        ],
        axis=1,
    )
    query_bias, value_bias = triple_bias_grad(column_sum(triple_grad))
    hidden_grad = input_grad(triple_grad, qkv_weight)
    norm_value, norm_back = jax.vjp(modulate, residual, pieces[0], pieces[1])
    residual_grad, offset_grad, scaling_grad = norm_back(hidden_grad)
    table_grad = table_sums([offset_grad, scaling_grad, gate_grad] + ffn_table)
    vector_grad = jnp.concatenate(
        [
            jnp.stack([query_bias, value_bias, out_bias, ffn_grads[3]]),
            table_grad,
            ffn_grads[2].reshape(4, D),
        ],
        axis=0,
    )
    return (
        middle_grad + residual_grad,
        (qkv_grad, out_weight_grad, ffn_grads[0], ffn_grads[1], vector_grad),
    )


def temporal_scores(triple, same_clip):
    scores = jnp.einsum(
        "sfphe,sgphe->sphfg",
        triple[..., :HEAD_DIM],
        triple[..., HEAD_DIM : 2 * HEAD_DIM],
        preferred_element_type=jnp.float32,
    ) * HEAD_DIM ** (-0.5)
    return jax.nn.softmax(jnp.where(same_clip, scores, masked_score), axis=-1)


def caption_scores(queries, keyval, allowed):
    scores = jnp.einsum(
        "sfphe,srhe->sfphr", queries, keyval[..., :HEAD_DIM], preferred_element_type=jnp.float32
    ) * HEAD_DIM ** (-0.5)
    return jax.nn.softmax(jnp.where(allowed, scores, masked_score), axis=-1)


def temporal_forward(residual, weights, frame_mod, same_clip, allowed, context):
    qkv_weight, out_weight, expand, shrink, query_weight, keyval_weight, cross_weight, vectors = (
        weights
    )
    vectors_f = as_float(vectors)
    pieces = block_pieces(vectors_f[8:14], frame_mod)
    groups, frames, patches = residual.shape[:3]
    hidden = modulate(residual, pieces[0], pieces[1]).astype(jnp.bfloat16)
    triple = (project(hidden, qkv_weight) + triple_bias(vectors_f[0], vectors_f[1])).astype(
        jnp.bfloat16
    )
    triple = triple.reshape(groups, frames, patches, HEADS, 3 * HEAD_DIM)
    attention = temporal_scores(triple, same_clip).astype(jnp.bfloat16)
    mixture = (
        jnp.einsum(
            "sphfg,sgphe->sfphe",
            attention,
            triple[..., 2 * HEAD_DIM :],
            preferred_element_type=jnp.float32,
        )
        .astype(jnp.bfloat16)
        .reshape(groups, frames, patches, D)
    )
    branch = project(mixture, out_weight) + vectors_f[2]
    middle = residual + pieces[2] * branch
    lowered = middle.astype(jnp.bfloat16)
    queries = (project(lowered, query_weight) + vectors_f[4]).astype(jnp.bfloat16)
    queries = queries.reshape(groups, frames, patches, HEADS, HEAD_DIM)
    keyval = (project(context, keyval_weight) + pair_bias(vectors_f[5])).astype(jnp.bfloat16)
    keyval = keyval.reshape(groups, -1, HEADS, 2 * HEAD_DIM)
    cross_probs = caption_scores(queries, keyval, allowed).astype(jnp.bfloat16)
    cross_mix = (
        jnp.einsum(
            "sfphr,srhe->sfphe",
            cross_probs,
            keyval[..., HEAD_DIM:],
            preferred_element_type=jnp.float32,
        )
        .astype(jnp.bfloat16)
        .reshape(groups, frames, patches, D)
    )
    crossed = middle + project(cross_mix, cross_weight) + vectors_f[6]
    stored_ffn, result = feed_forward(
        crossed, pieces[3], pieces[4], pieces[5], expand, shrink, vectors_f, 14
    )
    return (
        result,
        (
            hidden,
            triple,
            mixture,
            branch,
            middle,
            lowered,
            queries,
            keyval,
            cross_mix,
            crossed,
            stored_ffn,
        ),
    )


def temporal_backward(grad_out, residual, weights, frame_mod, same_clip, allowed, stored):
    qkv_weight, out_weight, expand, shrink, query_weight, keyval_weight, cross_weight, vectors = (
        weights
    )
    pieces = block_pieces(as_float(vectors)[8:14], frame_mod)
    (
        hidden,
        triple,
        mixture,
        branch,
        middle,
        lowered,
        queries,
        keyval,
        cross_mix,
        crossed,
        stored_ffn,
    ) = stored
    groups, frames, patches = residual.shape[:3]
    scaling = HEAD_DIM ** (-0.5)
    crossed_grad, ffn_table, ffn_grads = feed_backward(
        grad_out, crossed, pieces[3], pieces[4], pieces[5], stored_ffn, expand, shrink
    )
    cross_branch_grad = crossed_grad.astype(jnp.bfloat16)
    cross_weight_grad = scatter_grad(cross_mix, cross_branch_grad, False, True)
    cross_bias = column_sum(cross_branch_grad)
    mix_grad = input_grad(cross_branch_grad, cross_weight).astype(jnp.bfloat16)
    mix_grad = mix_grad.reshape(groups, frames, patches, HEADS, HEAD_DIM)
    cross_probs = caption_scores(queries, keyval, allowed)
    rounded = cross_probs.astype(jnp.bfloat16)
    prob_grad = jnp.einsum(
        "sfphe,srhe->sfphr", mix_grad, keyval[..., HEAD_DIM:], preferred_element_type=jnp.float32
    )
    centre = jnp.sum(prob_grad * cross_probs, axis=-1, keepdims=True)
    score_grad = (cross_probs * (prob_grad - centre)).astype(jnp.bfloat16)
    query_grad = (
        jnp.einsum(
            "sfphr,srhe->sfphe",
            score_grad,
            keyval[..., :HEAD_DIM],
            preferred_element_type=jnp.float32,
        )
        * scaling
    )
    query_grad = query_grad.astype(jnp.bfloat16).reshape(groups, frames, patches, D)
    key_grad = (
        jnp.einsum("sfphr,sfphe->srhe", score_grad, queries, preferred_element_type=jnp.float32)
        * scaling
    )
    value_grad = jnp.einsum(
        "sfphr,sfphe->srhe", rounded, mix_grad, preferred_element_type=jnp.float32
    )
    keyval_grad = jnp.concatenate([key_grad, value_grad], axis=-1).reshape(groups, -1, 2 * D)
    keyval_grad = lax.psum(keyval_grad.astype(jnp.bfloat16), "sp")
    query_weight_grad = scatter_grad(lowered, query_grad, False, False)
    cross_query_bias = column_sum(query_grad)
    middle_grad = crossed_grad + input_grad(query_grad, query_weight)
    branch_grad, gate_grad = gated_back(middle_grad, pieces[2], branch)
    out_weight_grad = scatter_grad(mixture, branch_grad, False, True)
    out_bias = column_sum(branch_grad)
    mixture_grad = input_grad(branch_grad, out_weight).astype(jnp.bfloat16)
    mixture_grad = mixture_grad.reshape(groups, frames, patches, HEADS, HEAD_DIM)
    attention = temporal_scores(triple, same_clip)
    rounded_t = attention.astype(jnp.bfloat16)
    prob_grad_t = jnp.einsum(
        "sfphe,sgphe->sphfg",
        mixture_grad,
        triple[..., 2 * HEAD_DIM :],
        preferred_element_type=jnp.float32,
    )
    centre_t = jnp.sum(prob_grad_t * attention, axis=-1, keepdims=True)
    score_grad_t = (attention * (prob_grad_t - centre_t)).astype(jnp.bfloat16)
    query_part = (
        jnp.einsum(
            "sphfg,sgphe->sfphe",
            score_grad_t,
            triple[..., HEAD_DIM : 2 * HEAD_DIM],
            preferred_element_type=jnp.float32,
        )
        * scaling
    )
    key_part = (
        jnp.einsum(
            "sphfg,sfphe->sgphe",
            score_grad_t,
            triple[..., :HEAD_DIM],
            preferred_element_type=jnp.float32,
        )
        * scaling
    )
    value_part = jnp.einsum(
        "sphfg,sfphe->sgphe", rounded_t, mixture_grad, preferred_element_type=jnp.float32
    )
    triple_grad = jnp.concatenate([query_part, key_part, value_part], axis=-1).astype(jnp.bfloat16)
    triple_grad = triple_grad.reshape(groups, frames, patches, 3 * D)
    qkv_grad = scatter_grad(hidden, triple_grad, False, False)
    query_bias, value_bias = triple_bias_grad(column_sum(triple_grad))
    hidden_grad = input_grad(triple_grad, qkv_weight)
    norm_value, norm_back = jax.vjp(modulate, residual, pieces[0], pieces[1])
    residual_grad, offset_grad, scaling_grad = norm_back(hidden_grad)
    table_grad = table_sums([offset_grad, scaling_grad, gate_grad] + ffn_table)
    zero_row = jnp.zeros((D,), jnp.float32)
    vector_grad = jnp.concatenate(
        [
            jnp.stack(
                [
                    query_bias,
                    value_bias,
                    out_bias,
                    ffn_grads[3],
                    cross_query_bias,
                    zero_row,
                    cross_bias,
                    zero_row,
                ]
            ),
            table_grad,
            ffn_grads[2].reshape(4, D),
        ],
        axis=0,
    )
    terms = (
        qkv_grad,
        out_weight_grad,
        ffn_grads[0],
        ffn_grads[1],
        query_weight_grad,
        cross_weight_grad,
        vector_grad,
    )
    return (middle_grad + residual_grad, terms, keyval_grad)


def on_device(
    video,
    segment_ids,
    timesteps,
    drop_mask,
    captions,
    null_caption,
    caption_weight,
    spatial_qkv,
    spatial_out,
    spatial_expand,
    spatial_shrink,
    spatial_vectors,
    temporal_qkv,
    temporal_out,
    temporal_expand,
    temporal_shrink,
    cross_query,
    cross_keyval,
    cross_out,
    temporal_vectors,
    cotangent,
):
    groups, frames, patches = video.shape[:3]
    size = lax.axis_size("sp")
    third = D
    full_sqkv, full_sout = gather_columns(
        [spatial_qkv, spatial_out],
        [
            ([(0, 0, third)], [(0, 2 * third, third)]),
            ([(0, third, third)], [(1, 0, third)]),
        ],
        [False, True],
        0,
    )
    (full_sexp,) = gather_columns(
        [spatial_expand], [([(0, 0, FF // 2)], [(0, FF // 2, FF // 2)])], [False], 1
    )
    full_sshr = gather_tall(spatial_shrink, True, 2)
    full_tqkv, full_tout = gather_columns(
        [temporal_qkv, temporal_out],
        [
            (
                [(0, 0, 2 * third)],
                [(0, 2 * third, third), (1, 0, third)],
            ),
        ],
        [False],
        3,
    )
    full_cq, full_ckv, full_cout = gather_columns(
        [cross_query, cross_keyval, cross_out],
        [
            (
                [(0, 0, third), (1, 0, third)],
                [(1, third, third), (2, 0, third)],
            ),
        ],
        [True],
        4,
    )
    (full_texp,) = gather_columns(
        [temporal_expand], [([(0, 0, FF // 2)], [(0, FF // 2, FF // 2)])], [False], 5
    )
    full_tshr = gather_tall(temporal_shrink, True, 6)
    all_vectors = lax.all_gather(
        jnp.concatenate([spatial_vectors, temporal_vectors], axis=0), "sp", axis=1, tiled=True
    )
    n_spatial = spatial_vectors.shape[0]
    spatial = (full_sqkv, full_sout, full_sexp, full_sshr, all_vectors[:n_spatial])
    temporal = (
        full_tqkv,
        full_tout,
        full_texp,
        full_tshr,
        full_cq,
        full_ckv,
        full_cout,
        all_vectors[n_spatial:],
    )
    dropped = (drop_mask > 0).astype(jnp.float32)
    text_local = jnp.where(drop_mask[:, :, None, None] > 0, null_caption[None, None], captions)
    text_rows = text_local.reshape(groups, CLIPS * CAP, -1)
    caption_sum = lax.psum(project(text_rows, caption_weight), "sp")
    frame_mod = frame_modulation(segment_ids, timesteps).reshape(groups, frames, 6, D)
    same_clip = (segment_ids[:, :, None] == segment_ids[:, None, :])[:, None, None]
    row_clip = jnp.arange(CLIPS * CAP) // CAP
    allowed = (segment_ids[:, :, None] == row_clip[None, None, :])[:, :, None, None, :]
    residual = video.astype(jnp.float32)
    middle, spatial_kept = spatial_forward(residual, spatial, frame_mod)
    context = (caption_sum + as_float(temporal[7])[7]).astype(jnp.bfloat16)
    result, temporal_kept = temporal_forward(
        middle, temporal, frame_mod, same_clip, allowed, context
    )
    output = result.astype(jnp.bfloat16)
    middle_grad, temporal_terms, keyval_grad = temporal_backward(
        cotangent.astype(jnp.float32),
        middle,
        temporal,
        frame_mod,
        same_clip,
        allowed,
        temporal_kept,
    )
    shard_rows = D // lax.axis_size("sp")
    first_row = lax.axis_index("sp") * shard_rows
    context_grad = input_grad(keyval_grad, temporal[5]).astype(jnp.bfloat16)
    local_context = lax.dynamic_slice_in_dim(context, first_row, shard_rows, 2)
    keyval_weight_grad = weight_grad(local_context, keyval_grad)
    value_bias_full = column_sum(keyval_grad).reshape(HEADS, 2, HEAD_DIM)[:, 1].reshape(D)
    caption_bias_full = column_sum(context_grad)
    caption_weight_grad = weight_grad(text_rows, context_grad)
    text_grad = input_grad(context_grad, caption_weight).reshape(groups, CLIPS, CAP, -1)
    null_grad = jnp.sum(text_grad * dropped[:, :, None, None], axis=(0, 1))
    video_grad, spatial_terms = spatial_backward(
        middle_grad, residual, spatial, frame_mod, spatial_kept
    )
    vector_fix = jnp.zeros((18, D), jnp.float32)
    vector_fix = vector_fix.at[5].set(value_bias_full)
    vector_fix = vector_fix.at[7].set(caption_bias_full)
    vector_terms = lax.psum(
        jnp.concatenate([spatial_terms[4], temporal_terms[6]], axis=0), "sp"
    )
    vector_terms = vector_terms + jnp.concatenate(
        [jnp.zeros((n_spatial, D), jnp.float32), vector_fix], axis=0
    )
    vector_total = sum_seq(lax.dynamic_slice_in_dim(vector_terms, first_row, shard_rows, 1))
    return (
        output,
        video_grad.astype(jnp.bfloat16),
        sum_seq(null_grad),
        sum_seq(caption_weight_grad),
        spatial_terms[0],
        spatial_terms[1],
        spatial_terms[2],
        spatial_terms[3],
        vector_total[:n_spatial],
        temporal_terms[0],
        temporal_terms[1],
        temporal_terms[2],
        temporal_terms[3],
        temporal_terms[4],
        sum_seq(keyval_weight_grad),
        temporal_terms[5],
        vector_total[n_spatial:],
    )


def solution(mesh):
    return jax.shard_map(
        on_device,
        mesh=mesh,
        in_specs=(
            P("seq", None, "sp", None),
            P("seq", None),
            P("seq", None),
            P("seq", None),
            P("seq", None, None, "sp"),
            P(None, "sp"),
            P("sp", None),
            P("sp", None),
            P("sp", None),
            P("sp", None),
            P("sp", None),
            P(None, "sp"),
            P("sp", None),
            P("sp", None),
            P("sp", None),
            P("sp", None),
            P("sp", None),
            P("sp", None),
            P("sp", None),
            P(None, "sp"),
            P("seq", None, "sp", None),
        ),
        out_specs=(
            P("seq", None, "sp", None),
            P("seq", None, "sp", None),
            P(None, "sp"),
            P("sp", None),
            P("sp", None),
            P("sp", None),
            P("sp", None),
            P("sp", None),
            P(None, "sp"),
            P("sp", None),
            P("sp", None),
            P("sp", None),
            P("sp", None),
            P("sp", None),
            P("sp", None),
            P("sp", None),
            P(None, "sp"),
        ),
        check_vma=False,
    )
```

```python
import functools
import math

import jax
import jax.numpy as jnp
from jax import lax
from jax.experimental import pallas as pl
from jax.experimental.pallas import tpu as pltpu
from jax.sharding import PartitionSpec as P

D = 1152
HEADS = 16
HEAD_DIM = 72
FF = 4608
CAP = 120
CLIPS = 2


norm_eps = 1e-06
masked_score = -1e30


def time_features(timestep):
    half_width = 3 * D
    frequency = jnp.exp(
        jnp.arange(half_width, dtype=jnp.float32) * (-math.log(10000.0) / half_width)
    )
    angles = timestep.astype(jnp.float32)[..., None] * frequency
    return 0.5 * jnp.concatenate([jnp.cos(angles), jnp.sin(angles)], axis=-1)


def layer_norm(residual):
    center = residual - jnp.mean(residual, axis=-1, keepdims=True)
    return center * lax.rsqrt(jnp.mean(center * center, axis=-1, keepdims=True) + norm_eps)


def modulate(residual, offset, scaling):
    return layer_norm(residual) * (1.0 + scaling) + offset


def gelu_tanh(inner_sum):
    return jax.nn.gelu(inner_sum, approximate=True)


def as_float(member):
    return member.astype(jnp.float32)


def project(inputs, weight):
    return jnp.dot(inputs, weight, preferred_element_type=jnp.float32)


def weight_grad(inputs, gradients):
    left_rows = inputs.reshape(-1, inputs.shape[-1])
    right_rows = gradients.reshape(-1, gradients.shape[-1])
    return lax.dot_general(
        left_rows, right_rows, (((0,), (0,)), ((), ())), preferred_element_type=jnp.float32
    )


def input_grad(gradients, weight):
    return lax.dot_general(
        gradients,
        weight,
        (((gradients.ndim - 1,), (1,)), ((), ())),
        preferred_element_type=jnp.float32,
    )


def column_sum(gradients):
    return jnp.sum(gradients.astype(jnp.float32).reshape(-1, gradients.shape[-1]), axis=0)


def index_bits():
    return lax.axis_size("sp").bit_length() - 1


def after(values, earlier):
    if not earlier:
        return values
    return lax.optimization_barrier((values, tuple(earlier)))[0]


def in_turn(links, key, values, exchange):
    last = links.get(key)
    result = exchange(values if last is None else after(values, [last]))
    links[key] = result
    return result


def swap_sp(values, bit, links):
    size = lax.axis_size("sp")
    pairs = [(i, i ^ (1 << bit)) for i in range(size)]
    return in_turn(links, min(bit, 2), values, lambda v: lax.ppermute(v, "sp", pairs))


def swap_seq(values, links, key="seq"):
    return in_turn(links, key, values, lambda v: lax.ppermute(v, "seq", [(0, 1), (1, 0)]))


def gather_kernel(rounds, n_in, n_out, *refs):
    shards, outs = refs[:n_in], refs[n_in : n_in + n_out]
    local_sem, send_sem, recv_sem = refs[n_in + n_out :]
    me = lax.axis_index("sp")
    plane = lax.axis_index("seq")
    count = index_bits()
    place = [(me // (1 << (count - 1 - d))) % 2 for d in range(count)]

    def flip(bit):
        mine = (me // (1 << bit)) % 2
        return (plane, me + (1 << bit) * (1 - 2 * mine))

    across = (1 - plane, me)
    partners = [flip(bit) for bit in range(count)] + [across]
    barrier = pltpu.get_barrier_semaphore()
    for partner in partners:
        pl.semaphore_signal(
            barrier, inc=1, device_id=partner, device_id_type=pl.DeviceIdType.MESH
        )
    pl.semaphore_wait(barrier, len(partners))

    def part(ref, lead, piece):
        weight, rows, columns = piece
        if rows is None:
            return ref.at[(*lead, slice(None), pl.ds(*columns))]
        half, first, size = rows
        return ref.at[(*lead, half, pl.ds(first, size), slice(None))]

    def stage_places(stage):
        return tuple(
            slice(None) if d < stage else place[d] for d in range(count)
        )

    for own_half in (0, 1):

        @pl.when(plane == own_half)
        def _():
            started = []

            def send(number, stage, slot, source, target, partner):
                copy = pltpu.make_async_remote_copy(
                    src_ref=source,
                    dst_ref=target,
                    send_sem=send_sem.at[number, stage, slot],
                    recv_sem=recv_sem.at[number, stage, slot],
                    device_id=partner,
                    device_id_type=pl.DeviceIdType.MESH,
                )
                copy.start()
                return copy

            def own(chunk):
                return chunk[own_half]

            def other(chunk):
                return chunk[1 - own_half]

            def step(number, stage):
                first, second = rounds[number]
                lead = stage_places(min(stage, count - 2))
                if stage < count - 2:
                    moves = [(own(first), flip(count - 1 - stage)), (own(second), flip(count - 1 - stage))]
                elif stage == count - 2:
                    moves = [(own(first), flip(1)), (own(second), across)]
                elif stage == count - 1:
                    moves = [
                        (own(first), across),
                        (own(second), flip(1)),
                        (other(second), flip(1)),
                    ]
                else:
                    moves = [
                        (piece, flip(0))
                        for chunk in (first, second)
                        for piece in (own(chunk), other(chunk))
                    ]
                copies = []
                for slot, (piece, partner) in enumerate(moves):
                    places = lead
                    if stage == count - 1 and partner is across or stage == count:
                        places = stage_places(count - 1)
                    target = part(outs[piece[0]], places, piece)
                    source = target
                    if stage == 0:
                        source = part(shards[piece[0]], (), piece)
                    copies.append(send(number, stage, slot, source, target, partner))
                return copies

            copies = {}
            local = []
            for number, pair in enumerate(rounds):
                for slot, chunk in enumerate(pair):
                    piece = own(chunk)
                    copy = pltpu.make_async_copy(
                        part(shards[piece[0]], (), piece),
                        part(outs[piece[0]], stage_places(0), piece),
                        local_sem.at[number, slot],
                    )
                    copy.start()
                    local.append(copy)
            lags = list(range(count - 1)) + [count - 1, count + 1]
            for time in range(len(rounds) + lags[-1]):
                for stage, lag in enumerate(lags):
                    number = time - lag
                    if not 0 <= number < len(rounds):
                        continue
                    if stage == 1 and number == 0:
                        for copy in local:
                            copy.wait()
                    if stage:
                        for copy in copies[number, stage - 1]:
                            copy.wait_recv()
                    copies[number, stage] = step(number, stage)
            for number in range(len(rounds)):
                for copy in copies[number, count]:
                    copy.wait_recv()
                for stage in range(count + 1):
                    for copy in copies[number, stage]:
                        copy.wait_send()


def gather_weights(shards, rounds, collective_id):
    size = lax.axis_size("sp")
    lead = (2,) * index_bits()
    shapes = [lead + shard.shape for shard in shards]
    total = sum(2 * math.prod(shape) for shape in shapes)
    stages = index_bits() + 1
    placed = pl.pallas_call(
        functools.partial(gather_kernel, rounds, len(shards), len(shards)),
        out_shape=[jax.ShapeDtypeStruct(shape, jnp.bfloat16) for shape in shapes],
        in_specs=[pl.BlockSpec(memory_space=pltpu.VMEM)] * len(shards),
        out_specs=[pl.BlockSpec(memory_space=pl.ANY)] * len(shards),
        scratch_shapes=[
            pltpu.SemaphoreType.DMA((len(rounds), 2)),
            pltpu.SemaphoreType.DMA((len(rounds), stages, 4)),
            pltpu.SemaphoreType.DMA((len(rounds), stages, 4)),
        ],
        compiler_params=pltpu.CompilerParams(
            collective_id=collective_id, has_side_effects=True, vmem_limit_bytes=32 << 20
        ),
        cost_estimate=pl.CostEstimate(flops=0, bytes_accessed=total, transcendentals=0),
    )(*shards)
    return [full.reshape(size * math.prod(full.shape[index_bits() : -1]), -1) for full in placed]


def columns_round(*quarters):
    pieces = [(weight, None, (first, width)) for weight, first, width in quarters]
    return ((pieces[0], pieces[2]), (pieces[1], pieces[3]))


def rows_round(weight, rows):
    cut = rows // 32 * 16 + (rows // 16 % 2) * 16
    return (
        ((weight, (0, 0, cut), None), (weight, (1, 0, cut), None)),
        ((weight, (0, cut, rows - cut), None), (weight, (1, cut, rows - cut), None)),
    )


def gather_all(tall, wide, rounds_of, collective_id):
    if wide[0].shape[0] % 8 or lax.axis_size("seq") != 2:
        return [lax.all_gather(shard, "sp", axis=0, tiled=True) for shard in wide + tall]
    shards = list(wide) + [
        shard.reshape(2, shard.shape[0] // 2, shard.shape[1]) for shard in tall
    ]
    return gather_weights(shards, rounds_of(tall[0].shape[0] // 2), collective_id)


def pick_half(first, second):
    return jnp.where(lax.axis_index("seq") == 0, first, second)


def low_sum(*members):
    total = members[0].astype(jnp.float32)
    for member in members[1:]:
        total = total + member.astype(jnp.float32)
    return total.astype(jnp.bfloat16)


def pick(values, index, axis):
    return lax.dynamic_index_in_dim(values, index, axis, keepdims=False)


def split_blocks(values, bit_value):
    paired = values.reshape(values.shape[0] // 2, 2, *values.shape[1:])
    return pick(paired, 1 - bit_value, 1), pick(paired, bit_value, 1)


def scatter_grad(inputs, gradients, by_rows, seq_first, links):
    size = lax.axis_size("sp")
    me = lax.axis_index("sp")
    plane = lax.axis_index("seq")
    bits = [(me // (1 << b)) % 2 for b in range(index_bits())]
    left = inputs.reshape(-1, inputs.shape[-1])
    right = gradients.reshape(-1, gradients.shape[-1])
    depth = left.shape[1]
    columns = right.shape[1]
    rows = depth // size
    half = (rows if by_rows else columns) // 2
    if not by_rows:
        padded = -(-half // 128) * 128
        fill = ((0, 0), (0, padded - half))
        right = jnp.concatenate(
            [
                jnp.pad(pick_half(right[:, :half], right[:, half:]), fill),
                jnp.pad(pick_half(right[:, half:], right[:, :half]), fill),
            ],
            axis=1,
        )
    total = lax.dot_general(
        left, right, (((0,), (0,)), ((), ())), preferred_element_type=jnp.float32
    ).astype(jnp.bfloat16)
    if by_rows:
        total = total.reshape(size, 2, half, columns)
    else:
        total = total.reshape(size, rows, 2 * padded)
    sent, kept = split_blocks(total, bits[0])
    came = swap_sp(sent, 0, links)
    if by_rows:
        own, other = [
            (pick(kept, which, 1), pick(came, which, 1)) for which in (plane, 1 - plane)
        ]
    else:
        own = (kept[:, :, :padded], came[:, :, :padded])
        other = (kept[:, :, padded:], came[:, :, padded:])
    if seq_first:
        current = (*own, swap_seq(low_sum(*other), links))
        current = halve(current, bits[1], 1, links)
    else:
        own = halve(own, bits[1], 1, links)
        other = halve(other, bits[1], 1, links)
        current = (*own, swap_seq(low_sum(*other), links))
    for bit in range(2, index_bits()):
        current = halve(current, bits[bit], bit, links)
    mine = low_sum(*current)[0]
    theirs = swap_seq(mine, links, "last")
    if not by_rows:
        mine, theirs = mine[:, :half], theirs[:, :half]
    axis = 0 if by_rows else 1
    return pick_half(
        jnp.concatenate([mine, theirs], axis=axis), jnp.concatenate([theirs, mine], axis=axis)
    ).astype(jnp.float32)


def halve(members, bit_value, bit, links):
    parts = [split_blocks(member, bit_value) for member in members]
    sent = low_sum(*[part[0] for part in parts])
    return (low_sum(*[part[1] for part in parts]), swap_sp(sent, bit, links))


def sum_seq(values):
    mine = values.astype(jnp.bfloat16)
    return mine.astype(jnp.float32) + swap_seq(mine, {}).astype(jnp.float32)


def triple_bias(query_bias, value_bias):
    head_query = query_bias.reshape(HEADS, 1, HEAD_DIM)
    head_value = value_bias.reshape(HEADS, 1, HEAD_DIM)
    return jnp.concatenate([head_query, jnp.zeros_like(head_query), head_value], axis=1).reshape(
        3 * D
    )


def pair_bias(value_bias):
    head_value = value_bias.reshape(HEADS, 1, HEAD_DIM)
    return jnp.concatenate([jnp.zeros_like(head_value), head_value], axis=1).reshape(2 * D)


def triple_bias_grad(totals):
    split_rows = totals.reshape(HEADS, 3, HEAD_DIM)
    return (split_rows[:, 0].reshape(D), split_rows[:, 2].reshape(D))


def frame_modulation(segment_ids, timesteps):
    onehot = (segment_ids[:, :, None] == jnp.arange(CLIPS)[None, None, :]).astype(jnp.float32)
    features = time_features(timesteps)
    return jnp.einsum("sfc,scz->sfz", onehot, features, precision=lax.Precision.HIGHEST)


def block_pieces(table_rows, frame_mod):
    modulation = table_rows[None, None] + frame_mod
    return [modulation[:, :, number][:, :, None, :] for number in range(6)]


def gated_back(grad_out, gating, branch):
    branch_grad = (gating * grad_out).astype(jnp.bfloat16)
    gate_grad = jnp.sum(grad_out * branch, axis=2, keepdims=True)
    return (branch_grad, gate_grad)


def to_pairs(values):
    groups, frames, patches, head_count, columns = values.shape
    reordered = jnp.transpose(values, (0, 1, 3, 2, 4))
    return reordered.reshape(lax.axis_size("sp"), -1, patches, columns)


def from_pairs(values, groups, frames):
    devices, pair_count, patches, columns = values.shape
    reordered = values.reshape(groups, frames, -1, patches, columns)
    return jnp.transpose(reordered, (0, 1, 3, 2, 4))


def pair_scores(triple):
    queries = triple[..., :HEAD_DIM]
    key_rows = triple[..., HEAD_DIM : 2 * HEAD_DIM]
    scores = jnp.einsum(
        "zkqe,zkre->zkqr", queries, key_rows, preferred_element_type=jnp.float32
    ) * HEAD_DIM ** (-0.5)
    return jax.nn.softmax(scores, axis=-1)


def attend_pairs(triple):
    attention = pair_scores(triple).astype(jnp.bfloat16)
    mixture = jnp.einsum(
        "zkqr,zkre->zkqe",
        attention,
        triple[..., 2 * HEAD_DIM :],
        preferred_element_type=jnp.float32,
    ).astype(jnp.bfloat16)
    return lax.all_to_all(mixture, "sp", split_axis=2, concat_axis=0, tiled=True)


def pair_backward(members):
    triple, out_grad = members
    queries = triple[..., :HEAD_DIM]
    key_rows = triple[..., HEAD_DIM : 2 * HEAD_DIM]
    value_rows = triple[..., 2 * HEAD_DIM :]
    attention = pair_scores(triple)
    rounded = attention.astype(jnp.bfloat16)
    prob_grad = jnp.einsum(
        "zkqe,zkre->zkqr", out_grad, value_rows, preferred_element_type=jnp.float32
    )
    centre = jnp.sum(prob_grad * attention, axis=-1, keepdims=True)
    score_grad = (attention * (prob_grad - centre)).astype(jnp.bfloat16)
    scaling = HEAD_DIM ** (-0.5)
    query_grad = (
        jnp.einsum("zkqr,zkre->zkqe", score_grad, key_rows, preferred_element_type=jnp.float32)
        * scaling
    )
    key_grad = (
        jnp.einsum("zkqr,zkqe->zkre", score_grad, queries, preferred_element_type=jnp.float32)
        * scaling
    )
    value_grad = jnp.einsum(
        "zkqr,zkqe->zkre", rounded, out_grad, preferred_element_type=jnp.float32
    )
    gradients = jnp.concatenate([query_grad, key_grad, value_grad], axis=-1).astype(jnp.bfloat16)
    return lax.all_to_all(gradients, "sp", split_axis=2, concat_axis=0, tiled=True)


def pair_attention(triple):
    groups, frames, patches = triple.shape[:3]
    shaped = triple.reshape(groups, frames, patches, HEADS, 3 * HEAD_DIM)
    pairs = lax.all_to_all(to_pairs(shaped), "sp", split_axis=0, concat_axis=2, tiled=True)
    exchanged = attend_pairs(pairs)
    return from_pairs(exchanged, groups, frames).reshape(groups, frames, patches, D), pairs


def pair_attention_back(pairs, mixture_grad):
    groups, frames, patches = mixture_grad.shape[:3]
    grad_shaped = mixture_grad.reshape(groups, frames, patches, HEADS, HEAD_DIM)
    returned = pair_backward(
        (
            pairs,
            lax.all_to_all(to_pairs(grad_shaped), "sp", split_axis=0, concat_axis=2, tiled=True),
        )
    )
    return from_pairs(returned, groups, frames).reshape(groups, frames, patches, 3 * D)


def feed_forward(residual, offset, scaling, gating, expand, shrink, vectors, start_row):
    hidden = modulate(residual, offset, scaling).astype(jnp.bfloat16)
    inner_sum = project(hidden, expand) + vectors[start_row : start_row + 4].reshape(FF)
    active = gelu_tanh(inner_sum).astype(jnp.bfloat16)
    branch = project(active, shrink) + vectors[3]
    return ((hidden, inner_sum, active, branch), residual + gating * branch)


def feed_backward(grad_out, residual, offset, scaling, gating, stored, expand, shrink, links):
    hidden, inner_sum, active, branch = stored
    branch_grad, gate_grad = gated_back(grad_out, gating, branch)
    shrink_grad = scatter_grad(active, branch_grad, True, True, links)
    active_grad = input_grad(branch_grad, shrink)
    gelu_value, gelu_back = jax.vjp(gelu_tanh, inner_sum)
    inner_grad = gelu_back(active_grad)[0].astype(jnp.bfloat16)
    expand_grad = scatter_grad(hidden, inner_grad, False, False, links)
    hidden_grad = input_grad(inner_grad, expand)
    norm_value, norm_back = jax.vjp(modulate, residual, offset, scaling)
    residual_grad, offset_grad, scaling_grad = norm_back(hidden_grad)
    return (
        grad_out + residual_grad,
        [offset_grad, scaling_grad, gate_grad],
        (expand_grad, shrink_grad, column_sum(inner_grad), column_sum(branch_grad)),
    )


def table_sums(members):
    return jnp.stack([jnp.sum(member, axis=(0, 1, 2)) for member in members])


def spatial_forward(residual, weights, frame_mod):
    qkv_weight, out_weight, expand, shrink, vectors = weights
    vectors_f = as_float(vectors)
    pieces = block_pieces(vectors_f[4:10], frame_mod)
    hidden = modulate(residual, pieces[0], pieces[1]).astype(jnp.bfloat16)
    triple = (project(hidden, qkv_weight) + triple_bias(vectors_f[0], vectors_f[1])).astype(
        jnp.bfloat16
    )
    mixture, pairs = pair_attention(triple)
    branch = project(mixture, out_weight) + vectors_f[2]
    middle = residual + pieces[2] * branch
    stored_ffn, result = feed_forward(
        middle, pieces[3], pieces[4], pieces[5], expand, shrink, vectors_f, 10
    )
    return (result, (hidden, pairs, mixture, branch, middle, stored_ffn))


def spatial_backward(grad_out, residual, weights, frame_mod, stored, links):
    qkv_weight, out_weight, expand, shrink, vectors = weights
    pieces = block_pieces(as_float(vectors)[4:10], frame_mod)
    hidden, pairs, mixture, branch, middle, stored_ffn = stored
    middle_grad, ffn_table, ffn_grads = feed_backward(
        grad_out, middle, pieces[3], pieces[4], pieces[5], stored_ffn, expand, shrink, links
    )
    branch_grad, gate_grad = gated_back(middle_grad, pieces[2], branch)
    out_weight_grad = scatter_grad(mixture, branch_grad, False, True, links)
    out_bias = column_sum(branch_grad)
    mixture_grad = input_grad(branch_grad, out_weight).astype(jnp.bfloat16)
    triple_grad = pair_attention_back(pairs, mixture_grad)
    qkv_grad = jnp.concatenate(
        [
            scatter_grad(hidden, triple_grad[..., : 3 * D // 2], False, True, links),
            scatter_grad(hidden, triple_grad[..., 3 * D // 2 :], False, False, links),
        ],
        axis=1,
    )
    query_bias, value_bias = triple_bias_grad(column_sum(triple_grad))
    hidden_grad = input_grad(triple_grad, qkv_weight)
    norm_value, norm_back = jax.vjp(modulate, residual, pieces[0], pieces[1])
    residual_grad, offset_grad, scaling_grad = norm_back(hidden_grad)
    table_grad = table_sums([offset_grad, scaling_grad, gate_grad] + ffn_table)
    vector_grad = jnp.concatenate(
        [
            jnp.stack([query_bias, value_bias, out_bias, ffn_grads[3]]),
            table_grad,
            ffn_grads[2].reshape(4, D),
        ],
        axis=0,
    )
    return (
        middle_grad + residual_grad,
        (qkv_grad, out_weight_grad, ffn_grads[0], ffn_grads[1], vector_grad),
    )


def temporal_scores(triple, same_clip):
    scores = jnp.einsum(
        "sfphe,sgphe->sphfg",
        triple[..., :HEAD_DIM],
        triple[..., HEAD_DIM : 2 * HEAD_DIM],
        preferred_element_type=jnp.float32,
    ) * HEAD_DIM ** (-0.5)
    return jax.nn.softmax(jnp.where(same_clip, scores, masked_score), axis=-1)


def caption_scores(queries, keyval, allowed):
    scores = jnp.einsum(
        "sfphe,srhe->sfphr", queries, keyval[..., :HEAD_DIM], preferred_element_type=jnp.float32
    ) * HEAD_DIM ** (-0.5)
    return jax.nn.softmax(jnp.where(allowed, scores, masked_score), axis=-1)


def temporal_forward(residual, weights, frame_mod, same_clip, allowed, context):
    qkv_weight, out_weight, expand, shrink, query_weight, keyval_weight, cross_weight, vectors = (
        weights
    )
    vectors_f = as_float(vectors)
    pieces = block_pieces(vectors_f[8:14], frame_mod)
    groups, frames, patches = residual.shape[:3]
    hidden = modulate(residual, pieces[0], pieces[1]).astype(jnp.bfloat16)
    triple = (project(hidden, qkv_weight) + triple_bias(vectors_f[0], vectors_f[1])).astype(
        jnp.bfloat16
    )
    triple = triple.reshape(groups, frames, patches, HEADS, 3 * HEAD_DIM)
    attention = temporal_scores(triple, same_clip).astype(jnp.bfloat16)
    mixture = (
        jnp.einsum(
            "sphfg,sgphe->sfphe",
            attention,
            triple[..., 2 * HEAD_DIM :],
            preferred_element_type=jnp.float32,
        )
        .astype(jnp.bfloat16)
        .reshape(groups, frames, patches, D)
    )
    branch = project(mixture, out_weight) + vectors_f[2]
    middle = residual + pieces[2] * branch
    lowered = middle.astype(jnp.bfloat16)
    queries = (project(lowered, query_weight) + vectors_f[4]).astype(jnp.bfloat16)
    queries = queries.reshape(groups, frames, patches, HEADS, HEAD_DIM)
    keyval = (project(context, keyval_weight) + pair_bias(vectors_f[5])).astype(jnp.bfloat16)
    keyval = keyval.reshape(groups, -1, HEADS, 2 * HEAD_DIM)
    cross_probs = caption_scores(queries, keyval, allowed).astype(jnp.bfloat16)
    cross_mix = (
        jnp.einsum(
            "sfphr,srhe->sfphe",
            cross_probs,
            keyval[..., HEAD_DIM:],
            preferred_element_type=jnp.float32,
        )
        .astype(jnp.bfloat16)
        .reshape(groups, frames, patches, D)
    )
    crossed = middle + project(cross_mix, cross_weight) + vectors_f[6]
    stored_ffn, result = feed_forward(
        crossed, pieces[3], pieces[4], pieces[5], expand, shrink, vectors_f, 14
    )
    return (
        result,
        (
            hidden,
            triple,
            mixture,
            branch,
            middle,
            lowered,
            queries,
            keyval,
            cross_mix,
            crossed,
            stored_ffn,
        ),
    )


def temporal_backward(grad_out, residual, weights, frame_mod, same_clip, allowed, stored, links):
    qkv_weight, out_weight, expand, shrink, query_weight, keyval_weight, cross_weight, vectors = (
        weights
    )
    pieces = block_pieces(as_float(vectors)[8:14], frame_mod)
    (
        hidden,
        triple,
        mixture,
        branch,
        middle,
        lowered,
        queries,
        keyval,
        cross_mix,
        crossed,
        stored_ffn,
    ) = stored
    groups, frames, patches = residual.shape[:3]
    scaling = HEAD_DIM ** (-0.5)
    crossed_grad, ffn_table, ffn_grads = feed_backward(
        grad_out, crossed, pieces[3], pieces[4], pieces[5], stored_ffn, expand, shrink, links
    )
    cross_branch_grad = crossed_grad.astype(jnp.bfloat16)
    cross_weight_grad = scatter_grad(cross_mix, cross_branch_grad, False, True, links)
    cross_bias = column_sum(cross_branch_grad)
    mix_grad = input_grad(cross_branch_grad, cross_weight).astype(jnp.bfloat16)
    mix_grad = mix_grad.reshape(groups, frames, patches, HEADS, HEAD_DIM)
    cross_probs = caption_scores(queries, keyval, allowed)
    rounded = cross_probs.astype(jnp.bfloat16)
    prob_grad = jnp.einsum(
        "sfphe,srhe->sfphr", mix_grad, keyval[..., HEAD_DIM:], preferred_element_type=jnp.float32
    )
    centre = jnp.sum(prob_grad * cross_probs, axis=-1, keepdims=True)
    score_grad = (cross_probs * (prob_grad - centre)).astype(jnp.bfloat16)
    query_grad = (
        jnp.einsum(
            "sfphr,srhe->sfphe",
            score_grad,
            keyval[..., :HEAD_DIM],
            preferred_element_type=jnp.float32,
        )
        * scaling
    )
    query_grad = query_grad.astype(jnp.bfloat16).reshape(groups, frames, patches, D)
    key_grad = (
        jnp.einsum("sfphr,sfphe->srhe", score_grad, queries, preferred_element_type=jnp.float32)
        * scaling
    )
    value_grad = jnp.einsum(
        "sfphr,sfphe->srhe", rounded, mix_grad, preferred_element_type=jnp.float32
    )
    keyval_grad = jnp.concatenate([key_grad, value_grad], axis=-1).reshape(groups, -1, 2 * D)
    keyval_grad = lax.psum(keyval_grad.astype(jnp.bfloat16), "sp")
    query_weight_grad = scatter_grad(lowered, query_grad, False, False, links)
    cross_query_bias = column_sum(query_grad)
    middle_grad = crossed_grad + input_grad(query_grad, query_weight)
    branch_grad, gate_grad = gated_back(middle_grad, pieces[2], branch)
    out_weight_grad = scatter_grad(mixture, branch_grad, False, True, links)
    out_bias = column_sum(branch_grad)
    mixture_grad = input_grad(branch_grad, out_weight).astype(jnp.bfloat16)
    mixture_grad = mixture_grad.reshape(groups, frames, patches, HEADS, HEAD_DIM)
    attention = temporal_scores(triple, same_clip)
    rounded_t = attention.astype(jnp.bfloat16)
    prob_grad_t = jnp.einsum(
        "sfphe,sgphe->sphfg",
        mixture_grad,
        triple[..., 2 * HEAD_DIM :],
        preferred_element_type=jnp.float32,
    )
    centre_t = jnp.sum(prob_grad_t * attention, axis=-1, keepdims=True)
    score_grad_t = (attention * (prob_grad_t - centre_t)).astype(jnp.bfloat16)
    query_part = (
        jnp.einsum(
            "sphfg,sgphe->sfphe",
            score_grad_t,
            triple[..., HEAD_DIM : 2 * HEAD_DIM],
            preferred_element_type=jnp.float32,
        )
        * scaling
    )
    key_part = (
        jnp.einsum(
            "sphfg,sfphe->sgphe",
            score_grad_t,
            triple[..., :HEAD_DIM],
            preferred_element_type=jnp.float32,
        )
        * scaling
    )
    value_part = jnp.einsum(
        "sphfg,sfphe->sgphe", rounded_t, mixture_grad, preferred_element_type=jnp.float32
    )
    triple_grad = jnp.concatenate([query_part, key_part, value_part], axis=-1).astype(jnp.bfloat16)
    triple_grad = triple_grad.reshape(groups, frames, patches, 3 * D)
    qkv_grad = scatter_grad(hidden, triple_grad, False, False, links)
    query_bias, value_bias = triple_bias_grad(column_sum(triple_grad))
    hidden_grad = input_grad(triple_grad, qkv_weight)
    norm_value, norm_back = jax.vjp(modulate, residual, pieces[0], pieces[1])
    residual_grad, offset_grad, scaling_grad = norm_back(hidden_grad)
    table_grad = table_sums([offset_grad, scaling_grad, gate_grad] + ffn_table)
    zero_row = jnp.zeros((D,), jnp.float32)
    vector_grad = jnp.concatenate(
        [
            jnp.stack(
                [
                    query_bias,
                    value_bias,
                    out_bias,
                    ffn_grads[3],
                    cross_query_bias,
                    zero_row,
                    cross_bias,
                    zero_row,
                ]
            ),
            table_grad,
            ffn_grads[2].reshape(4, D),
        ],
        axis=0,
    )
    terms = (
        qkv_grad,
        out_weight_grad,
        ffn_grads[0],
        ffn_grads[1],
        query_weight_grad,
        cross_weight_grad,
        vector_grad,
    )
    return (middle_grad + residual_grad, terms, keyval_grad)


def on_device(
    video,
    segment_ids,
    timesteps,
    drop_mask,
    captions,
    null_caption,
    caption_weight,
    spatial_qkv,
    spatial_out,
    spatial_expand,
    spatial_shrink,
    spatial_vectors,
    temporal_qkv,
    temporal_out,
    temporal_expand,
    temporal_shrink,
    cross_query,
    cross_keyval,
    cross_out,
    temporal_vectors,
    cotangent,
):
    groups, frames, patches = video.shape[:3]
    size = lax.axis_size("sp")
    third = D
    wide = [
        spatial_qkv,
        spatial_out,
        spatial_expand,
        temporal_qkv,
        temporal_out,
        cross_query,
        cross_keyval,
        cross_out,
        temporal_expand,
    ]

    def rounds_of(rows):
        def block_round(qkv, out):
            return columns_round(
                (qkv, 0, third), (qkv, third, third), (qkv, 2 * third, third), (out, 0, third)
            )

        def expand_round(weight):
            quarter = FF // 4
            return columns_round(*[(weight, k * quarter, quarter) for k in range(4)])

        return [
            block_round(0, 1),
            expand_round(2),
            rows_round(9, rows),
            block_round(3, 4),
            columns_round((5, 0, third), (6, 0, third), (6, third, third), (7, 0, third)),
            expand_round(8),
            rows_round(10, rows),
        ]

    (
        full_sqkv,
        full_sout,
        full_sexp,
        full_tqkv,
        full_tout,
        full_cq,
        full_ckv,
        full_cout,
        full_texp,
        full_sshr,
        full_tshr,
    ) = gather_all([spatial_shrink, temporal_shrink], wide, rounds_of, 0)
    all_vectors = lax.all_gather(
        jnp.concatenate([spatial_vectors, temporal_vectors], axis=0), "sp", axis=1, tiled=True
    )
    n_spatial = spatial_vectors.shape[0]
    spatial = (full_sqkv, full_sout, full_sexp, full_sshr, all_vectors[:n_spatial])
    temporal = (
        full_tqkv,
        full_tout,
        full_texp,
        full_tshr,
        full_cq,
        full_ckv,
        full_cout,
        all_vectors[n_spatial:],
    )
    dropped = (drop_mask > 0).astype(jnp.float32)
    text_local = jnp.where(drop_mask[:, :, None, None] > 0, null_caption[None, None], captions)
    text_rows = text_local.reshape(groups, CLIPS * CAP, -1)
    caption_sum = lax.psum(project(text_rows, caption_weight), "sp")
    frame_mod = frame_modulation(segment_ids, timesteps).reshape(groups, frames, 6, D)
    same_clip = (segment_ids[:, :, None] == segment_ids[:, None, :])[:, None, None]
    row_clip = jnp.arange(CLIPS * CAP) // CAP
    allowed = (segment_ids[:, :, None] == row_clip[None, None, :])[:, :, None, None, :]
    residual = video.astype(jnp.float32)
    middle, spatial_kept = spatial_forward(residual, spatial, frame_mod)
    context = (caption_sum + as_float(temporal[7])[7]).astype(jnp.bfloat16)
    result, temporal_kept = temporal_forward(
        middle, temporal, frame_mod, same_clip, allowed, context
    )
    output = result.astype(jnp.bfloat16)
    links = {}
    middle_grad, temporal_terms, keyval_grad = temporal_backward(
        cotangent.astype(jnp.float32),
        middle,
        temporal,
        frame_mod,
        same_clip,
        allowed,
        temporal_kept,
        links,
    )
    shard_rows = D // lax.axis_size("sp")
    first_row = lax.axis_index("sp") * shard_rows
    context_grad = input_grad(keyval_grad, temporal[5]).astype(jnp.bfloat16)
    local_context = lax.dynamic_slice_in_dim(context, first_row, shard_rows, 2)
    keyval_weight_grad = weight_grad(local_context, keyval_grad)
    value_bias_full = column_sum(keyval_grad).reshape(HEADS, 2, HEAD_DIM)[:, 1].reshape(D)
    caption_bias_full = column_sum(context_grad)
    caption_weight_grad = weight_grad(text_rows, context_grad)
    text_grad = input_grad(context_grad, caption_weight).reshape(groups, CLIPS, CAP, -1)
    null_grad = jnp.sum(text_grad * dropped[:, :, None, None], axis=(0, 1))
    video_grad, spatial_terms = spatial_backward(
        middle_grad, residual, spatial, frame_mod, spatial_kept, links
    )
    vector_fix = jnp.zeros((18, D), jnp.float32)
    vector_fix = vector_fix.at[5].set(value_bias_full)
    vector_fix = vector_fix.at[7].set(caption_bias_full)
    vector_terms = lax.psum(
        jnp.concatenate([spatial_terms[4], temporal_terms[6]], axis=0), "sp"
    )
    vector_terms = vector_terms + jnp.concatenate(
        [jnp.zeros((n_spatial, D), jnp.float32), vector_fix], axis=0
    )
    vector_total = sum_seq(lax.dynamic_slice_in_dim(vector_terms, first_row, shard_rows, 1))
    return (
        output,
        video_grad.astype(jnp.bfloat16),
        sum_seq(null_grad),
        sum_seq(caption_weight_grad),
        spatial_terms[0],
        spatial_terms[1],
        spatial_terms[2],
        spatial_terms[3],
        vector_total[:n_spatial],
        temporal_terms[0],
        temporal_terms[1],
        temporal_terms[2],
        temporal_terms[3],
        temporal_terms[4],
        sum_seq(keyval_weight_grad),
        temporal_terms[5],
        vector_total[n_spatial:],
    )


def solution(mesh):
    return jax.shard_map(
        on_device,
        mesh=mesh,
        in_specs=(
            P("seq", None, "sp", None),
            P("seq", None),
            P("seq", None),
            P("seq", None),
            P("seq", None, None, "sp"),
            P(None, "sp"),
            P("sp", None),
            P("sp", None),
            P("sp", None),
            P("sp", None),
            P("sp", None),
            P(None, "sp"),
            P("sp", None),
            P("sp", None),
            P("sp", None),
            P("sp", None),
            P("sp", None),
            P("sp", None),
            P("sp", None),
            P(None, "sp"),
            P("seq", None, "sp", None),
        ),
        out_specs=(
            P("seq", None, "sp", None),
            P("seq", None, "sp", None),
            P(None, "sp"),
            P("sp", None),
            P("sp", None),
            P("sp", None),
            P("sp", None),
            P("sp", None),
            P(None, "sp"),
            P("sp", None),
            P("sp", None),
            P("sp", None),
            P("sp", None),
            P("sp", None),
            P("sp", None),
            P("sp", None),
            P(None, "sp"),
        ),
        check_vma=False,
    )
```

```python
import functools
import math

import jax
import jax.numpy as jnp
from jax import lax
from jax.experimental import pallas as pl
from jax.experimental.pallas import tpu as pltpu
from jax.sharding import PartitionSpec as P

D = 1152
HEADS = 16
HEAD_DIM = 72
FF = 4608
CAP = 120
CLIPS = 2


norm_eps = 1e-06
masked_score = -1e30


def time_features(timestep):
    half_width = 3 * D
    frequency = jnp.exp(
        jnp.arange(half_width, dtype=jnp.float32) * (-math.log(10000.0) / half_width)
    )
    angles = timestep.astype(jnp.float32)[..., None] * frequency
    return 0.5 * jnp.concatenate([jnp.cos(angles), jnp.sin(angles)], axis=-1)


def layer_norm(residual):
    center = residual - jnp.mean(residual, axis=-1, keepdims=True)
    return center * lax.rsqrt(jnp.mean(center * center, axis=-1, keepdims=True) + norm_eps)


def modulate(residual, offset, scaling):
    return layer_norm(residual) * (1.0 + scaling) + offset


def gelu_tanh(inner_sum):
    return jax.nn.gelu(inner_sum, approximate=True)


def as_float(member):
    return member.astype(jnp.float32)


def project(inputs, weight):
    return jnp.dot(inputs, weight, preferred_element_type=jnp.float32)


def weight_grad(inputs, gradients):
    left_rows = inputs.reshape(-1, inputs.shape[-1])
    right_rows = gradients.reshape(-1, gradients.shape[-1])
    return lax.dot_general(
        left_rows, right_rows, (((0,), (0,)), ((), ())), preferred_element_type=jnp.float32
    )


def input_grad(gradients, weight):
    return lax.dot_general(
        gradients,
        weight,
        (((gradients.ndim - 1,), (1,)), ((), ())),
        preferred_element_type=jnp.float32,
    )


def column_sum(gradients):
    return jnp.sum(gradients.astype(jnp.float32).reshape(-1, gradients.shape[-1]), axis=0)


def index_bits():
    return lax.axis_size("sp").bit_length() - 1


def after(values, earlier):
    if not earlier:
        return values
    return lax.optimization_barrier((values, tuple(earlier)))[0]


def in_turn(links, key, values, exchange):
    last = links.get(key)
    result = exchange(values if last is None else after(values, [last]))
    links[key] = result
    return result


def swap_sp(values, bit, links):
    size = lax.axis_size("sp")
    pairs = [(i, i ^ (1 << bit)) for i in range(size)]
    return in_turn(links, min(bit, 2), values, lambda v: lax.ppermute(v, "sp", pairs))


def swap_seq(values, links, key="seq"):
    return in_turn(links, key, values, lambda v: lax.ppermute(v, "seq", [(0, 1), (1, 0)]))


def gather_kernel(rounds, n_in, n_out, *refs):
    shards, outs = refs[:n_in], refs[n_in : n_in + n_out]
    local_sem, send_sem, recv_sem, small_local, small_send, small_recv = refs[n_in + n_out :]
    me = lax.axis_index("sp")
    plane = lax.axis_index("seq")
    count = index_bits()
    place = [(me // (1 << (count - 1 - d))) % 2 for d in range(count)]

    def flip(bit):
        mine = (me // (1 << bit)) % 2
        return (plane, me + (1 << bit) * (1 - 2 * mine))

    across = (1 - plane, me)
    partners = [flip(bit) for bit in range(count)] + [across]
    barrier = pltpu.get_barrier_semaphore()
    for partner in partners:
        pl.semaphore_signal(
            barrier, inc=1, device_id=partner, device_id_type=pl.DeviceIdType.MESH
        )
    pl.semaphore_wait(barrier, len(partners))

    def part(ref, lead, piece):
        weight, rows, columns = piece
        if rows is None:
            return ref.at[(*lead, slice(None), pl.ds(*columns))]
        half, first, size = rows
        return ref.at[(*lead, half, pl.ds(first, size), slice(None))]

    def stage_places(stage):
        return tuple(
            slice(None) if d < stage else place[d] for d in range(count)
        )

    for own_half in (0, 1):

        @pl.when(plane == own_half)
        def _():
            started = []

            def send(number, stage, slot, source, target, partner):
                copy = pltpu.make_async_remote_copy(
                    src_ref=source,
                    dst_ref=target,
                    send_sem=send_sem.at[number, stage, slot],
                    recv_sem=recv_sem.at[number, stage, slot],
                    device_id=partner,
                    device_id_type=pl.DeviceIdType.MESH,
                )
                copy.start()
                return copy

            def own(chunk):
                return chunk[own_half]

            def other(chunk):
                return chunk[1 - own_half]

            def step(number, stage):
                first, second = rounds[number]
                lead = stage_places(min(stage, count - 2))
                if stage < count - 2:
                    moves = [(own(first), flip(count - 1 - stage)), (own(second), flip(count - 1 - stage))]
                elif stage == count - 2:
                    moves = [(own(first), flip(1)), (own(second), across)]
                elif stage == count - 1:
                    moves = [
                        (own(first), across),
                        (own(second), flip(1)),
                        (other(second), flip(1)),
                    ]
                else:
                    moves = [
                        (piece, flip(0))
                        for chunk in (first, second)
                        for piece in (own(chunk), other(chunk))
                    ]
                copies = []
                for slot, (piece, partner) in enumerate(moves):
                    places = lead
                    if stage == count - 1 and partner is across or stage == count:
                        places = stage_places(count - 1)
                    target = part(outs[piece[0]], places, piece)
                    source = target
                    if stage == 0:
                        source = part(shards[piece[0]], (), piece)
                    copies.append(send(number, stage, slot, source, target, partner))
                return copies

            def small_step(stage):
                target = outs[-1].at[stage_places(stage)]
                copy = pltpu.make_async_remote_copy(
                    src_ref=target if stage else shards[-1],
                    dst_ref=target,
                    send_sem=small_send.at[stage],
                    recv_sem=small_recv.at[stage],
                    device_id=flip(count - 1 - stage),
                    device_id_type=pl.DeviceIdType.MESH,
                )
                copy.start()
                return copy

            copies = {}
            small = [small_step(0)]
            local = [
                pltpu.make_async_copy(shards[-1], outs[-1].at[stage_places(0)], small_local)
            ]
            local[0].start()
            for number, pair in enumerate(rounds):
                for slot, chunk in enumerate(pair):
                    piece = own(chunk)
                    copy = pltpu.make_async_copy(
                        part(shards[piece[0]], (), piece),
                        part(outs[piece[0]], stage_places(0), piece),
                        local_sem.at[number, slot],
                    )
                    copy.start()
                    local.append(copy)
            lags = list(range(count - 1)) + [count - 1, count + 1]
            for time in range(len(rounds) + lags[-1]):
                for stage, lag in enumerate(lags):
                    number = time - lag
                    if not 0 <= number < len(rounds):
                        continue
                    if stage == 0 and 0 < number < count:
                        if number == 1:
                            for copy in local:
                                copy.wait()
                        small[-1].wait_recv()
                        small.append(small_step(number))
                    if stage:
                        for copy in copies[number, stage - 1]:
                            copy.wait_recv()
                    copies[number, stage] = step(number, stage)
            small[-1].wait_recv()
            for copy in small:
                copy.wait_send()
            for number in range(len(rounds)):
                for copy in copies[number, count]:
                    copy.wait_recv()
                for stage in range(count + 1):
                    for copy in copies[number, stage]:
                        copy.wait_send()


def gather_weights(shards, rounds, collective_id):
    size = lax.axis_size("sp")
    lead = (2,) * index_bits()
    shapes = [lead + shard.shape for shard in shards]
    total = sum(2 * math.prod(shape) for shape in shapes)
    stages = index_bits() + 1
    placed = pl.pallas_call(
        functools.partial(gather_kernel, rounds, len(shards), len(shards)),
        out_shape=[jax.ShapeDtypeStruct(shape, jnp.bfloat16) for shape in shapes],
        in_specs=[pl.BlockSpec(memory_space=pltpu.VMEM)] * len(shards),
        out_specs=[pl.BlockSpec(memory_space=pl.ANY)] * len(shards),
        scratch_shapes=[
            pltpu.SemaphoreType.DMA((len(rounds), 2)),
            pltpu.SemaphoreType.DMA((len(rounds), stages, 4)),
            pltpu.SemaphoreType.DMA((len(rounds), stages, 4)),
            pltpu.SemaphoreType.DMA,
            pltpu.SemaphoreType.DMA((index_bits(),)),
            pltpu.SemaphoreType.DMA((index_bits(),)),
        ],
        compiler_params=pltpu.CompilerParams(
            collective_id=collective_id, has_side_effects=True, vmem_limit_bytes=32 << 20
        ),
        cost_estimate=pl.CostEstimate(flops=0, bytes_accessed=total, transcendentals=0),
    )(*shards)
    *large, small = placed
    full = [member.reshape(size * math.prod(member.shape[index_bits() : -1]), -1) for member in large]
    small = jnp.swapaxes(small.reshape(size, *small.shape[-2:]), 0, 1)
    return full + [small.reshape(small.shape[0], -1)]


def columns_round(*quarters):
    pieces = [(weight, None, (first, width)) for weight, first, width in quarters]
    return ((pieces[0], pieces[2]), (pieces[1], pieces[3]))


def rows_round(weight, rows):
    cut = rows // 32 * 16 + (rows // 16 % 2) * 16
    return (
        ((weight, (0, 0, cut), None), (weight, (1, 0, cut), None)),
        ((weight, (0, cut, rows - cut), None), (weight, (1, cut, rows - cut), None)),
    )


def gather_all(tall, wide, small, rounds_of, collective_id):
    if wide[0].shape[0] % 8 or lax.axis_size("seq") != 2:
        full = [lax.all_gather(shard, "sp", axis=0, tiled=True) for shard in wide + tall]
        return full + [lax.all_gather(small, "sp", axis=1, tiled=True)]
    shards = list(wide) + [
        shard.reshape(2, shard.shape[0] // 2, shard.shape[1]) for shard in tall
    ]
    shards.append(small)
    return gather_weights(shards, rounds_of(tall[0].shape[0] // 2), collective_id)


def pick_half(first, second):
    return jnp.where(lax.axis_index("seq") == 0, first, second)


def low_sum(*members):
    total = members[0].astype(jnp.float32)
    for member in members[1:]:
        total = total + member.astype(jnp.float32)
    return total.astype(jnp.bfloat16)


def pick(values, index, axis):
    return lax.dynamic_index_in_dim(values, index, axis, keepdims=False)


def split_blocks(values, bit_value):
    paired = values.reshape(values.shape[0] // 2, 2, *values.shape[1:])
    return pick(paired, 1 - bit_value, 1), pick(paired, bit_value, 1)


def scatter_grad(inputs, gradients, by_rows, seq_first, links):
    size = lax.axis_size("sp")
    me = lax.axis_index("sp")
    plane = lax.axis_index("seq")
    bits = [(me // (1 << b)) % 2 for b in range(index_bits())]
    left = inputs.reshape(-1, inputs.shape[-1])
    right = gradients.reshape(-1, gradients.shape[-1])
    depth = left.shape[1]
    columns = right.shape[1]
    rows = depth // size
    half = (rows if by_rows else columns) // 2
    if not by_rows:
        padded = -(-half // 128) * 128
        fill = ((0, 0), (0, padded - half))
        right = jnp.concatenate(
            [
                jnp.pad(pick_half(right[:, :half], right[:, half:]), fill),
                jnp.pad(pick_half(right[:, half:], right[:, :half]), fill),
            ],
            axis=1,
        )
    total = lax.dot_general(
        left, right, (((0,), (0,)), ((), ())), preferred_element_type=jnp.float32
    ).astype(jnp.bfloat16)
    if by_rows:
        total = total.reshape(size, 2, half, columns)
    else:
        total = total.reshape(size, rows, 2 * padded)
    sent, kept = split_blocks(total, bits[0])
    came = swap_sp(sent, 0, links)
    if by_rows:
        own, other = [
            (pick(kept, which, 1), pick(came, which, 1)) for which in (plane, 1 - plane)
        ]
    else:
        own = (kept[:, :, :padded], came[:, :, :padded])
        other = (kept[:, :, padded:], came[:, :, padded:])
    if seq_first:
        current = (*own, swap_seq(low_sum(*other), links))
        current = halve(current, bits[1], 1, links)
    else:
        own = halve(own, bits[1], 1, links)
        other = halve(other, bits[1], 1, links)
        current = (*own, swap_seq(low_sum(*other), links))
    for bit in range(2, index_bits()):
        current = halve(current, bits[bit], bit, links)
    mine = low_sum(*current)[0]
    theirs = swap_seq(mine, links, "last")
    if not by_rows:
        mine, theirs = mine[:, :half], theirs[:, :half]
    axis = 0 if by_rows else 1
    return pick_half(
        jnp.concatenate([mine, theirs], axis=axis), jnp.concatenate([theirs, mine], axis=axis)
    ).astype(jnp.float32)


def scatter_kernel(pairs, full_pairs, places, left, right, small, *refs):
    came, out, small_out = refs[:5], refs[5], refs[6]
    scratch = refs[7:]
    left_in, right_in, product, core_send, core_own, loaded = scratch[:6]
    sends, keeps = scratch[6:11], scratch[11:15]
    in_sem, load_sem, out_sem, core_send_sem, core_recv_sem, send_sem, recv_sem = scratch[15:22]
    small_sum, small_came, small_send, small_recv = scratch[22:]
    me = lax.axis_index("sp")
    plane = lax.axis_index("seq")

    def bit_of(bit):
        return (me // (1 << bit)) % 2

    def flip(bit):
        return (plane, me + (1 << bit) * (1 - 2 * bit_of(bit)))

    across = (1 - plane, me)
    core = bit_of(0)
    rows = out.shape[3]
    barrier = pltpu.get_barrier_semaphore()
    partners = [flip(bit) for bit in range(4)] + [across]
    for partner in partners:
        pl.semaphore_signal(
            barrier, inc=1, device_id=partner, device_id_type=pl.DeviceIdType.MESH
        )
    pl.semaphore_wait(barrier, len(partners))

    def remote(source, target, send, recv, partner):
        return pltpu.make_async_remote_copy(
            src_ref=source,
            dst_ref=target,
            send_sem=send,
            recv_sem=recv,
            device_id=partner,
            device_id_type=pl.DeviceIdType.MESH,
        )

    def half_of(side):
        return plane if side == 0 else 1 - plane

    def core_copy(pair, chunk, side):
        number = 2 * chunk + side
        return remote(
            core_send.at[number],
            came[0].at[pair, number],
            core_send_sem.at[number],
            core_recv_sem.at[pair, number],
            flip(0),
        )

    def stage_partner(stage, chunk):
        if stage == 1:
            return across if chunk == 0 else flip(1)
        if stage == 2:
            return flip(1) if chunk == 0 else across
        return flip(2) if stage == 3 else flip(3) if stage == 4 else across

    def stage_copy(stage, pair, chunk):
        source = sends[stage - 1].at[pair % 2, chunk]
        target = out.at[pair, chunk, plane] if stage == 5 else came[stage].at[pair, chunk]
        return remote(
            source,
            target,
            send_sem.at[stage - 1, pair % 2, chunk],
            recv_sem.at[stage - 1, pair, chunk],
            stage_partner(stage, chunk),
        )

    def out_copy(pair, chunk):
        return pltpu.make_async_copy(
            sends[4].at[pair % 2, chunk], out.at[pair, chunk, plane], out_sem.at[pair % 2, chunk]
        )

    def has(pair, chunk):
        return pair < (pairs if chunk == 0 else full_pairs)

    def inputs(pair, chunk, side, slot):
        of_left, of_right = places(pair, 2 * chunk + half_of(side))
        return (
            pltpu.make_async_copy(left.at[of_left], left_in.at[slot], in_sem.at[slot, 0]),
            pltpu.make_async_copy(right.at[of_right], right_in.at[slot], in_sem.at[slot, 1]),
        )

    def start_inputs(pair, chunk, side, slot):
        for copy in inputs(pair, chunk, side, slot):
            copy.start()

    def products(pair):
        start_inputs(pair, 0, 0, 0)
        for chunk in (0, 1):

            @pl.when(has(pair, chunk))
            def _():
                for side in (0, 1):
                    number = 2 * chunk + side

                    if side == 0:
                        start_inputs(pair, chunk, 1, 1)
                    elif chunk == 0:

                        @pl.when(has(pair, 1))
                        def _():
                            start_inputs(pair, 1, 0, 0)

                    for copy in inputs(pair, chunk, side, side):
                        copy.wait()

                    @pl.when((pair > 0))
                    def _():
                        core_copy(pair, chunk, side).wait_send()

                    for which, target in ((1 - core, core_send), (core, core_own)):
                        product[...] = jnp.dot(
                            left_in[side, which],
                            right_in[side],
                            preferred_element_type=jnp.float32,
                        )

                        def store(block, carry):
                            first = pl.multiple_of(block * rows, 8)
                            target[number, block] = product[pl.ds(first, rows), :].astype(
                                jnp.bfloat16
                            )
                            return carry

                        lax.fori_loop(0, 8, store, 0)
                        if target is core_send:
                            core_copy(pair, chunk, side).start()

    def add(a, b):
        return (a.astype(jnp.float32) + b.astype(jnp.float32)).astype(jnp.bfloat16)

    def load(source, slot, blocks):
        return pltpu.make_async_copy(
            source, loaded.at[slot, pl.ds(0, blocks)], load_sem.at[slot]
        )

    def free_send(stage, pair, chunk):
        @pl.when(pair >= 2)
        def _():
            stage_copy(stage, pair, chunk).wait_send()

    def add_core(pair):
        slot = pair % 2
        x = bit_of(1)
        for chunk in (0, 1):

            @pl.when(has(pair, chunk))
            def _():
                for side in (1, 0):
                    core_copy(pair, chunk, side).wait_recv()
                    load(came[0].at[pair, 2 * chunk + side], side, 8).start()
                free_send(1, pair, chunk)
                for side in (1, 0):
                    number = 2 * chunk + side
                    load(came[0].at[pair, number], side, 8).wait()
                    if chunk == 0:
                        target = sends[0] if side == 1 else keeps[0]

                        def both(block, carry):
                            target[slot, chunk, block] = add(
                                core_own[number, block], loaded[side, block]
                            )
                            return carry

                        lax.fori_loop(0, 8, both, 0)
                    else:

                        def split(z, carry):
                            for target, block in (
                                (sends[0], 2 * z + 1 - x),
                                (keeps[0], 2 * z + x),
                            ):
                                target[slot, chunk, 4 * side + z] = add(
                                    core_own[number, block], loaded[side, block]
                                )
                            return carry

                        lax.fori_loop(0, 4, split, 0)
                    if chunk == 0 and side == 1:
                        stage_copy(1, pair, chunk).start()
                if chunk == 1:
                    stage_copy(1, pair, chunk).start()

    def add_stage(stage, pair):
        slot = pair % 2
        blocks = 16 >> stage
        for chunk in (0, 1):

            @pl.when(has(pair, chunk))
            def _():
                stage_copy(stage, pair, chunk).wait_recv()
                load(came[stage].at[pair, chunk], chunk, blocks).start()
        for chunk in (0, 1):

            @pl.when(has(pair, chunk))
            def _():
                free_send(stage + 1, pair, chunk)
                if stage == 4:

                    @pl.when(pair >= 2)
                    def _():
                        out_copy(pair, chunk).wait()

                load(came[stage].at[pair, chunk], chunk, blocks).wait()
                old, new = keeps[stage - 1], keeps[stage] if stage < 4 else None

                def one(i, carry):
                    if stage == 1 and chunk == 0:
                        x = bit_of(1)
                        gone, kept = 2 * i + 1 - x, 2 * i + x
                    elif stage == 1:
                        gone, kept = 4 + i, i
                    elif stage == 2:
                        low = bit_of(2)
                        gone, kept = 2 * i + 1 - low, 2 * i + low
                    else:
                        gone, kept = 1 - bit_of(3), bit_of(3)
                    sends[stage][slot, chunk, i] = add(
                        old[slot, chunk, gone], loaded[chunk, gone]
                    )
                    new[slot, chunk, i] = add(old[slot, chunk, kept], loaded[chunk, kept])
                    return carry

                if stage < 4:
                    lax.fori_loop(0, blocks // 2, one, 0)
                else:
                    sends[4][slot, chunk] = add(old[slot, chunk, 0], loaded[chunk, 0])
                    out_copy(pair, chunk).start()
                stage_copy(stage + 1, pair, chunk).start()

    def small_copy(stage):
        return remote(
            small_sum.at[stage],
            small_came.at[stage],
            small_send.at[stage],
            small_recv.at[stage],
            partners[stage],
        )

    small_sum[0] = small[...]
    small_copy(0).start()

    def turn(time, carry):
        for stage in range(len(partners)):

            @pl.when(time == stage)
            def _():
                small_copy(stage).wait_recv()
                total = small_sum[stage] + small_came[stage]
                if stage + 1 < len(partners):
                    small_sum[stage + 1] = total
                    small_copy(stage + 1).start()
                else:
                    small_out[...] = total

        for lag, work in (
            (1, add_core),
            (2, functools.partial(add_stage, 1)),
            (3, functools.partial(add_stage, 2)),
            (4, functools.partial(add_stage, 3)),
            (5, functools.partial(add_stage, 4)),
            (0, products),
        ):
            pair = time - lag

            @pl.when((pair >= 0) & (pair < pairs))
            def _():
                work(pair)

        return carry

    lax.fori_loop(0, pairs + 5, turn, 0)
    for stage in range(len(partners)):
        small_copy(stage).wait_send()
    for chunk in (0, 1):
        mine = pairs if chunk == 0 else full_pairs
        for side in (0, 1):
            core_copy(mine - 1, chunk, side).wait_send()
        for pair in range(max(mine - 2, 0), mine):
            out_copy(pair, chunk).wait()
            for stage in range(1, 6):
                stage_copy(stage, pair, chunk).wait_send()
        for pair in range(mine):
            stage_copy(5, pair, chunk).wait_recv()


def scatter_products(left, right, small, pairs, full_pairs, places, collective_id):
    depth, tokens = left.shape[2:]
    width = right.shape[2]
    rows = depth // 8
    low = jnp.bfloat16

    def blocks(*lead):
        return jax.ShapeDtypeStruct((*lead, rows, width), low)

    hbm = [
        blocks(pairs, 4, 8),
        blocks(pairs, 2, 8),
        blocks(pairs, 2, 4),
        blocks(pairs, 2, 2),
        blocks(pairs, 2, 1),
        blocks(pairs, 2, 2),
    ]
    any_space = pl.BlockSpec(memory_space=pl.ANY)

    def vmem(*lead):
        return pltpu.VMEM((*lead, rows, width), low)

    dma = pltpu.SemaphoreType.DMA
    whole = pl.BlockSpec(memory_space=pltpu.VMEM)
    *_, out, total = pl.pallas_call(
        functools.partial(scatter_kernel, pairs, full_pairs, places),
        out_shape=hbm + [jax.ShapeDtypeStruct(small.shape, small.dtype)],
        in_specs=[any_space] * 2 + [whole],
        out_specs=[any_space] * len(hbm) + [whole],
        scratch_shapes=[
            pltpu.VMEM((2, 2, depth, tokens), low),
            pltpu.VMEM((2, tokens, width), low),
            pltpu.VMEM((depth, width), jnp.float32),
            vmem(4, 8),
            vmem(4, 8),
            vmem(2, 8),
            vmem(2, 2, 8),
            vmem(2, 2, 4),
            vmem(2, 2, 2),
            vmem(2, 2, 1),
            vmem(2, 2),
            vmem(2, 2, 8),
            vmem(2, 2, 4),
            vmem(2, 2, 2),
            vmem(2, 2, 1),
            dma((2, 2)),
            dma((2,)),
            dma((2, 2)),
            dma((4,)),
            dma((pairs, 4)),
            dma((5, 2, 2)),
            dma((5, pairs, 2)),
            pltpu.VMEM((5, *small.shape), small.dtype),
            pltpu.VMEM((5, *small.shape), small.dtype),
            dma((5,)),
            dma((5,)),
        ],
        compiler_params=pltpu.CompilerParams(
            collective_id=collective_id, has_side_effects=True, vmem_limit_bytes=58 << 20
        ),
        cost_estimate=pl.CostEstimate(
            flops=4 * left.shape[0] * depth * tokens * width,
            bytes_accessed=2 * left.size + 2 * right.size,
            transcendentals=0,
        ),
    )(left, right, small)
    return out, total


def core_rows(inputs):
    flat = inputs.reshape(-1, inputs.shape[-1])
    size = lax.axis_size("sp")
    rows = flat.shape[1] // size
    grouped = flat.T.reshape(size // 2, 2, rows, flat.shape[0])
    return jnp.swapaxes(grouped, 0, 1).reshape(2, size // 2 * rows, flat.shape[0])


def quarter_rows(inputs):
    flat = inputs.reshape(-1, inputs.shape[-1])
    size = lax.axis_size("sp")
    rows = flat.shape[1] // size // 4
    grouped = flat.T.reshape(size // 2, 2, 4, rows, flat.shape[0])
    moved = jnp.transpose(grouped, (2, 1, 0, 3, 4))
    return moved.reshape(4, 2, size // 2 * rows, flat.shape[0])


def token_rows(gradients):
    return gradients.reshape(-1, gradients.shape[-1])


def scatter_all(terms, small):
    size = lax.axis_size("sp")
    if size != 16 or lax.axis_size("seq") != 2:
        links = {}
        flags = [(False, False), (True, True), (False, False), (False, True)]
        blocks = [
            [scatter_grad(*pair, *flag, links) for pair, flag in zip(block, flags)]
            for block in terms[:2]
        ]
        last = [scatter_grad(*pair, False, False, links) for pair in terms[2]]
        return blocks[0], blocks[1], last, lax.psum(small, ("seq", "sp"))
    lefts, rights = [], []
    for expand, shrink, qkv, out in (terms[1], terms[0]):
        lefts.append(quarter_rows(shrink[0]))
        lefts += [core_rows(member[0])[None] for member in (expand, qkv, out)]
        rights.append(token_rows(shrink[1])[None])
        for member, count in ((expand, 4), (qkv, 3)):
            cut = token_rows(member[1])
            rights.append(jnp.swapaxes(cut.reshape(cut.shape[0], count, -1), 0, 1))
        rights.append(token_rows(out[1])[None])
    lefts += [core_rows(pair[0])[None] for pair in terms[2]]
    rights += [token_rows(pair[1])[None] for pair in terms[2]]

    def places(pair, k):
        block = pair // 3
        kind = pair % 3
        tail = block // 2
        shrink = (2 - kind) // 2 * (1 - tail)
        wide = kind // 2
        expand = (1 - wide) * (kind % 2)
        of_left = 7 * block + (shrink + tail) * k + expand * 4 + wide * (5 + k // 3)
        of_right = 9 * block + tail * k + expand * (1 + k) + wide * (5 + k)
        return of_left, of_right

    left = jnp.concatenate(lefts, axis=0)
    right = jnp.concatenate(rights, axis=0)
    done, total = scatter_products(left, right, small, 7, 6, places, 1)
    done = done.astype(jnp.float32)

    def quarter(pair, k):
        return done[pair, k // 2, k % 2]

    results = []
    for first in (0, 3):
        shrink = jnp.concatenate([quarter(first, k) for k in range(4)], axis=0)
        expand = jnp.concatenate([quarter(first + 1, k) for k in range(4)], axis=1)
        qkv = jnp.concatenate([quarter(first + 2, k) for k in range(3)], axis=1)
        results.append([expand, shrink, qkv, quarter(first + 2, 3)])
    return results[1], results[0], [quarter(6, 0), quarter(6, 1)], total


def halve(members, bit_value, bit, links):
    parts = [split_blocks(member, bit_value) for member in members]
    sent = low_sum(*[part[0] for part in parts])
    return (low_sum(*[part[1] for part in parts]), swap_sp(sent, bit, links))


def sum_seq(values):
    mine = values.astype(jnp.bfloat16)
    return mine.astype(jnp.float32) + swap_seq(mine, {}).astype(jnp.float32)


def triple_bias(query_bias, value_bias):
    head_query = query_bias.reshape(HEADS, 1, HEAD_DIM)
    head_value = value_bias.reshape(HEADS, 1, HEAD_DIM)
    return jnp.concatenate([head_query, jnp.zeros_like(head_query), head_value], axis=1).reshape(
        3 * D
    )


def pair_bias(value_bias):
    head_value = value_bias.reshape(HEADS, 1, HEAD_DIM)
    return jnp.concatenate([jnp.zeros_like(head_value), head_value], axis=1).reshape(2 * D)


def triple_bias_grad(totals):
    split_rows = totals.reshape(HEADS, 3, HEAD_DIM)
    return (split_rows[:, 0].reshape(D), split_rows[:, 2].reshape(D))


def frame_modulation(segment_ids, timesteps):
    onehot = (segment_ids[:, :, None] == jnp.arange(CLIPS)[None, None, :]).astype(jnp.float32)
    features = time_features(timesteps)
    return jnp.einsum("sfc,scz->sfz", onehot, features, precision=lax.Precision.HIGHEST)


def block_pieces(table_rows, frame_mod):
    modulation = table_rows[None, None] + frame_mod
    return [modulation[:, :, number][:, :, None, :] for number in range(6)]


def gated_back(grad_out, gating, branch):
    branch_grad = (gating * grad_out).astype(jnp.bfloat16)
    gate_grad = jnp.sum(grad_out * branch, axis=2, keepdims=True)
    return (branch_grad, gate_grad)


def to_pairs(values):
    groups, frames, patches, head_count, columns = values.shape
    reordered = jnp.transpose(values, (0, 1, 3, 2, 4))
    return reordered.reshape(lax.axis_size("sp"), -1, patches, columns)


def from_pairs(values, groups, frames):
    devices, pair_count, patches, columns = values.shape
    reordered = values.reshape(groups, frames, -1, patches, columns)
    return jnp.transpose(reordered, (0, 1, 3, 2, 4))


def pair_scores(triple):
    queries = triple[..., :HEAD_DIM]
    key_rows = triple[..., HEAD_DIM : 2 * HEAD_DIM]
    scores = jnp.einsum(
        "zkqe,zkre->zkqr", queries, key_rows, preferred_element_type=jnp.float32
    ) * HEAD_DIM ** (-0.5)
    return jax.nn.softmax(scores, axis=-1)


def attend_pairs(triple):
    attention = pair_scores(triple).astype(jnp.bfloat16)
    mixture = jnp.einsum(
        "zkqr,zkre->zkqe",
        attention,
        triple[..., 2 * HEAD_DIM :],
        preferred_element_type=jnp.float32,
    ).astype(jnp.bfloat16)
    return lax.all_to_all(mixture, "sp", split_axis=2, concat_axis=0, tiled=True)


def pair_backward(members):
    triple, out_grad = members
    queries = triple[..., :HEAD_DIM]
    key_rows = triple[..., HEAD_DIM : 2 * HEAD_DIM]
    value_rows = triple[..., 2 * HEAD_DIM :]
    attention = pair_scores(triple)
    rounded = attention.astype(jnp.bfloat16)
    prob_grad = jnp.einsum(
        "zkqe,zkre->zkqr", out_grad, value_rows, preferred_element_type=jnp.float32
    )
    centre = jnp.sum(prob_grad * attention, axis=-1, keepdims=True)
    score_grad = (attention * (prob_grad - centre)).astype(jnp.bfloat16)
    scaling = HEAD_DIM ** (-0.5)
    query_grad = (
        jnp.einsum("zkqr,zkre->zkqe", score_grad, key_rows, preferred_element_type=jnp.float32)
        * scaling
    )
    key_grad = (
        jnp.einsum("zkqr,zkqe->zkre", score_grad, queries, preferred_element_type=jnp.float32)
        * scaling
    )
    value_grad = jnp.einsum(
        "zkqr,zkqe->zkre", rounded, out_grad, preferred_element_type=jnp.float32
    )
    gradients = jnp.concatenate([query_grad, key_grad, value_grad], axis=-1).astype(jnp.bfloat16)
    return lax.all_to_all(gradients, "sp", split_axis=2, concat_axis=0, tiled=True)


def pair_attention(triple):
    groups, frames, patches = triple.shape[:3]
    shaped = triple.reshape(groups, frames, patches, HEADS, 3 * HEAD_DIM)
    pairs = lax.all_to_all(to_pairs(shaped), "sp", split_axis=0, concat_axis=2, tiled=True)
    exchanged = attend_pairs(pairs)
    return from_pairs(exchanged, groups, frames).reshape(groups, frames, patches, D), pairs


def pair_attention_back(pairs, mixture_grad):
    groups, frames, patches = mixture_grad.shape[:3]
    grad_shaped = mixture_grad.reshape(groups, frames, patches, HEADS, HEAD_DIM)
    returned = pair_backward(
        (
            pairs,
            lax.all_to_all(to_pairs(grad_shaped), "sp", split_axis=0, concat_axis=2, tiled=True),
        )
    )
    return from_pairs(returned, groups, frames).reshape(groups, frames, patches, 3 * D)


def feed_forward(residual, offset, scaling, gating, expand, shrink, vectors, start_row):
    hidden = modulate(residual, offset, scaling).astype(jnp.bfloat16)
    inner_sum = project(hidden, expand) + vectors[start_row : start_row + 4].reshape(FF)
    active = gelu_tanh(inner_sum).astype(jnp.bfloat16)
    branch = project(active, shrink) + vectors[3]
    return ((hidden, inner_sum, active, branch), residual + gating * branch)


def feed_backward(grad_out, residual, offset, scaling, gating, stored, expand, shrink):
    hidden, inner_sum, active, branch = stored
    branch_grad, gate_grad = gated_back(grad_out, gating, branch)
    shrink_grad = (active, branch_grad)
    active_grad = input_grad(branch_grad, shrink)
    gelu_value, gelu_back = jax.vjp(gelu_tanh, inner_sum)
    inner_grad = gelu_back(active_grad)[0].astype(jnp.bfloat16)
    expand_grad = (hidden, inner_grad)
    hidden_grad = input_grad(inner_grad, expand)
    norm_value, norm_back = jax.vjp(modulate, residual, offset, scaling)
    residual_grad, offset_grad, scaling_grad = norm_back(hidden_grad)
    return (
        grad_out + residual_grad,
        [offset_grad, scaling_grad, gate_grad],
        (expand_grad, shrink_grad, column_sum(inner_grad), column_sum(branch_grad)),
    )


def table_sums(members):
    return jnp.stack([jnp.sum(member, axis=(0, 1, 2)) for member in members])


def spatial_forward(residual, weights, frame_mod):
    qkv_weight, out_weight, expand, shrink, vectors = weights
    vectors_f = as_float(vectors)
    pieces = block_pieces(vectors_f[4:10], frame_mod)
    hidden = modulate(residual, pieces[0], pieces[1]).astype(jnp.bfloat16)
    triple = (project(hidden, qkv_weight) + triple_bias(vectors_f[0], vectors_f[1])).astype(
        jnp.bfloat16
    )
    mixture, pairs = pair_attention(triple)
    branch = project(mixture, out_weight) + vectors_f[2]
    middle = residual + pieces[2] * branch
    stored_ffn, result = feed_forward(
        middle, pieces[3], pieces[4], pieces[5], expand, shrink, vectors_f, 10
    )
    return (result, (hidden, pairs, mixture, branch, middle, stored_ffn))


def spatial_backward(grad_out, residual, weights, frame_mod, stored):
    qkv_weight, out_weight, expand, shrink, vectors = weights
    pieces = block_pieces(as_float(vectors)[4:10], frame_mod)
    hidden, pairs, mixture, branch, middle, stored_ffn = stored
    middle_grad, ffn_table, ffn_grads = feed_backward(
        grad_out, middle, pieces[3], pieces[4], pieces[5], stored_ffn, expand, shrink
    )
    branch_grad, gate_grad = gated_back(middle_grad, pieces[2], branch)
    out_weight_grad = (mixture, branch_grad)
    out_bias = column_sum(branch_grad)
    mixture_grad = input_grad(branch_grad, out_weight).astype(jnp.bfloat16)
    triple_grad = pair_attention_back(pairs, mixture_grad)
    qkv_grad = (hidden, triple_grad)
    query_bias, value_bias = triple_bias_grad(column_sum(triple_grad))
    hidden_grad = input_grad(triple_grad, qkv_weight)
    norm_value, norm_back = jax.vjp(modulate, residual, pieces[0], pieces[1])
    residual_grad, offset_grad, scaling_grad = norm_back(hidden_grad)
    table_grad = table_sums([offset_grad, scaling_grad, gate_grad] + ffn_table)
    vector_grad = jnp.concatenate(
        [
            jnp.stack([query_bias, value_bias, out_bias, ffn_grads[3]]),
            table_grad,
            ffn_grads[2].reshape(4, D),
        ],
        axis=0,
    )
    return (
        middle_grad + residual_grad,
        (qkv_grad, out_weight_grad, ffn_grads[0], ffn_grads[1], vector_grad),
    )


def temporal_scores(triple, same_clip):
    scores = jnp.einsum(
        "sfphe,sgphe->sphfg",
        triple[..., :HEAD_DIM],
        triple[..., HEAD_DIM : 2 * HEAD_DIM],
        preferred_element_type=jnp.float32,
    ) * HEAD_DIM ** (-0.5)
    return jax.nn.softmax(jnp.where(same_clip, scores, masked_score), axis=-1)


def caption_scores(queries, keyval, allowed):
    scores = jnp.einsum(
        "sfphe,srhe->sfphr", queries, keyval[..., :HEAD_DIM], preferred_element_type=jnp.float32
    ) * HEAD_DIM ** (-0.5)
    return jax.nn.softmax(jnp.where(allowed, scores, masked_score), axis=-1)


def temporal_forward(residual, weights, frame_mod, same_clip, allowed, context):
    qkv_weight, out_weight, expand, shrink, query_weight, keyval_weight, cross_weight, vectors = (
        weights
    )
    vectors_f = as_float(vectors)
    pieces = block_pieces(vectors_f[8:14], frame_mod)
    groups, frames, patches = residual.shape[:3]
    hidden = modulate(residual, pieces[0], pieces[1]).astype(jnp.bfloat16)
    triple = (project(hidden, qkv_weight) + triple_bias(vectors_f[0], vectors_f[1])).astype(
        jnp.bfloat16
    )
    triple = triple.reshape(groups, frames, patches, HEADS, 3 * HEAD_DIM)
    attention = temporal_scores(triple, same_clip).astype(jnp.bfloat16)
    mixture = (
        jnp.einsum(
            "sphfg,sgphe->sfphe",
            attention,
            triple[..., 2 * HEAD_DIM :],
            preferred_element_type=jnp.float32,
        )
        .astype(jnp.bfloat16)
        .reshape(groups, frames, patches, D)
    )
    branch = project(mixture, out_weight) + vectors_f[2]
    middle = residual + pieces[2] * branch
    lowered = middle.astype(jnp.bfloat16)
    queries = (project(lowered, query_weight) + vectors_f[4]).astype(jnp.bfloat16)
    queries = queries.reshape(groups, frames, patches, HEADS, HEAD_DIM)
    keyval = (project(context, keyval_weight) + pair_bias(vectors_f[5])).astype(jnp.bfloat16)
    keyval = keyval.reshape(groups, -1, HEADS, 2 * HEAD_DIM)
    cross_probs = caption_scores(queries, keyval, allowed).astype(jnp.bfloat16)
    cross_mix = (
        jnp.einsum(
            "sfphr,srhe->sfphe",
            cross_probs,
            keyval[..., HEAD_DIM:],
            preferred_element_type=jnp.float32,
        )
        .astype(jnp.bfloat16)
        .reshape(groups, frames, patches, D)
    )
    crossed = middle + project(cross_mix, cross_weight) + vectors_f[6]
    stored_ffn, result = feed_forward(
        crossed, pieces[3], pieces[4], pieces[5], expand, shrink, vectors_f, 14
    )
    return (
        result,
        (
            hidden,
            triple,
            mixture,
            branch,
            middle,
            lowered,
            queries,
            keyval,
            cross_mix,
            crossed,
            stored_ffn,
        ),
    )


def temporal_backward(grad_out, residual, weights, frame_mod, same_clip, allowed, stored):
    qkv_weight, out_weight, expand, shrink, query_weight, keyval_weight, cross_weight, vectors = (
        weights
    )
    pieces = block_pieces(as_float(vectors)[8:14], frame_mod)
    (
        hidden,
        triple,
        mixture,
        branch,
        middle,
        lowered,
        queries,
        keyval,
        cross_mix,
        crossed,
        stored_ffn,
    ) = stored
    groups, frames, patches = residual.shape[:3]
    scaling = HEAD_DIM ** (-0.5)
    crossed_grad, ffn_table, ffn_grads = feed_backward(
        grad_out, crossed, pieces[3], pieces[4], pieces[5], stored_ffn, expand, shrink
    )
    cross_branch_grad = crossed_grad.astype(jnp.bfloat16)
    cross_weight_grad = (cross_mix, cross_branch_grad)
    cross_bias = column_sum(cross_branch_grad)
    mix_grad = input_grad(cross_branch_grad, cross_weight).astype(jnp.bfloat16)
    mix_grad = mix_grad.reshape(groups, frames, patches, HEADS, HEAD_DIM)
    cross_probs = caption_scores(queries, keyval, allowed)
    rounded = cross_probs.astype(jnp.bfloat16)
    prob_grad = jnp.einsum(
        "sfphe,srhe->sfphr", mix_grad, keyval[..., HEAD_DIM:], preferred_element_type=jnp.float32
    )
    centre = jnp.sum(prob_grad * cross_probs, axis=-1, keepdims=True)
    score_grad = (cross_probs * (prob_grad - centre)).astype(jnp.bfloat16)
    query_grad = (
        jnp.einsum(
            "sfphr,srhe->sfphe",
            score_grad,
            keyval[..., :HEAD_DIM],
            preferred_element_type=jnp.float32,
        )
        * scaling
    )
    query_grad = query_grad.astype(jnp.bfloat16).reshape(groups, frames, patches, D)
    key_grad = (
        jnp.einsum("sfphr,sfphe->srhe", score_grad, queries, preferred_element_type=jnp.float32)
        * scaling
    )
    value_grad = jnp.einsum(
        "sfphr,sfphe->srhe", rounded, mix_grad, preferred_element_type=jnp.float32
    )
    keyval_grad = jnp.concatenate([key_grad, value_grad], axis=-1).reshape(groups, -1, 2 * D)
    keyval_grad = lax.psum(keyval_grad.astype(jnp.bfloat16), "sp")
    query_weight_grad = (lowered, query_grad)
    cross_query_bias = column_sum(query_grad)
    middle_grad = crossed_grad + input_grad(query_grad, query_weight)
    branch_grad, gate_grad = gated_back(middle_grad, pieces[2], branch)
    out_weight_grad = (mixture, branch_grad)
    out_bias = column_sum(branch_grad)
    mixture_grad = input_grad(branch_grad, out_weight).astype(jnp.bfloat16)
    mixture_grad = mixture_grad.reshape(groups, frames, patches, HEADS, HEAD_DIM)
    attention = temporal_scores(triple, same_clip)
    rounded_t = attention.astype(jnp.bfloat16)
    prob_grad_t = jnp.einsum(
        "sfphe,sgphe->sphfg",
        mixture_grad,
        triple[..., 2 * HEAD_DIM :],
        preferred_element_type=jnp.float32,
    )
    centre_t = jnp.sum(prob_grad_t * attention, axis=-1, keepdims=True)
    score_grad_t = (attention * (prob_grad_t - centre_t)).astype(jnp.bfloat16)
    query_part = (
        jnp.einsum(
            "sphfg,sgphe->sfphe",
            score_grad_t,
            triple[..., HEAD_DIM : 2 * HEAD_DIM],
            preferred_element_type=jnp.float32,
        )
        * scaling
    )
    key_part = (
        jnp.einsum(
            "sphfg,sfphe->sgphe",
            score_grad_t,
            triple[..., :HEAD_DIM],
            preferred_element_type=jnp.float32,
        )
        * scaling
    )
    value_part = jnp.einsum(
        "sphfg,sfphe->sgphe", rounded_t, mixture_grad, preferred_element_type=jnp.float32
    )
    triple_grad = jnp.concatenate([query_part, key_part, value_part], axis=-1).astype(jnp.bfloat16)
    triple_grad = triple_grad.reshape(groups, frames, patches, 3 * D)
    qkv_grad = (hidden, triple_grad)
    query_bias, value_bias = triple_bias_grad(column_sum(triple_grad))
    hidden_grad = input_grad(triple_grad, qkv_weight)
    norm_value, norm_back = jax.vjp(modulate, residual, pieces[0], pieces[1])
    residual_grad, offset_grad, scaling_grad = norm_back(hidden_grad)
    table_grad = table_sums([offset_grad, scaling_grad, gate_grad] + ffn_table)
    zero_row = jnp.zeros((D,), jnp.float32)
    vector_grad = jnp.concatenate(
        [
            jnp.stack(
                [
                    query_bias,
                    value_bias,
                    out_bias,
                    ffn_grads[3],
                    cross_query_bias,
                    zero_row,
                    cross_bias,
                    zero_row,
                ]
            ),
            table_grad,
            ffn_grads[2].reshape(4, D),
        ],
        axis=0,
    )
    terms = (
        qkv_grad,
        out_weight_grad,
        ffn_grads[0],
        ffn_grads[1],
        query_weight_grad,
        cross_weight_grad,
        vector_grad,
    )
    return (middle_grad + residual_grad, terms, keyval_grad)


def on_device(
    video,
    segment_ids,
    timesteps,
    drop_mask,
    captions,
    null_caption,
    caption_weight,
    spatial_qkv,
    spatial_out,
    spatial_expand,
    spatial_shrink,
    spatial_vectors,
    temporal_qkv,
    temporal_out,
    temporal_expand,
    temporal_shrink,
    cross_query,
    cross_keyval,
    cross_out,
    temporal_vectors,
    cotangent,
):
    groups, frames, patches = video.shape[:3]
    size = lax.axis_size("sp")
    third = D
    wide = [
        spatial_qkv,
        spatial_out,
        spatial_expand,
        temporal_qkv,
        temporal_out,
        cross_query,
        cross_keyval,
        cross_out,
        temporal_expand,
    ]

    def rounds_of(rows):
        def block_round(qkv, out):
            return columns_round(
                (qkv, 0, third), (qkv, third, third), (qkv, 2 * third, third), (out, 0, third)
            )

        def expand_round(weight):
            quarter = FF // 4
            return columns_round(*[(weight, k * quarter, quarter) for k in range(4)])

        return [
            block_round(0, 1),
            expand_round(2),
            rows_round(9, rows),
            block_round(3, 4),
            columns_round((5, 0, third), (6, 0, third), (6, third, third), (7, 0, third)),
            expand_round(8),
            rows_round(10, rows),
        ]

    (
        full_sqkv,
        full_sout,
        full_sexp,
        full_tqkv,
        full_tout,
        full_cq,
        full_ckv,
        full_cout,
        full_texp,
        full_sshr,
        full_tshr,
        all_vectors,
    ) = gather_all(
        [spatial_shrink, temporal_shrink],
        wide,
        jnp.concatenate([spatial_vectors, temporal_vectors], axis=0),
        rounds_of,
        0,
    )
    n_spatial = spatial_vectors.shape[0]
    spatial = (full_sqkv, full_sout, full_sexp, full_sshr, all_vectors[:n_spatial])
    temporal = (
        full_tqkv,
        full_tout,
        full_texp,
        full_tshr,
        full_cq,
        full_ckv,
        full_cout,
        all_vectors[n_spatial:],
    )
    dropped = (drop_mask > 0).astype(jnp.float32)
    text_local = jnp.where(drop_mask[:, :, None, None] > 0, null_caption[None, None], captions)
    text_rows = text_local.reshape(groups, CLIPS * CAP, -1)
    caption_sum = lax.psum(project(text_rows, caption_weight), "sp")
    caption_sum, first = lax.optimization_barrier((caption_sum, spatial[0]))
    spatial = (first, *spatial[1:])
    frame_mod = frame_modulation(segment_ids, timesteps).reshape(groups, frames, 6, D)
    same_clip = (segment_ids[:, :, None] == segment_ids[:, None, :])[:, None, None]
    row_clip = jnp.arange(CLIPS * CAP) // CAP
    allowed = (segment_ids[:, :, None] == row_clip[None, None, :])[:, :, None, None, :]
    residual = video.astype(jnp.float32)
    middle, spatial_kept = spatial_forward(residual, spatial, frame_mod)
    context = (caption_sum + as_float(temporal[7])[7]).astype(jnp.bfloat16)
    result, temporal_kept = temporal_forward(
        middle, temporal, frame_mod, same_clip, allowed, context
    )
    output = result.astype(jnp.bfloat16)
    middle_grad, temporal_terms, keyval_grad = temporal_backward(
        cotangent.astype(jnp.float32),
        middle,
        temporal,
        frame_mod,
        same_clip,
        allowed,
        temporal_kept,
    )
    shard_rows = D // lax.axis_size("sp")
    first_row = lax.axis_index("sp") * shard_rows
    video_grad, spatial_terms = spatial_backward(
        middle_grad, residual, spatial, frame_mod, spatial_kept
    )
    spatial_sums, temporal_sums, cross_sums, vector_total = scatter_all(
        (
            (spatial_terms[2], spatial_terms[3], spatial_terms[0], spatial_terms[1]),
            (temporal_terms[2], temporal_terms[3], temporal_terms[0], temporal_terms[1]),
            (temporal_terms[4], temporal_terms[5]),
        ),
        jnp.concatenate([spatial_terms[4], temporal_terms[6]], axis=0),
    )
    vector_total = lax.dynamic_slice_in_dim(vector_total, first_row, shard_rows, 1)
    keyval_grad, video_grad = lax.optimization_barrier((keyval_grad, video_grad))
    context_grad = input_grad(keyval_grad, temporal[5]).astype(jnp.bfloat16)
    local_context = lax.dynamic_slice_in_dim(context, first_row, shard_rows, 2)
    keyval_weight_grad = weight_grad(local_context, keyval_grad)
    value_bias_full = column_sum(keyval_grad).reshape(HEADS, 2, HEAD_DIM)[:, 1].reshape(D)
    caption_bias_full = column_sum(context_grad)
    caption_weight_grad = weight_grad(text_rows, context_grad)
    text_grad = input_grad(context_grad, caption_weight).reshape(groups, CLIPS, CAP, -1)
    null_grad = jnp.sum(text_grad * dropped[:, :, None, None], axis=(0, 1))
    own_rows = [
        lax.dynamic_slice_in_dim(row, first_row, shard_rows, 0)
        for row in (value_bias_full, caption_bias_full)
    ]
    width = null_grad.shape[1]
    flat = jnp.stack([jnp.pad(row, (0, width - shard_rows)) for row in own_rows])
    small_total = sum_seq(jnp.concatenate([null_grad, flat], axis=0))
    null_total = small_total[: null_grad.shape[0]]
    bias_total = small_total[null_grad.shape[0] :, :shard_rows]
    vector_total = vector_total.at[n_spatial + 5].add(bias_total[0])
    vector_total = vector_total.at[n_spatial + 7].add(bias_total[1])
    return (
        output,
        video_grad.astype(jnp.bfloat16),
        null_total,
        sum_seq(caption_weight_grad),
        spatial_sums[2],
        spatial_sums[3],
        spatial_sums[0],
        spatial_sums[1],
        vector_total[:n_spatial],
        temporal_sums[2],
        temporal_sums[3],
        temporal_sums[0],
        temporal_sums[1],
        cross_sums[0],
        sum_seq(keyval_weight_grad),
        cross_sums[1],
        vector_total[n_spatial:],
    )


def solution(mesh):
    return jax.shard_map(
        on_device,
        mesh=mesh,
        in_specs=(
            P("seq", None, "sp", None),
            P("seq", None),
            P("seq", None),
            P("seq", None),
            P("seq", None, None, "sp"),
            P(None, "sp"),
            P("sp", None),
            P("sp", None),
            P("sp", None),
            P("sp", None),
            P("sp", None),
            P(None, "sp"),
            P("sp", None),
            P("sp", None),
            P("sp", None),
            P("sp", None),
            P("sp", None),
            P("sp", None),
            P("sp", None),
            P(None, "sp"),
            P("seq", None, "sp", None),
        ),
        out_specs=(
            P("seq", None, "sp", None),
            P("seq", None, "sp", None),
            P(None, "sp"),
            P("sp", None),
            P("sp", None),
            P("sp", None),
            P("sp", None),
            P("sp", None),
            P(None, "sp"),
            P("sp", None),
            P("sp", None),
            P("sp", None),
            P("sp", None),
            P("sp", None),
            P("sp", None),
            P("sp", None),
            P(None, "sp"),
        ),
        check_vma=False,
    )
```

```python
import functools
import math

import jax
import jax.numpy as jnp
from jax import lax
from jax.experimental import pallas as pl
from jax.experimental.pallas import tpu as pltpu
from jax.sharding import PartitionSpec as P

D = 1152
HEADS = 16
HEAD_DIM = 72
FF = 4608
CAP = 120
CLIPS = 2


norm_eps = 1e-06
masked_score = -1e30


def time_features(timestep):
    half_width = 3 * D
    frequency = jnp.exp(
        jnp.arange(half_width, dtype=jnp.float32) * (-math.log(10000.0) / half_width)
    )
    angles = timestep.astype(jnp.float32)[..., None] * frequency
    return 0.5 * jnp.concatenate([jnp.cos(angles), jnp.sin(angles)], axis=-1)


def layer_norm(residual):
    center = residual - jnp.mean(residual, axis=-1, keepdims=True)
    return center * lax.rsqrt(jnp.mean(center * center, axis=-1, keepdims=True) + norm_eps)


def modulate(residual, offset, scaling):
    return layer_norm(residual) * (1.0 + scaling) + offset


def gelu_tanh(inner_sum):
    return jax.nn.gelu(inner_sum, approximate=True)


def as_float(member):
    return member.astype(jnp.float32)


def project(inputs, weight):
    return jnp.dot(inputs, weight, preferred_element_type=jnp.float32)


def weight_grad(inputs, gradients):
    left_rows = inputs.reshape(-1, inputs.shape[-1])
    right_rows = gradients.reshape(-1, gradients.shape[-1])
    return lax.dot_general(
        left_rows, right_rows, (((0,), (0,)), ((), ())), preferred_element_type=jnp.float32
    )


def input_grad(gradients, weight):
    return lax.dot_general(
        gradients,
        weight,
        (((gradients.ndim - 1,), (1,)), ((), ())),
        preferred_element_type=jnp.float32,
    )


def column_sum(gradients):
    return jnp.sum(gradients.astype(jnp.float32).reshape(-1, gradients.shape[-1]), axis=0)


def index_bits():
    return lax.axis_size("sp").bit_length() - 1


def after(values, earlier):
    if not earlier:
        return values
    return lax.optimization_barrier((values, tuple(earlier)))[0]


def in_turn(links, key, values, exchange):
    last = links.get(key)
    result = exchange(values if last is None else after(values, [last]))
    links[key] = result
    return result


def swap_sp(values, bit, links):
    size = lax.axis_size("sp")
    pairs = [(i, i ^ (1 << bit)) for i in range(size)]
    return in_turn(links, min(bit, 2), values, lambda v: lax.ppermute(v, "sp", pairs))


def swap_seq(values, links, key="seq"):
    return in_turn(links, key, values, lambda v: lax.ppermute(v, "seq", [(0, 1), (1, 0)]))


def gather_kernel(rounds, n_in, n_out, *refs):
    shards, outs = refs[:n_in], refs[n_in : n_in + n_out]
    local_sem, send_sem, recv_sem, small_local, small_send, small_recv = refs[n_in + n_out :]
    me = lax.axis_index("sp")
    plane = lax.axis_index("seq")
    count = index_bits()
    place = [(me // (1 << (count - 1 - d))) % 2 for d in range(count)]

    def flip(bit):
        mine = (me // (1 << bit)) % 2
        return (plane, me + (1 << bit) * (1 - 2 * mine))

    across = (1 - plane, me)
    partners = [flip(bit) for bit in range(count)] + [across]
    barrier = pltpu.get_barrier_semaphore()
    for partner in partners:
        pl.semaphore_signal(
            barrier, inc=1, device_id=partner, device_id_type=pl.DeviceIdType.MESH
        )
    pl.semaphore_wait(barrier, len(partners))

    def part(ref, lead, piece):
        weight, rows, columns = piece
        if rows is None:
            return ref.at[(*lead, slice(None), pl.ds(*columns))]
        half, first, size = rows
        return ref.at[(*lead, half, pl.ds(first, size), slice(None))]

    def stage_places(stage):
        return tuple(
            slice(None) if d < stage else place[d] for d in range(count)
        )

    for own_half in (0, 1):

        @pl.when(plane == own_half)
        def _():
            started = []

            def send(number, stage, slot, source, target, partner):
                copy = pltpu.make_async_remote_copy(
                    src_ref=source,
                    dst_ref=target,
                    send_sem=send_sem.at[number, stage, slot],
                    recv_sem=recv_sem.at[number, stage, slot],
                    device_id=partner,
                    device_id_type=pl.DeviceIdType.MESH,
                )
                copy.start()
                return copy

            def own(chunk):
                return chunk[own_half]

            def other(chunk):
                return chunk[1 - own_half]

            def step(number, stage):
                first, second = rounds[number]
                lead = stage_places(min(stage, count - 2))
                if stage < count - 2:
                    moves = [(own(first), flip(count - 1 - stage)), (own(second), flip(count - 1 - stage))]
                elif stage == count - 2:
                    moves = [(own(first), flip(1)), (own(second), across)]
                elif stage == count - 1:
                    moves = [
                        (own(first), across),
                        (own(second), flip(1)),
                        (other(second), flip(1)),
                    ]
                else:
                    moves = [
                        (piece, flip(0))
                        for chunk in (first, second)
                        for piece in (own(chunk), other(chunk))
                    ]
                copies = []
                for slot, (piece, partner) in enumerate(moves):
                    places = lead
                    if stage == count - 1 and partner is across or stage == count:
                        places = stage_places(count - 1)
                    target = part(outs[piece[0]], places, piece)
                    source = target
                    if stage == 0:
                        source = part(shards[piece[0]], (), piece)
                    copies.append(send(number, stage, slot, source, target, partner))
                return copies

            def small_step(stage):
                target = outs[-1].at[stage_places(stage)]
                copy = pltpu.make_async_remote_copy(
                    src_ref=target if stage else shards[-1],
                    dst_ref=target,
                    send_sem=small_send.at[stage],
                    recv_sem=small_recv.at[stage],
                    device_id=flip(count - 1 - stage),
                    device_id_type=pl.DeviceIdType.MESH,
                )
                copy.start()
                return copy

            copies = {}
            small = [small_step(0)]
            local = [
                pltpu.make_async_copy(shards[-1], outs[-1].at[stage_places(0)], small_local)
            ]
            local[0].start()
            for number, pair in enumerate(rounds):
                for slot, chunk in enumerate(pair):
                    piece = own(chunk)
                    copy = pltpu.make_async_copy(
                        part(shards[piece[0]], (), piece),
                        part(outs[piece[0]], stage_places(0), piece),
                        local_sem.at[number, slot],
                    )
                    copy.start()
                    local.append(copy)
            lags = list(range(count - 1)) + [count - 1, count + 1]
            for time in range(len(rounds) + lags[-1]):
                if time == 1:
                    for copy in local:
                        copy.wait()
                if 0 < time < count:
                    small[-1].wait_recv()
                    small.append(small_step(time))
                for stage, lag in enumerate(lags):
                    number = time - lag
                    if not 0 <= number < len(rounds):
                        continue
                    if stage:
                        for copy in copies[number, stage - 1]:
                            copy.wait_recv()
                    copies[number, stage] = step(number, stage)
            small[-1].wait_recv()
            for copy in small:
                copy.wait_send()
            for number in range(len(rounds)):
                for copy in copies[number, count]:
                    copy.wait_recv()
                for stage in range(count + 1):
                    for copy in copies[number, stage]:
                        copy.wait_send()


def gather_weights(shards, rounds, collective_id):
    size = lax.axis_size("sp")
    lead = (2,) * index_bits()
    shapes = [lead + shard.shape for shard in shards]
    total = sum(2 * math.prod(shape) for shape in shapes)
    stages = index_bits() + 1
    placed = pl.pallas_call(
        functools.partial(gather_kernel, rounds, len(shards), len(shards)),
        out_shape=[jax.ShapeDtypeStruct(shape, jnp.bfloat16) for shape in shapes],
        in_specs=[pl.BlockSpec(memory_space=pltpu.VMEM)] * len(shards),
        out_specs=[pl.BlockSpec(memory_space=pl.ANY)] * len(shards),
        scratch_shapes=[
            pltpu.SemaphoreType.DMA((len(rounds), 2)),
            pltpu.SemaphoreType.DMA((len(rounds), stages, 4)),
            pltpu.SemaphoreType.DMA((len(rounds), stages, 4)),
            pltpu.SemaphoreType.DMA,
            pltpu.SemaphoreType.DMA((index_bits(),)),
            pltpu.SemaphoreType.DMA((index_bits(),)),
        ],
        compiler_params=pltpu.CompilerParams(
            collective_id=collective_id, has_side_effects=True, vmem_limit_bytes=32 << 20
        ),
        cost_estimate=pl.CostEstimate(flops=0, bytes_accessed=total, transcendentals=0),
    )(*shards)
    *large, small = placed
    full = [member.reshape(size * math.prod(member.shape[index_bits() : -1]), -1) for member in large]
    small = jnp.swapaxes(small.reshape(size, *small.shape[-2:]), 0, 1)
    return full + [small.reshape(small.shape[0], -1)]


def columns_round(*quarters):
    pieces = [(weight, None, (first, width)) for weight, first, width in quarters]
    return ((pieces[0], pieces[2]), (pieces[1], pieces[3]))


def rows_round(weight, rows):
    cut = rows // 32 * 16 + (rows // 16 % 2) * 16
    return (
        ((weight, (0, 0, cut), None), (weight, (1, 0, cut), None)),
        ((weight, (0, cut, rows - cut), None), (weight, (1, cut, rows - cut), None)),
    )


def gather_all(tall, wide, small, rounds_of, collective_id):
    if wide[0].shape[0] % 8 or lax.axis_size("seq") != 2:
        full = [lax.all_gather(shard, "sp", axis=0, tiled=True) for shard in wide + tall]
        return full + [lax.all_gather(small, "sp", axis=1, tiled=True)]
    shards = list(wide) + [
        shard.reshape(2, shard.shape[0] // 2, shard.shape[1]) for shard in tall
    ]
    shards.append(small)
    return gather_weights(shards, rounds_of(tall[0].shape[0] // 2), collective_id)


def pick_half(first, second):
    return jnp.where(lax.axis_index("seq") == 0, first, second)


def low_sum(*members):
    total = members[0].astype(jnp.float32)
    for member in members[1:]:
        total = total + member.astype(jnp.float32)
    return total.astype(jnp.bfloat16)


def pick(values, index, axis):
    return lax.dynamic_index_in_dim(values, index, axis, keepdims=False)


def split_blocks(values, bit_value):
    paired = values.reshape(values.shape[0] // 2, 2, *values.shape[1:])
    return pick(paired, 1 - bit_value, 1), pick(paired, bit_value, 1)


def scatter_grad(inputs, gradients, by_rows, seq_first, links):
    size = lax.axis_size("sp")
    me = lax.axis_index("sp")
    plane = lax.axis_index("seq")
    bits = [(me // (1 << b)) % 2 for b in range(index_bits())]
    left = inputs.reshape(-1, inputs.shape[-1])
    right = gradients.reshape(-1, gradients.shape[-1])
    depth = left.shape[1]
    columns = right.shape[1]
    rows = depth // size
    half = (rows if by_rows else columns) // 2
    if not by_rows:
        padded = -(-half // 128) * 128
        fill = ((0, 0), (0, padded - half))
        right = jnp.concatenate(
            [
                jnp.pad(pick_half(right[:, :half], right[:, half:]), fill),
                jnp.pad(pick_half(right[:, half:], right[:, :half]), fill),
            ],
            axis=1,
        )
    total = lax.dot_general(
        left, right, (((0,), (0,)), ((), ())), preferred_element_type=jnp.float32
    ).astype(jnp.bfloat16)
    if by_rows:
        total = total.reshape(size, 2, half, columns)
    else:
        total = total.reshape(size, rows, 2 * padded)
    sent, kept = split_blocks(total, bits[0])
    came = swap_sp(sent, 0, links)
    if by_rows:
        own, other = [
            (pick(kept, which, 1), pick(came, which, 1)) for which in (plane, 1 - plane)
        ]
    else:
        own = (kept[:, :, :padded], came[:, :, :padded])
        other = (kept[:, :, padded:], came[:, :, padded:])
    if seq_first:
        current = (*own, swap_seq(low_sum(*other), links))
        current = halve(current, bits[1], 1, links)
    else:
        own = halve(own, bits[1], 1, links)
        other = halve(other, bits[1], 1, links)
        current = (*own, swap_seq(low_sum(*other), links))
    for bit in range(2, index_bits()):
        current = halve(current, bits[bit], bit, links)
    mine = low_sum(*current)[0]
    theirs = swap_seq(mine, links, "last")
    if not by_rows:
        mine, theirs = mine[:, :half], theirs[:, :half]
    axis = 0 if by_rows else 1
    return pick_half(
        jnp.concatenate([mine, theirs], axis=axis), jnp.concatenate([theirs, mine], axis=axis)
    ).astype(jnp.float32)


def scatter_kernel(pairs, full_pairs, sources, n_in, *refs):
    factors, small = refs[:n_in], refs[n_in]
    refs = refs[n_in + 1 :]
    came, out, small_out = refs[:5], refs[5], refs[6]
    scratch = refs[7:]
    left_in, right_in, product, core_both, loaded = scratch[:5]
    sends, keeps = scratch[5:10], scratch[10:14]
    in_sem, load_sem, out_sem, core_send_sem, core_recv_sem, send_sem, recv_sem = scratch[14:21]
    small_sum, small_came, small_send, small_recv = scratch[21:]
    core_own, core_send = core_both.at[0], core_both.at[1]
    me = lax.axis_index("sp")
    plane = lax.axis_index("seq")

    def bit_of(bit):
        return (me // (1 << bit)) % 2

    def flip(bit):
        return (plane, me + (1 << bit) * (1 - 2 * bit_of(bit)))

    across = (1 - plane, me)
    core = bit_of(0)
    rows = out.shape[3]
    barrier = pltpu.get_barrier_semaphore()
    partners = [flip(bit) for bit in range(4)] + [across]
    for partner in partners:
        pl.semaphore_signal(
            barrier, inc=1, device_id=partner, device_id_type=pl.DeviceIdType.MESH
        )
    pl.semaphore_wait(barrier, len(partners))

    def remote(source, target, send, recv, partner):
        return pltpu.make_async_remote_copy(
            src_ref=source,
            dst_ref=target,
            send_sem=send,
            recv_sem=recv,
            device_id=partner,
            device_id_type=pl.DeviceIdType.MESH,
        )

    def half_of(side):
        return plane if side == 0 else 1 - plane

    def core_copy(pair, chunk, side):
        number = 2 * chunk + side
        return remote(
            core_send.at[number],
            came[0].at[pair, number],
            core_send_sem.at[number],
            core_recv_sem.at[pair, number],
            flip(0),
        )

    def stage_partner(stage, chunk):
        if stage == 1:
            return across if chunk == 0 else flip(1)
        if stage == 2:
            return flip(1) if chunk == 0 else across
        return flip(2) if stage == 3 else flip(3) if stage == 4 else across

    def stage_copy(stage, pair, chunk):
        source = sends[stage - 1].at[pair % 2, chunk]
        target = out.at[pair, chunk, plane] if stage == 5 else came[stage].at[pair, chunk]
        return remote(
            source,
            target,
            send_sem.at[stage - 1, pair % 2, chunk],
            recv_sem.at[stage - 1, pair, chunk],
            stage_partner(stage, chunk),
        )

    def out_copy(pair, chunk):
        return pltpu.make_async_copy(
            sends[4].at[pair % 2, chunk], out.at[pair, chunk, plane], out_sem.at[pair % 2, chunk]
        )

    def has(pair, chunk):
        return pair < (pairs if chunk == 0 else full_pairs)

    width = out.shape[4]

    def start_inputs(q, slot):
        for number, source in enumerate(sources):

            @pl.when(q == number)
            def _():
                for place, target, k in ((source[0], left_in, 0), (source[1], right_in, 1)):
                    pltpu.make_async_copy(
                        factors[place[0]].at[:, pl.ds(place[1], width)],
                        target.at[slot],
                        in_sem.at[slot, k],
                    ).start()

    def wait_inputs(slot):
        for target, k in ((left_in, 0), (right_in, 1)):
            pltpu.make_async_copy(
                factors[0].at[:, pl.ds(0, width)], target.at[slot], in_sem.at[slot, k]
            ).wait()

    def products(pair):
        start_inputs(4 * pair, 0)
        for chunk in (0, 1):

            @pl.when((pair > 0) & has(pair - 1, chunk))
            def _():
                for side in (0, 1):
                    core_copy(pair - 1, chunk, side).wait_send()

        last = pair // 6
        shrink = (2 - pair % 3) // 2 * (1 - last)

        def one(j, carry):
            slot = j % 2

            @pl.when(j + 1 < 4 - 2 * last)
            def _():
                start_inputs(4 * pair + j + 1, 1 - slot)

            wait_inputs(slot)
            product[...] = lax.dot_general(
                left_in[slot],
                right_in[slot],
                (((0,), (0,)), ((), ())),
                preferred_element_type=jnp.float32,
            )

            def store(i, carry):
                owner = shrink * (4 * j + i // 4) + (1 - shrink) * i
                quarter = shrink * (i % 4) + (1 - shrink) * j
                number = quarter // 2 * 2 + (quarter % 2 + plane) % 2
                first = pl.multiple_of(i * rows, 8)
                core_both[(owner + core) % 2, number, owner // 2] = product[
                    pl.ds(first, rows), :
                ].astype(jnp.bfloat16)
                return carry

            lax.fori_loop(0, 16, store, 0)
            return carry

        lax.fori_loop(0, 4 - 2 * last, one, 0)
        for chunk in (0, 1):

            @pl.when(has(pair, chunk))
            def _():
                for side in (0, 1):
                    core_copy(pair, chunk, side).start()

    def add(a, b):
        return (a.astype(jnp.float32) + b.astype(jnp.float32)).astype(jnp.bfloat16)

    def load(source, slot, blocks):
        return pltpu.make_async_copy(
            source, loaded.at[slot, pl.ds(0, blocks)], load_sem.at[slot]
        )

    def free_send(stage, pair, chunk):
        @pl.when(pair >= 2)
        def _():
            stage_copy(stage, pair, chunk).wait_send()

    def add_core(pair):
        slot = pair % 2
        x = bit_of(1)
        for chunk in (0, 1):

            @pl.when(has(pair, chunk))
            def _():
                for side in (1, 0):
                    core_copy(pair, chunk, side).wait_recv()
                    load(came[0].at[pair, 2 * chunk + side], side, 8).start()
                free_send(1, pair, chunk)
                for side in (1, 0):
                    number = 2 * chunk + side
                    load(came[0].at[pair, number], side, 8).wait()
                    if chunk == 0:
                        target = sends[0] if side == 1 else keeps[0]

                        def both(block, carry):
                            target[slot, chunk, block] = add(
                                core_own[number, block], loaded[side, block]
                            )
                            return carry

                        lax.fori_loop(0, 8, both, 0)
                    else:

                        def split(z, carry):
                            for target, block in (
                                (sends[0], 2 * z + 1 - x),
                                (keeps[0], 2 * z + x),
                            ):
                                target[slot, chunk, 4 * side + z] = add(
                                    core_own[number, block], loaded[side, block]
                                )
                            return carry

                        lax.fori_loop(0, 4, split, 0)
                    if chunk == 0 and side == 1:
                        stage_copy(1, pair, chunk).start()
                if chunk == 1:
                    stage_copy(1, pair, chunk).start()

    def add_stage(stage, pair):
        slot = pair % 2
        blocks = 16 >> stage
        for chunk in (0, 1):

            @pl.when(has(pair, chunk))
            def _():
                stage_copy(stage, pair, chunk).wait_recv()
                load(came[stage].at[pair, chunk], chunk, blocks).start()
        for chunk in (0, 1):

            @pl.when(has(pair, chunk))
            def _():
                free_send(stage + 1, pair, chunk)
                if stage == 4:

                    @pl.when(pair >= 2)
                    def _():
                        out_copy(pair, chunk).wait()

                load(came[stage].at[pair, chunk], chunk, blocks).wait()
                old, new = keeps[stage - 1], keeps[stage] if stage < 4 else None

                def one(i, carry):
                    if stage == 1 and chunk == 0:
                        x = bit_of(1)
                        gone, kept = 2 * i + 1 - x, 2 * i + x
                    elif stage == 1:
                        gone, kept = 4 + i, i
                    elif stage == 2:
                        low = bit_of(2)
                        gone, kept = 2 * i + 1 - low, 2 * i + low
                    else:
                        gone, kept = 1 - bit_of(3), bit_of(3)
                    sends[stage][slot, chunk, i] = add(
                        old[slot, chunk, gone], loaded[chunk, gone]
                    )
                    new[slot, chunk, i] = add(old[slot, chunk, kept], loaded[chunk, kept])
                    return carry

                if stage < 4:
                    lax.fori_loop(0, blocks // 2, one, 0)
                else:
                    sends[4][slot, chunk] = add(old[slot, chunk, 0], loaded[chunk, 0])
                    out_copy(pair, chunk).start()
                stage_copy(stage + 1, pair, chunk).start()

    def small_copy(stage):
        return remote(
            small_sum.at[stage],
            small_came.at[stage],
            small_send.at[stage],
            small_recv.at[stage],
            partners[stage],
        )

    small_sum[0] = small[...]
    small_copy(0).start()

    def turn(time, carry):
        for stage in range(len(partners)):

            @pl.when(time == stage)
            def _():
                small_copy(stage).wait_recv()
                total = small_sum[stage] + small_came[stage]
                if stage + 1 < len(partners):
                    small_sum[stage + 1] = total
                    small_copy(stage + 1).start()
                else:
                    small_out[...] = total

        for lag, work in (
            (1, add_core),
            (2, functools.partial(add_stage, 1)),
            (3, functools.partial(add_stage, 2)),
            (4, functools.partial(add_stage, 3)),
            (5, functools.partial(add_stage, 4)),
            (0, products),
        ):
            pair = time - lag

            @pl.when((pair >= 0) & (pair < pairs))
            def _():
                work(pair)

        return carry

    lax.fori_loop(0, pairs + 5, turn, 0)
    for stage in range(len(partners)):
        small_copy(stage).wait_send()
    for chunk in (0, 1):
        mine = pairs if chunk == 0 else full_pairs
        if mine == pairs:
            for side in (0, 1):
                core_copy(mine - 1, chunk, side).wait_send()
        for pair in range(max(mine - 2, 0), mine):
            out_copy(pair, chunk).wait()
            for stage in range(1, 6):
                stage_copy(stage, pair, chunk).wait_send()
        for pair in range(mine):
            stage_copy(5, pair, chunk).wait_recv()


def scatter_products(factors, sources, small, pairs, full_pairs, rows, width, collective_id):
    tokens = factors[0].shape[0]
    depth = 16 * rows
    low = jnp.bfloat16

    def blocks(*lead):
        return jax.ShapeDtypeStruct((*lead, rows, width), low)

    hbm = [
        blocks(pairs, 4, 8),
        blocks(pairs, 2, 8),
        blocks(pairs, 2, 4),
        blocks(pairs, 2, 2),
        blocks(pairs, 2, 1),
        blocks(pairs, 2, 2),
    ]
    any_space = pl.BlockSpec(memory_space=pl.ANY)

    def vmem(*lead):
        return pltpu.VMEM((*lead, rows, width), low)

    dma = pltpu.SemaphoreType.DMA
    whole = pl.BlockSpec(memory_space=pltpu.VMEM)
    *_, out, total = pl.pallas_call(
        functools.partial(scatter_kernel, pairs, full_pairs, sources, len(factors)),
        out_shape=hbm + [jax.ShapeDtypeStruct(small.shape, small.dtype)],
        in_specs=[any_space] * len(factors) + [whole],
        out_specs=[any_space] * len(hbm) + [whole],
        scratch_shapes=[
            pltpu.VMEM((2, tokens, width), low),
            pltpu.VMEM((2, tokens, width), low),
            pltpu.VMEM((depth, width), jnp.float32),
            vmem(2, 4, 8),
            vmem(2, 8),
            vmem(2, 2, 8),
            vmem(2, 2, 4),
            vmem(2, 2, 2),
            vmem(2, 2, 1),
            vmem(2, 2),
            vmem(2, 2, 8),
            vmem(2, 2, 4),
            vmem(2, 2, 2),
            vmem(2, 2, 1),
            dma((2, 2)),
            dma((2,)),
            dma((2, 2)),
            dma((4,)),
            dma((pairs, 4)),
            dma((5, 2, 2)),
            dma((5, pairs, 2)),
            pltpu.VMEM((5, *small.shape), small.dtype),
            pltpu.VMEM((5, *small.shape), small.dtype),
            dma((5,)),
            dma((5,)),
        ],
        compiler_params=pltpu.CompilerParams(
            collective_id=collective_id, has_side_effects=True, vmem_limit_bytes=58 << 20
        ),
        cost_estimate=pl.CostEstimate(
            flops=2 * len(sources) * depth * tokens * width,
            bytes_accessed=16 * len(sources) * depth * width,
            transcendentals=0,
        ),
    )(*factors, small)
    return out, total


def token_rows(gradients):
    return gradients.reshape(-1, gradients.shape[-1])


def scatter_all(terms, small):
    size = lax.axis_size("sp")
    if size != 16 or lax.axis_size("seq") != 2:
        links = {}
        flags = [(False, False), (True, True), (False, False), (False, True)]
        blocks = [
            [scatter_grad(*pair, *flag, links) for pair, flag in zip(block, flags)]
            for block in terms[:2]
        ]
        last = [scatter_grad(*pair, False, False, links) for pair in terms[2]]
        return blocks[0], blocks[1], last, lax.psum(small, ("seq", "sp"))
    factors, sources = [], []

    def add_factors(pair):
        factors.extend(token_rows(member) for member in pair)
        return len(factors) - 2, len(factors) - 1

    for expand, shrink, qkv, out in (terms[1], terms[0]):
        left, right = add_factors(shrink)
        sources += [((left, j * D), (right, 0)) for j in range(4)]
        left, right = add_factors(expand)
        sources += [((left, 0), (right, j * D)) for j in range(4)]
        left, right = add_factors(qkv)
        sources += [((left, 0), (right, j * D)) for j in range(3)]
        left, right = add_factors(out)
        sources.append(((left, 0), (right, 0)))
    for pair in terms[2]:
        left, right = add_factors(pair)
        sources.append(((left, 0), (right, 0)))
    done, total = scatter_products(factors, sources, small, 7, 6, D // size, D, 1)
    done = done.astype(jnp.float32)

    def quarter(pair, k):
        return done[pair, k // 2, k % 2]

    results = []
    for first in (0, 3):
        shrink = jnp.concatenate([quarter(first, k) for k in range(4)], axis=0)
        expand = jnp.concatenate([quarter(first + 1, k) for k in range(4)], axis=1)
        qkv = jnp.concatenate([quarter(first + 2, k) for k in range(3)], axis=1)
        results.append([expand, shrink, qkv, quarter(first + 2, 3)])
    return results[1], results[0], [quarter(6, 0), quarter(6, 1)], total


def halve(members, bit_value, bit, links):
    parts = [split_blocks(member, bit_value) for member in members]
    sent = low_sum(*[part[0] for part in parts])
    return (low_sum(*[part[1] for part in parts]), swap_sp(sent, bit, links))


def sum_seq(values):
    mine = values.astype(jnp.bfloat16)
    return mine.astype(jnp.float32) + swap_seq(mine, {}).astype(jnp.float32)


def triple_bias(query_bias, value_bias):
    head_query = query_bias.reshape(HEADS, 1, HEAD_DIM)
    head_value = value_bias.reshape(HEADS, 1, HEAD_DIM)
    return jnp.concatenate([head_query, jnp.zeros_like(head_query), head_value], axis=1).reshape(
        3 * D
    )


def pair_bias(value_bias):
    head_value = value_bias.reshape(HEADS, 1, HEAD_DIM)
    return jnp.concatenate([jnp.zeros_like(head_value), head_value], axis=1).reshape(2 * D)


def triple_bias_grad(totals):
    split_rows = totals.reshape(HEADS, 3, HEAD_DIM)
    return (split_rows[:, 0].reshape(D), split_rows[:, 2].reshape(D))


def frame_modulation(segment_ids, timesteps):
    onehot = (segment_ids[:, :, None] == jnp.arange(CLIPS)[None, None, :]).astype(jnp.float32)
    features = time_features(timesteps)
    return jnp.einsum("sfc,scz->sfz", onehot, features, precision=lax.Precision.HIGHEST)


def block_pieces(table_rows, frame_mod):
    modulation = table_rows[None, None] + frame_mod
    return [modulation[:, :, number][:, :, None, :] for number in range(6)]


def gated_back(grad_out, gating, branch):
    branch_grad = (gating * grad_out).astype(jnp.bfloat16)
    gate_grad = jnp.sum(grad_out * branch, axis=2, keepdims=True)
    return (branch_grad, gate_grad)


def to_pairs(values):
    groups, frames, patches, head_count, columns = values.shape
    reordered = jnp.transpose(values, (0, 1, 3, 2, 4))
    return reordered.reshape(lax.axis_size("sp"), -1, patches, columns)


def from_pairs(values, groups, frames):
    devices, pair_count, patches, columns = values.shape
    reordered = values.reshape(groups, frames, -1, patches, columns)
    return jnp.transpose(reordered, (0, 1, 3, 2, 4))


def pair_scores(triple):
    queries = triple[..., :HEAD_DIM]
    key_rows = triple[..., HEAD_DIM : 2 * HEAD_DIM]
    scores = jnp.einsum(
        "zkqe,zkre->zkqr", queries, key_rows, preferred_element_type=jnp.float32
    ) * HEAD_DIM ** (-0.5)
    return jax.nn.softmax(scores, axis=-1)


def attend_pairs(triple):
    attention = pair_scores(triple).astype(jnp.bfloat16)
    mixture = jnp.einsum(
        "zkqr,zkre->zkqe",
        attention,
        triple[..., 2 * HEAD_DIM :],
        preferred_element_type=jnp.float32,
    ).astype(jnp.bfloat16)
    return lax.all_to_all(mixture, "sp", split_axis=2, concat_axis=0, tiled=True)


def pair_backward(members):
    triple, out_grad = members
    queries = triple[..., :HEAD_DIM]
    key_rows = triple[..., HEAD_DIM : 2 * HEAD_DIM]
    value_rows = triple[..., 2 * HEAD_DIM :]
    attention = pair_scores(triple)
    rounded = attention.astype(jnp.bfloat16)
    prob_grad = jnp.einsum(
        "zkqe,zkre->zkqr", out_grad, value_rows, preferred_element_type=jnp.float32
    )
    centre = jnp.sum(prob_grad * attention, axis=-1, keepdims=True)
    score_grad = (attention * (prob_grad - centre)).astype(jnp.bfloat16)
    scaling = HEAD_DIM ** (-0.5)
    query_grad = (
        jnp.einsum("zkqr,zkre->zkqe", score_grad, key_rows, preferred_element_type=jnp.float32)
        * scaling
    )
    key_grad = (
        jnp.einsum("zkqr,zkqe->zkre", score_grad, queries, preferred_element_type=jnp.float32)
        * scaling
    )
    value_grad = jnp.einsum(
        "zkqr,zkqe->zkre", rounded, out_grad, preferred_element_type=jnp.float32
    )
    gradients = jnp.concatenate([query_grad, key_grad, value_grad], axis=-1).astype(jnp.bfloat16)
    return lax.all_to_all(gradients, "sp", split_axis=2, concat_axis=0, tiled=True)


def pair_attention(triple):
    groups, frames, patches = triple.shape[:3]
    shaped = triple.reshape(groups, frames, patches, HEADS, 3 * HEAD_DIM)
    pairs = lax.all_to_all(to_pairs(shaped), "sp", split_axis=0, concat_axis=2, tiled=True)
    exchanged = attend_pairs(pairs)
    return from_pairs(exchanged, groups, frames).reshape(groups, frames, patches, D), pairs


def pair_attention_back(pairs, mixture_grad):
    groups, frames, patches = mixture_grad.shape[:3]
    grad_shaped = mixture_grad.reshape(groups, frames, patches, HEADS, HEAD_DIM)
    returned = pair_backward(
        (
            pairs,
            lax.all_to_all(to_pairs(grad_shaped), "sp", split_axis=0, concat_axis=2, tiled=True),
        )
    )
    return from_pairs(returned, groups, frames).reshape(groups, frames, patches, 3 * D)


def feed_forward(residual, offset, scaling, gating, expand, shrink, vectors, start_row):
    hidden = modulate(residual, offset, scaling).astype(jnp.bfloat16)
    inner_sum = project(hidden, expand) + vectors[start_row : start_row + 4].reshape(FF)
    active = gelu_tanh(inner_sum).astype(jnp.bfloat16)
    branch = project(active, shrink) + vectors[3]
    return ((hidden, inner_sum, active, branch), residual + gating * branch)


def feed_backward(grad_out, residual, offset, scaling, gating, stored, expand, shrink):
    hidden, inner_sum, active, branch = stored
    branch_grad, gate_grad = gated_back(grad_out, gating, branch)
    shrink_grad = (active, branch_grad)
    active_grad = input_grad(branch_grad, shrink)
    gelu_value, gelu_back = jax.vjp(gelu_tanh, inner_sum)
    inner_grad = gelu_back(active_grad)[0].astype(jnp.bfloat16)
    expand_grad = (hidden, inner_grad)
    hidden_grad = input_grad(inner_grad, expand)
    norm_value, norm_back = jax.vjp(modulate, residual, offset, scaling)
    residual_grad, offset_grad, scaling_grad = norm_back(hidden_grad)
    return (
        grad_out + residual_grad,
        [offset_grad, scaling_grad, gate_grad],
        (expand_grad, shrink_grad, column_sum(inner_grad), column_sum(branch_grad)),
    )


def table_sums(members):
    return jnp.stack([jnp.sum(member, axis=(0, 1, 2)) for member in members])


def spatial_forward(residual, weights, frame_mod):
    qkv_weight, out_weight, expand, shrink, vectors = weights
    vectors_f = as_float(vectors)
    pieces = block_pieces(vectors_f[4:10], frame_mod)
    hidden = modulate(residual, pieces[0], pieces[1]).astype(jnp.bfloat16)
    triple = (project(hidden, qkv_weight) + triple_bias(vectors_f[0], vectors_f[1])).astype(
        jnp.bfloat16
    )
    mixture, pairs = pair_attention(triple)
    branch = project(mixture, out_weight) + vectors_f[2]
    middle = residual + pieces[2] * branch
    stored_ffn, result = feed_forward(
        middle, pieces[3], pieces[4], pieces[5], expand, shrink, vectors_f, 10
    )
    return (result, (hidden, pairs, mixture, branch, middle, stored_ffn))


def spatial_backward(grad_out, residual, weights, frame_mod, stored):
    qkv_weight, out_weight, expand, shrink, vectors = weights
    pieces = block_pieces(as_float(vectors)[4:10], frame_mod)
    hidden, pairs, mixture, branch, middle, stored_ffn = stored
    middle_grad, ffn_table, ffn_grads = feed_backward(
        grad_out, middle, pieces[3], pieces[4], pieces[5], stored_ffn, expand, shrink
    )
    branch_grad, gate_grad = gated_back(middle_grad, pieces[2], branch)
    out_weight_grad = (mixture, branch_grad)
    out_bias = column_sum(branch_grad)
    mixture_grad = input_grad(branch_grad, out_weight).astype(jnp.bfloat16)
    triple_grad = pair_attention_back(pairs, mixture_grad)
    qkv_grad = (hidden, triple_grad)
    query_bias, value_bias = triple_bias_grad(column_sum(triple_grad))
    hidden_grad = input_grad(triple_grad, qkv_weight)
    norm_value, norm_back = jax.vjp(modulate, residual, pieces[0], pieces[1])
    residual_grad, offset_grad, scaling_grad = norm_back(hidden_grad)
    table_grad = table_sums([offset_grad, scaling_grad, gate_grad] + ffn_table)
    vector_grad = jnp.concatenate(
        [
            jnp.stack([query_bias, value_bias, out_bias, ffn_grads[3]]),
            table_grad,
            ffn_grads[2].reshape(4, D),
        ],
        axis=0,
    )
    return (
        middle_grad + residual_grad,
        (qkv_grad, out_weight_grad, ffn_grads[0], ffn_grads[1], vector_grad),
    )


def temporal_scores(triple, same_clip):
    scores = jnp.einsum(
        "sfphe,sgphe->sphfg",
        triple[..., :HEAD_DIM],
        triple[..., HEAD_DIM : 2 * HEAD_DIM],
        preferred_element_type=jnp.float32,
    ) * HEAD_DIM ** (-0.5)
    return jax.nn.softmax(jnp.where(same_clip, scores, masked_score), axis=-1)


def caption_scores(queries, keyval, allowed):
    scores = jnp.einsum(
        "sfphe,srhe->sfphr", queries, keyval[..., :HEAD_DIM], preferred_element_type=jnp.float32
    ) * HEAD_DIM ** (-0.5)
    return jax.nn.softmax(jnp.where(allowed, scores, masked_score), axis=-1)


def temporal_forward(residual, weights, frame_mod, same_clip, allowed, context):
    qkv_weight, out_weight, expand, shrink, query_weight, keyval_weight, cross_weight, vectors = (
        weights
    )
    vectors_f = as_float(vectors)
    pieces = block_pieces(vectors_f[8:14], frame_mod)
    groups, frames, patches = residual.shape[:3]
    hidden = modulate(residual, pieces[0], pieces[1]).astype(jnp.bfloat16)
    triple = (project(hidden, qkv_weight) + triple_bias(vectors_f[0], vectors_f[1])).astype(
        jnp.bfloat16
    )
    triple = triple.reshape(groups, frames, patches, HEADS, 3 * HEAD_DIM)
    attention = temporal_scores(triple, same_clip).astype(jnp.bfloat16)
    mixture = (
        jnp.einsum(
            "sphfg,sgphe->sfphe",
            attention,
            triple[..., 2 * HEAD_DIM :],
            preferred_element_type=jnp.float32,
        )
        .astype(jnp.bfloat16)
        .reshape(groups, frames, patches, D)
    )
    branch = project(mixture, out_weight) + vectors_f[2]
    middle = residual + pieces[2] * branch
    lowered = middle.astype(jnp.bfloat16)
    queries = (project(lowered, query_weight) + vectors_f[4]).astype(jnp.bfloat16)
    queries = queries.reshape(groups, frames, patches, HEADS, HEAD_DIM)
    keyval = (project(context, keyval_weight) + pair_bias(vectors_f[5])).astype(jnp.bfloat16)
    keyval = keyval.reshape(groups, -1, HEADS, 2 * HEAD_DIM)
    cross_probs = caption_scores(queries, keyval, allowed).astype(jnp.bfloat16)
    cross_mix = (
        jnp.einsum(
            "sfphr,srhe->sfphe",
            cross_probs,
            keyval[..., HEAD_DIM:],
            preferred_element_type=jnp.float32,
        )
        .astype(jnp.bfloat16)
        .reshape(groups, frames, patches, D)
    )
    crossed = middle + project(cross_mix, cross_weight) + vectors_f[6]
    stored_ffn, result = feed_forward(
        crossed, pieces[3], pieces[4], pieces[5], expand, shrink, vectors_f, 14
    )
    return (
        result,
        (
            hidden,
            triple,
            mixture,
            branch,
            middle,
            lowered,
            queries,
            keyval,
            cross_mix,
            crossed,
            stored_ffn,
        ),
    )


def temporal_backward(grad_out, residual, weights, frame_mod, same_clip, allowed, stored):
    qkv_weight, out_weight, expand, shrink, query_weight, keyval_weight, cross_weight, vectors = (
        weights
    )
    pieces = block_pieces(as_float(vectors)[8:14], frame_mod)
    (
        hidden,
        triple,
        mixture,
        branch,
        middle,
        lowered,
        queries,
        keyval,
        cross_mix,
        crossed,
        stored_ffn,
    ) = stored
    groups, frames, patches = residual.shape[:3]
    scaling = HEAD_DIM ** (-0.5)
    crossed_grad, ffn_table, ffn_grads = feed_backward(
        grad_out, crossed, pieces[3], pieces[4], pieces[5], stored_ffn, expand, shrink
    )
    cross_branch_grad = crossed_grad.astype(jnp.bfloat16)
    cross_weight_grad = (cross_mix, cross_branch_grad)
    cross_bias = column_sum(cross_branch_grad)
    mix_grad = input_grad(cross_branch_grad, cross_weight).astype(jnp.bfloat16)
    mix_grad = mix_grad.reshape(groups, frames, patches, HEADS, HEAD_DIM)
    cross_probs = caption_scores(queries, keyval, allowed)
    rounded = cross_probs.astype(jnp.bfloat16)
    prob_grad = jnp.einsum(
        "sfphe,srhe->sfphr", mix_grad, keyval[..., HEAD_DIM:], preferred_element_type=jnp.float32
    )
    centre = jnp.sum(prob_grad * cross_probs, axis=-1, keepdims=True)
    score_grad = (cross_probs * (prob_grad - centre)).astype(jnp.bfloat16)
    query_grad = (
        jnp.einsum(
            "sfphr,srhe->sfphe",
            score_grad,
            keyval[..., :HEAD_DIM],
            preferred_element_type=jnp.float32,
        )
        * scaling
    )
    query_grad = query_grad.astype(jnp.bfloat16).reshape(groups, frames, patches, D)
    key_grad = (
        jnp.einsum("sfphr,sfphe->srhe", score_grad, queries, preferred_element_type=jnp.float32)
        * scaling
    )
    value_grad = jnp.einsum(
        "sfphr,sfphe->srhe", rounded, mix_grad, preferred_element_type=jnp.float32
    )
    keyval_grad = jnp.concatenate([key_grad, value_grad], axis=-1).reshape(groups, -1, 2 * D)
    keyval_grad = lax.psum(keyval_grad.astype(jnp.bfloat16), "sp")
    query_weight_grad = (lowered, query_grad)
    cross_query_bias = column_sum(query_grad)
    middle_grad = crossed_grad + input_grad(query_grad, query_weight)
    branch_grad, gate_grad = gated_back(middle_grad, pieces[2], branch)
    out_weight_grad = (mixture, branch_grad)
    out_bias = column_sum(branch_grad)
    mixture_grad = input_grad(branch_grad, out_weight).astype(jnp.bfloat16)
    mixture_grad = mixture_grad.reshape(groups, frames, patches, HEADS, HEAD_DIM)
    attention = temporal_scores(triple, same_clip)
    rounded_t = attention.astype(jnp.bfloat16)
    prob_grad_t = jnp.einsum(
        "sfphe,sgphe->sphfg",
        mixture_grad,
        triple[..., 2 * HEAD_DIM :],
        preferred_element_type=jnp.float32,
    )
    centre_t = jnp.sum(prob_grad_t * attention, axis=-1, keepdims=True)
    score_grad_t = (attention * (prob_grad_t - centre_t)).astype(jnp.bfloat16)
    query_part = (
        jnp.einsum(
            "sphfg,sgphe->sfphe",
            score_grad_t,
            triple[..., HEAD_DIM : 2 * HEAD_DIM],
            preferred_element_type=jnp.float32,
        )
        * scaling
    )
    key_part = (
        jnp.einsum(
            "sphfg,sfphe->sgphe",
            score_grad_t,
            triple[..., :HEAD_DIM],
            preferred_element_type=jnp.float32,
        )
        * scaling
    )
    value_part = jnp.einsum(
        "sphfg,sfphe->sgphe", rounded_t, mixture_grad, preferred_element_type=jnp.float32
    )
    triple_grad = jnp.concatenate([query_part, key_part, value_part], axis=-1).astype(jnp.bfloat16)
    triple_grad = triple_grad.reshape(groups, frames, patches, 3 * D)
    qkv_grad = (hidden, triple_grad)
    query_bias, value_bias = triple_bias_grad(column_sum(triple_grad))
    hidden_grad = input_grad(triple_grad, qkv_weight)
    norm_value, norm_back = jax.vjp(modulate, residual, pieces[0], pieces[1])
    residual_grad, offset_grad, scaling_grad = norm_back(hidden_grad)
    table_grad = table_sums([offset_grad, scaling_grad, gate_grad] + ffn_table)
    zero_row = jnp.zeros((D,), jnp.float32)
    vector_grad = jnp.concatenate(
        [
            jnp.stack(
                [
                    query_bias,
                    value_bias,
                    out_bias,
                    ffn_grads[3],
                    cross_query_bias,
                    zero_row,
                    cross_bias,
                    zero_row,
                ]
            ),
            table_grad,
            ffn_grads[2].reshape(4, D),
        ],
        axis=0,
    )
    terms = (
        qkv_grad,
        out_weight_grad,
        ffn_grads[0],
        ffn_grads[1],
        query_weight_grad,
        cross_weight_grad,
        vector_grad,
    )
    return (middle_grad + residual_grad, terms, keyval_grad)


def on_device(
    video,
    segment_ids,
    timesteps,
    drop_mask,
    captions,
    null_caption,
    caption_weight,
    spatial_qkv,
    spatial_out,
    spatial_expand,
    spatial_shrink,
    spatial_vectors,
    temporal_qkv,
    temporal_out,
    temporal_expand,
    temporal_shrink,
    cross_query,
    cross_keyval,
    cross_out,
    temporal_vectors,
    cotangent,
):
    groups, frames, patches = video.shape[:3]
    size = lax.axis_size("sp")
    third = D
    wide = [
        spatial_qkv,
        spatial_out,
        spatial_expand,
        temporal_qkv,
        temporal_out,
        cross_query,
        cross_keyval,
        cross_out,
    ]

    def rounds_of(rows):
        def block_round(qkv, out):
            return columns_round(
                (qkv, 0, third), (qkv, third, third), (qkv, 2 * third, third), (out, 0, third)
            )

        def expand_round(weight):
            quarter = FF // 4
            return columns_round(*[(weight, k * quarter, quarter) for k in range(4)])

        return [
            block_round(0, 1),
            expand_round(2),
            rows_round(8, rows),
            block_round(3, 4),
            columns_round((5, 0, third), (6, 0, third), (6, third, third), (7, 0, third)),
        ]

    (
        full_sqkv,
        full_sout,
        full_sexp,
        full_tqkv,
        full_tout,
        full_cq,
        full_ckv,
        full_cout,
        full_sshr,
        all_vectors,
    ) = gather_all(
        [spatial_shrink],
        wide,
        jnp.concatenate([spatial_vectors, temporal_vectors], axis=0),
        rounds_of,
        0,
    )
    full_sqkv, expand_shard, shrink_shard = lax.optimization_barrier(
        (full_sqkv, temporal_expand, temporal_shrink)
    )
    full_texp = lax.all_gather(expand_shard, "sp", axis=0, tiled=True)
    full_tshr = lax.all_gather(shrink_shard, "sp", axis=0, tiled=True)
    n_spatial = spatial_vectors.shape[0]
    spatial = (full_sqkv, full_sout, full_sexp, full_sshr, all_vectors[:n_spatial])
    temporal = (
        full_tqkv,
        full_tout,
        full_texp,
        full_tshr,
        full_cq,
        full_ckv,
        full_cout,
        all_vectors[n_spatial:],
    )
    dropped = (drop_mask > 0).astype(jnp.float32)
    text_local = jnp.where(drop_mask[:, :, None, None] > 0, null_caption[None, None], captions)
    text_rows = text_local.reshape(groups, CLIPS * CAP, -1)
    caption_sum = lax.psum(project(text_rows, caption_weight).astype(jnp.float32), "sp")
    caption_sum, first = lax.optimization_barrier((caption_sum, spatial[0]))
    spatial = (first, *spatial[1:])
    frame_mod = frame_modulation(segment_ids, timesteps).reshape(groups, frames, 6, D)
    same_clip = (segment_ids[:, :, None] == segment_ids[:, None, :])[:, None, None]
    row_clip = jnp.arange(CLIPS * CAP) // CAP
    allowed = (segment_ids[:, :, None] == row_clip[None, None, :])[:, :, None, None, :]
    residual = video.astype(jnp.float32)
    middle, spatial_kept = spatial_forward(residual, spatial, frame_mod)
    context = (caption_sum + as_float(temporal[7])[7]).astype(jnp.bfloat16)
    result, temporal_kept = temporal_forward(
        middle, temporal, frame_mod, same_clip, allowed, context
    )
    output = result.astype(jnp.bfloat16)
    middle_grad, temporal_terms, keyval_grad = temporal_backward(
        cotangent.astype(jnp.float32),
        middle,
        temporal,
        frame_mod,
        same_clip,
        allowed,
        temporal_kept,
    )
    shard_rows = D // lax.axis_size("sp")
    first_row = lax.axis_index("sp") * shard_rows
    video_grad, spatial_terms = spatial_backward(
        middle_grad, residual, spatial, frame_mod, spatial_kept
    )
    spatial_sums, temporal_sums, cross_sums, vector_total = scatter_all(
        (
            (spatial_terms[2], spatial_terms[3], spatial_terms[0], spatial_terms[1]),
            (temporal_terms[2], temporal_terms[3], temporal_terms[0], temporal_terms[1]),
            (temporal_terms[4], temporal_terms[5]),
        ),
        jnp.concatenate([spatial_terms[4], temporal_terms[6]], axis=0),
    )
    vector_total = lax.dynamic_slice_in_dim(vector_total, first_row, shard_rows, 1)
    keyval_grad, vector_total = lax.optimization_barrier((keyval_grad, vector_total))
    context_grad = input_grad(keyval_grad, temporal[5]).astype(jnp.bfloat16)
    local_context = lax.dynamic_slice_in_dim(context, first_row, shard_rows, 2)
    keyval_weight_grad = weight_grad(local_context, keyval_grad)
    value_bias_full = column_sum(keyval_grad).reshape(HEADS, 2, HEAD_DIM)[:, 1].reshape(D)
    caption_bias_full = column_sum(context_grad)
    caption_weight_grad = weight_grad(text_rows, context_grad)
    text_grad = input_grad(context_grad, caption_weight).reshape(groups, CLIPS, CAP, -1)
    null_grad = jnp.sum(text_grad * dropped[:, :, None, None], axis=(0, 1))
    own_rows = [
        lax.dynamic_slice_in_dim(row, first_row, shard_rows, 0)
        for row in (value_bias_full, caption_bias_full)
    ]
    width = null_grad.shape[1]
    flat = jnp.stack([jnp.pad(row, (0, width - shard_rows)) for row in own_rows])
    small_total = sum_seq(jnp.concatenate([null_grad, flat], axis=0))
    null_total = small_total[: null_grad.shape[0]]
    bias_total = small_total[null_grad.shape[0] :, :shard_rows]
    vector_total = vector_total.at[n_spatial + 5].add(bias_total[0])
    vector_total = vector_total.at[n_spatial + 7].add(bias_total[1])
    return (
        output,
        video_grad.astype(jnp.bfloat16),
        null_total,
        sum_seq(caption_weight_grad),
        spatial_sums[2],
        spatial_sums[3],
        spatial_sums[0],
        spatial_sums[1],
        vector_total[:n_spatial],
        temporal_sums[2],
        temporal_sums[3],
        temporal_sums[0],
        temporal_sums[1],
        cross_sums[0],
        sum_seq(keyval_weight_grad),
        cross_sums[1],
        vector_total[n_spatial:],
    )


def solution(mesh):
    return jax.shard_map(
        on_device,
        mesh=mesh,
        in_specs=(
            P("seq", None, "sp", None),
            P("seq", None),
            P("seq", None),
            P("seq", None),
            P("seq", None, None, "sp"),
            P(None, "sp"),
            P("sp", None),
            P("sp", None),
            P("sp", None),
            P("sp", None),
            P("sp", None),
            P(None, "sp"),
            P("sp", None),
            P("sp", None),
            P("sp", None),
            P("sp", None),
            P("sp", None),
            P("sp", None),
            P("sp", None),
            P(None, "sp"),
            P("seq", None, "sp", None),
        ),
        out_specs=(
            P("seq", None, "sp", None),
            P("seq", None, "sp", None),
            P(None, "sp"),
            P("sp", None),
            P("sp", None),
            P("sp", None),
            P("sp", None),
            P("sp", None),
            P(None, "sp"),
            P("sp", None),
            P("sp", None),
            P("sp", None),
            P("sp", None),
            P("sp", None),
            P("sp", None),
            P("sp", None),
            P(None, "sp"),
        ),
        check_vma=False,
    )
```

```python
import functools
import math

import jax
import jax.numpy as jnp
from jax import lax
from jax.experimental import pallas as pl
from jax.experimental.pallas import tpu as pltpu
from jax.sharding import PartitionSpec as P

D = 1152
HEADS = 16
HEAD_DIM = 72
FF = 4608
CAP = 120
CLIPS = 2


norm_eps = 1e-06
masked_score = -1e30


def time_features(timestep):
    half_width = 3 * D
    frequency = jnp.exp(
        jnp.arange(half_width, dtype=jnp.float32) * (-math.log(10000.0) / half_width)
    )
    angles = timestep.astype(jnp.float32)[..., None] * frequency
    return 0.5 * jnp.concatenate([jnp.cos(angles), jnp.sin(angles)], axis=-1)


def layer_norm(residual):
    center = residual - jnp.mean(residual, axis=-1, keepdims=True)
    return center * lax.rsqrt(jnp.mean(center * center, axis=-1, keepdims=True) + norm_eps)


def modulate(residual, offset, scaling):
    return layer_norm(residual) * (1.0 + scaling) + offset


def gelu_tanh(inner_sum):
    return jax.nn.gelu(inner_sum, approximate=True)


def as_float(member):
    return member.astype(jnp.float32)


def project(inputs, weight):
    return jnp.dot(inputs, weight, preferred_element_type=jnp.float32)


def weight_grad(inputs, gradients):
    left_rows = inputs.reshape(-1, inputs.shape[-1])
    right_rows = gradients.reshape(-1, gradients.shape[-1])
    return lax.dot_general(
        left_rows, right_rows, (((0,), (0,)), ((), ())), preferred_element_type=jnp.float32
    )


def input_grad(gradients, weight):
    return lax.dot_general(
        gradients,
        weight,
        (((gradients.ndim - 1,), (1,)), ((), ())),
        preferred_element_type=jnp.float32,
    )


def column_sum(gradients):
    return jnp.sum(gradients.astype(jnp.float32).reshape(-1, gradients.shape[-1]), axis=0)


def index_bits():
    return lax.axis_size("sp").bit_length() - 1


def after(values, earlier):
    if not earlier:
        return values
    return lax.optimization_barrier((values, tuple(earlier)))[0]


def in_turn(links, key, values, exchange):
    last = links.get(key)
    result = exchange(values if last is None else after(values, [last]))
    links[key] = result
    return result


def swap_sp(values, bit, links):
    size = lax.axis_size("sp")
    pairs = [(i, i ^ (1 << bit)) for i in range(size)]
    return in_turn(links, min(bit, 2), values, lambda v: lax.ppermute(v, "sp", pairs))


def swap_seq(values, links, key="seq"):
    return in_turn(links, key, values, lambda v: lax.ppermute(v, "seq", [(0, 1), (1, 0)]))


def gather_kernel(rounds, n_in, n_out, *refs):
    shards, outs = refs[:n_in], refs[n_in : n_in + n_out]
    local_sem, send_sem, recv_sem, small_local, small_send, small_recv = refs[n_in + n_out :]
    me = lax.axis_index("sp")
    plane = lax.axis_index("seq")
    count = index_bits()
    place = [(me // (1 << (count - 1 - d))) % 2 for d in range(count)]

    def flip(bit):
        mine = (me // (1 << bit)) % 2
        return (plane, me + (1 << bit) * (1 - 2 * mine))

    across = (1 - plane, me)
    partners = [flip(bit) for bit in range(count)] + [across]
    barrier = pltpu.get_barrier_semaphore()
    for partner in partners:
        pl.semaphore_signal(
            barrier, inc=1, device_id=partner, device_id_type=pl.DeviceIdType.MESH
        )
    pl.semaphore_wait(barrier, len(partners))

    def part(ref, lead, piece):
        weight, rows, columns = piece
        if rows is None:
            return ref.at[(*lead, slice(None), pl.ds(*columns))]
        half, first, size = rows
        return ref.at[(*lead, half, pl.ds(first, size), slice(None))]

    def stage_places(stage):
        return tuple(
            slice(None) if d < stage else place[d] for d in range(count)
        )

    for own_half in (0, 1):

        @pl.when(plane == own_half)
        def _():
            started = []

            def send(number, stage, slot, source, target, partner):
                copy = pltpu.make_async_remote_copy(
                    src_ref=source,
                    dst_ref=target,
                    send_sem=send_sem.at[number, stage, slot],
                    recv_sem=recv_sem.at[number, stage, slot],
                    device_id=partner,
                    device_id_type=pl.DeviceIdType.MESH,
                )
                copy.start()
                return copy

            def own(chunk):
                return chunk[own_half]

            def other(chunk):
                return chunk[1 - own_half]

            def step(number, stage):
                (first, second), late = rounds[number]
                lead = stage_places(min(stage, count - 2))
                four = [piece for chunk in (first, second) for piece in (own(chunk), other(chunk))]
                if late and stage < count:
                    partner = [flip(1), across, *[flip(bit) for bit in range(count - 1, 1, -1)]][stage]
                    moves = [(piece, partner) for piece in (four if stage > 1 else four[::2])]
                    lead = tuple(
                        slice(None) if d < stage - 2 or (d == count - 2 and stage) else place[d]
                        for d in range(count)
                    )
                elif stage < count - 2:
                    moves = [(own(first), flip(count - 1 - stage)), (own(second), flip(count - 1 - stage))]
                elif stage == count - 2:
                    moves = [(own(first), flip(1)), (own(second), across)]
                elif stage == count - 1:
                    moves = [
                        (own(first), across),
                        (own(second), flip(1)),
                        (other(second), flip(1)),
                    ]
                else:
                    moves = [(piece, flip(0)) for piece in four]
                copies = []
                for slot, (piece, partner) in enumerate(moves):
                    places = lead
                    if not late and stage == count - 1 and partner is across or stage == count:
                        places = stage_places(count - 1)
                    target = part(outs[piece[0]], places, piece)
                    source = target
                    if stage == 0:
                        source = part(shards[piece[0]], (), piece)
                    copies.append(send(number, stage, slot, source, target, partner))
                return copies

            def small_step(stage):
                target = outs[-1].at[stage_places(stage)]
                copy = pltpu.make_async_remote_copy(
                    src_ref=target if stage else shards[-1],
                    dst_ref=target,
                    send_sem=small_send.at[stage],
                    recv_sem=small_recv.at[stage],
                    device_id=flip(count - 1 - stage),
                    device_id_type=pl.DeviceIdType.MESH,
                )
                copy.start()
                return copy

            copies = {}
            small = [small_step(0)]
            local = [
                pltpu.make_async_copy(shards[-1], outs[-1].at[stage_places(0)], small_local)
            ]
            local[0].start()
            for number, (pair, late) in enumerate(rounds):
                for slot, chunk in enumerate(pair):
                    piece = own(chunk)
                    copy = pltpu.make_async_copy(
                        part(shards[piece[0]], (), piece),
                        part(outs[piece[0]], stage_places(0), piece),
                        local_sem.at[number, slot],
                    )
                    copy.start()
                    local.append(copy)
            lags = {
                False: [*range(count), count + 1],
                True: [*range(count - 1), count, count + 2],
            }
            for time in range(len(rounds) + count + 2):
                if time == 1:
                    for copy in local:
                        copy.wait()
                if 0 < time < count:
                    small[-1].wait_recv()
                    small.append(small_step(time))
                for stage in range(count + 1):
                    for number, (_, late) in enumerate(rounds):
                        if number != time - lags[late][stage]:
                            continue
                        if stage:
                            for copy in copies[number, stage - 1]:
                                copy.wait_recv()
                        copies[number, stage] = step(number, stage)
            small[-1].wait_recv()
            for copy in small:
                copy.wait_send()
            for number in range(len(rounds)):
                for copy in copies[number, count]:
                    copy.wait_recv()
                for stage in range(count + 1):
                    for copy in copies[number, stage]:
                        copy.wait_send()


def gather_weights(shards, rounds, collective_id):
    size = lax.axis_size("sp")
    lead = (2,) * index_bits()
    shapes = [lead + shard.shape for shard in shards]
    total = sum(2 * math.prod(shape) for shape in shapes)
    stages = index_bits() + 1
    placed = pl.pallas_call(
        functools.partial(gather_kernel, rounds, len(shards), len(shards)),
        out_shape=[jax.ShapeDtypeStruct(shape, jnp.bfloat16) for shape in shapes],
        in_specs=[pl.BlockSpec(memory_space=pltpu.VMEM)] * len(shards),
        out_specs=[pl.BlockSpec(memory_space=pl.ANY)] * len(shards),
        scratch_shapes=[
            pltpu.SemaphoreType.DMA((len(rounds), 2)),
            pltpu.SemaphoreType.DMA((len(rounds), stages, 4)),
            pltpu.SemaphoreType.DMA((len(rounds), stages, 4)),
            pltpu.SemaphoreType.DMA,
            pltpu.SemaphoreType.DMA((index_bits(),)),
            pltpu.SemaphoreType.DMA((index_bits(),)),
        ],
        compiler_params=pltpu.CompilerParams(
            collective_id=collective_id, has_side_effects=True, vmem_limit_bytes=32 << 20
        ),
        cost_estimate=pl.CostEstimate(flops=0, bytes_accessed=total, transcendentals=0),
    )(*shards)
    *large, small = placed
    full = [member.reshape(size * math.prod(member.shape[index_bits() : -1]), -1) for member in large]
    small = jnp.swapaxes(small.reshape(size, *small.shape[-2:]), 0, 1)
    return full + [small.reshape(small.shape[0], -1)]


def columns_round(*quarters, late=False):
    pieces = [(weight, None, (first, width)) for weight, first, width in quarters]
    return ((pieces[0], pieces[2]), (pieces[1], pieces[3])), late


def rows_round(weight, rows):
    cut = rows // 32 * 16 + (rows // 16 % 2) * 16
    return (
        ((weight, (0, 0, cut), None), (weight, (1, 0, cut), None)),
        ((weight, (0, cut, rows - cut), None), (weight, (1, cut, rows - cut), None)),
    ), False


def gather_all(tall, wide, small, rounds_of, collective_id):
    if wide[0].shape[0] % 8 or lax.axis_size("seq") != 2:
        full = [lax.all_gather(shard, "sp", axis=0, tiled=True) for shard in wide + tall]
        return full + [lax.all_gather(small, "sp", axis=1, tiled=True)]
    shards = list(wide) + [
        shard.reshape(2, shard.shape[0] // 2, shard.shape[1]) for shard in tall
    ]
    shards.append(small)
    return gather_weights(shards, rounds_of(tall[0].shape[0] // 2), collective_id)


def pick_half(first, second):
    return jnp.where(lax.axis_index("seq") == 0, first, second)


def low_sum(*members):
    total = members[0].astype(jnp.float32)
    for member in members[1:]:
        total = total + member.astype(jnp.float32)
    return total.astype(jnp.bfloat16)


def pick(values, index, axis):
    return lax.dynamic_index_in_dim(values, index, axis, keepdims=False)


def split_blocks(values, bit_value):
    paired = values.reshape(values.shape[0] // 2, 2, *values.shape[1:])
    return pick(paired, 1 - bit_value, 1), pick(paired, bit_value, 1)


def scatter_grad(inputs, gradients, by_rows, seq_first, links):
    size = lax.axis_size("sp")
    me = lax.axis_index("sp")
    plane = lax.axis_index("seq")
    bits = [(me // (1 << b)) % 2 for b in range(index_bits())]
    left = inputs.reshape(-1, inputs.shape[-1])
    right = gradients.reshape(-1, gradients.shape[-1])
    depth = left.shape[1]
    columns = right.shape[1]
    rows = depth // size
    half = (rows if by_rows else columns) // 2
    if not by_rows:
        padded = -(-half // 128) * 128
        fill = ((0, 0), (0, padded - half))
        right = jnp.concatenate(
            [
                jnp.pad(pick_half(right[:, :half], right[:, half:]), fill),
                jnp.pad(pick_half(right[:, half:], right[:, :half]), fill),
            ],
            axis=1,
        )
    total = lax.dot_general(
        left, right, (((0,), (0,)), ((), ())), preferred_element_type=jnp.float32
    ).astype(jnp.bfloat16)
    if by_rows:
        total = total.reshape(size, 2, half, columns)
    else:
        total = total.reshape(size, rows, 2 * padded)
    sent, kept = split_blocks(total, bits[0])
    came = swap_sp(sent, 0, links)
    if by_rows:
        own, other = [
            (pick(kept, which, 1), pick(came, which, 1)) for which in (plane, 1 - plane)
        ]
    else:
        own = (kept[:, :, :padded], came[:, :, :padded])
        other = (kept[:, :, padded:], came[:, :, padded:])
    if seq_first:
        current = (*own, swap_seq(low_sum(*other), links))
        current = halve(current, bits[1], 1, links)
    else:
        own = halve(own, bits[1], 1, links)
        other = halve(other, bits[1], 1, links)
        current = (*own, swap_seq(low_sum(*other), links))
    for bit in range(2, index_bits()):
        current = halve(current, bits[bit], bit, links)
    mine = low_sum(*current)[0]
    theirs = swap_seq(mine, links, "last")
    if not by_rows:
        mine, theirs = mine[:, :half], theirs[:, :half]
    axis = 0 if by_rows else 1
    return pick_half(
        jnp.concatenate([mine, theirs], axis=axis), jnp.concatenate([theirs, mine], axis=axis)
    ).astype(jnp.float32)


def scatter_kernel(pairs, full_pairs, shrink_pairs, late_pairs, sources, n_in, *refs):
    factors, small = refs[:n_in], refs[n_in]
    refs = refs[n_in + 1 :]
    came, out, small_out = refs[:5], refs[5], refs[6]
    scratch = refs[7:]
    left_in, right_in, product, core_both, loaded = scratch[:5]
    sends, keeps = scratch[5:10], scratch[10:14]
    in_sem, load_sem, out_sem, core_send_sem, core_recv_sem, send_sem, recv_sem = scratch[14:21]
    small_sum, small_came, small_send, small_recv = scratch[21:]
    core_own, core_send = core_both.at[0], core_both.at[1]
    me = lax.axis_index("sp")
    plane = lax.axis_index("seq")

    def bit_of(bit):
        return (me // (1 << bit)) % 2

    def flip(bit):
        return (plane, me + (1 << bit) * (1 - 2 * bit_of(bit)))

    across = (1 - plane, me)
    core = bit_of(0)
    rows = out.shape[3]
    barrier = pltpu.get_barrier_semaphore()
    partners = [flip(bit) for bit in range(4)] + [across]
    for partner in partners:
        pl.semaphore_signal(
            barrier, inc=1, device_id=partner, device_id_type=pl.DeviceIdType.MESH
        )
    pl.semaphore_wait(barrier, len(partners))

    def among(pair, chosen):
        return sum([1 // (1 + (pair - p) * (pair - p)) for p in chosen], 0 * pair)

    def remote(source, target, send, recv, partner):
        return pltpu.make_async_remote_copy(
            src_ref=source,
            dst_ref=target,
            send_sem=send,
            recv_sem=recv,
            device_id=partner,
            device_id_type=pl.DeviceIdType.MESH,
        )

    def half_of(side):
        return plane if side == 0 else 1 - plane

    def core_copy(pair, chunk, side):
        number = 2 * chunk + side
        return remote(
            core_send.at[number],
            came[0].at[pair, number],
            core_send_sem.at[number],
            core_recv_sem.at[pair, number],
            flip(0),
        )

    def is_late(pair):
        return among(pair, late_pairs)

    def is_second(pair, chunk):
        return 0 * pair + 1 if chunk == 1 else among(pair, (pairs - 1,))

    def stage_partner(stage, chunk, pair):
        second = is_second(pair, chunk)
        if stage < 3:
            usual = (across, flip(1)) if stage == 1 else (flip(1), across)
            usual = tuple(a + second * (b - a) for a, b in zip(*usual))
        else:
            usual = flip(2) if stage == 3 else flip(3) if stage == 4 else across
        swapped = (flip(2), flip(3), across, flip(1), across)[stage - 1]
        late = is_late(pair)
        return tuple(a + late * (b - a) for a, b in zip(usual, swapped))

    def stage_copy(stage, pair, chunk):
        source = sends[stage - 1].at[pair % 2, chunk]
        target = out.at[pair, chunk, plane] if stage == 5 else came[stage].at[pair, chunk]
        return remote(
            source,
            target,
            send_sem.at[stage - 1, pair % 2, chunk],
            recv_sem.at[stage - 1, pair, chunk],
            stage_partner(stage, chunk, pair),
        )

    def out_copy(pair, chunk):
        return pltpu.make_async_copy(
            sends[4].at[pair % 2, chunk], out.at[pair, chunk, plane], out_sem.at[pair % 2, chunk]
        )

    def has(pair, chunk):
        return pair < (pairs if chunk == 0 else full_pairs)

    width = out.shape[4]

    def start_inputs(q, slot):
        for number, source in enumerate(sources):

            @pl.when(q == number)
            def _():
                for place, target, k in ((source[0], left_in, 0), (source[1], right_in, 1)):
                    pltpu.make_async_copy(
                        factors[place[0]].at[:, pl.ds(place[1], width)],
                        target.at[slot],
                        in_sem.at[slot, k],
                    ).start()

    def wait_inputs(slot):
        for target, k in ((left_in, 0), (right_in, 1)):
            pltpu.make_async_copy(
                factors[0].at[:, pl.ds(0, width)], target.at[slot], in_sem.at[slot, k]
            ).wait()

    def products(pair):
        start_inputs(4 * pair, 0)
        for chunk in (0, 1):

            @pl.when((pair > 0) & has(pair - 1, chunk))
            def _():
                for side in (0, 1):
                    core_copy(pair - 1, chunk, side).wait_send()

        last = pair // full_pairs
        shrink = among(pair, shrink_pairs)

        def one(j, carry):
            slot = j % 2

            @pl.when(j + 1 < 4 - 2 * last)
            def _():
                start_inputs(4 * pair + j + 1, 1 - slot)

            wait_inputs(slot)
            product[...] = lax.dot_general(
                left_in[slot],
                right_in[slot],
                (((0,), (0,)), ((), ())),
                preferred_element_type=jnp.float32,
            )

            def store(i, carry):
                owner = shrink * (4 * j + i // 4) + (1 - shrink) * i
                quarter = shrink * (i % 4) + (1 - shrink) * j
                number = quarter // 2 * 2 + (quarter % 2 + plane) % 2
                first = pl.multiple_of(i * rows, 8)
                core_both[(owner + core) % 2, number, owner // 2] = product[
                    pl.ds(first, rows), :
                ].astype(jnp.bfloat16)
                return carry

            lax.fori_loop(0, 16, store, 0)
            return carry

        lax.fori_loop(0, 4 - 2 * last, one, 0)
        for chunk in (0, 1):

            @pl.when(has(pair, chunk))
            def _():
                for side in (0, 1):
                    core_copy(pair, chunk, side).start()

    def add(a, b):
        return (a.astype(jnp.float32) + b.astype(jnp.float32)).astype(jnp.bfloat16)

    def load(source, slot, blocks):
        return pltpu.make_async_copy(
            source, loaded.at[slot, pl.ds(0, blocks)], load_sem.at[slot]
        )

    def free_send(stage, pair, chunk):
        @pl.when(pair >= 2)
        def _():
            stage_copy(stage, pair, chunk).wait_send()

    def add_core(pair):
        slot = pair % 2
        x = bit_of(1)
        for chunk in (0, 1):

            @pl.when(has(pair, chunk))
            def _():
                for side in (1, 0):
                    core_copy(pair, chunk, side).wait_recv()
                    load(came[0].at[pair, 2 * chunk + side], side, 8).start()
                free_send(1, pair, chunk)
                for side in (1, 0):
                    number = 2 * chunk + side
                    load(came[0].at[pair, number], side, 8).wait()
                    late = is_late(pair)

                    def both():
                        target = sends[0] if side == 1 else keeps[0]

                        def one(block, carry):
                            target[slot, chunk, block] = add(
                                core_own[number, block], loaded[side, block]
                            )
                            return carry

                        lax.fori_loop(0, 8, one, 0)
                        if side == 1:
                            stage_copy(1, pair, chunk).start()

                    def split():
                        def one(i, carry):
                            usual = 2 * i
                            other = 4 * (i // 2) + i % 2
                            low = bit_of(2)
                            for target, a, b in (
                                (sends[0], usual + 1 - x, other + 2 * (1 - low)),
                                (keeps[0], usual + x, other + 2 * low),
                            ):
                                block = a + late * (b - a)
                                target[slot, chunk, 4 * side + i] = add(
                                    core_own[number, block], loaded[side, block]
                                )
                            return carry

                        lax.fori_loop(0, 4, one, 0)
                        if side == 0:
                            stage_copy(1, pair, chunk).start()

                    if chunk == 0:
                        apart = late + is_second(pair, chunk)
                        pl.when(apart == 0)(both)
                        pl.when(apart == 1)(split)
                    else:
                        split()

    def add_stage(stage, pair):
        slot = pair % 2
        blocks = 16 >> stage
        for chunk in (0, 1):

            @pl.when(has(pair, chunk))
            def _():
                stage_copy(stage, pair, chunk).wait_recv()
                load(came[stage].at[pair, chunk], chunk, blocks).start()
        for chunk in (0, 1):

            @pl.when(has(pair, chunk))
            def _():
                free_send(stage + 1, pair, chunk)
                if stage == 4:

                    @pl.when(pair >= 2)
                    def _():
                        out_copy(pair, chunk).wait()

                load(came[stage].at[pair, chunk], chunk, blocks).wait()
                old, new = keeps[stage - 1], keeps[stage] if stage < 4 else None

                def one(i, carry):
                    late = is_late(pair)
                    x, low, high = bit_of(1), bit_of(2), bit_of(3)
                    if stage == 1:
                        second = is_second(pair, chunk)
                        a = (
                            2 * i + 1 - x + second * (3 + x - i),
                            2 * i + x + second * (-x - i),
                        )
                        start = 4 * (i // 2) + i % 2
                        b = (start + 2 * (1 - high), start + 2 * high)
                    elif stage == 2:
                        a = (2 * i + 1 - low, 2 * i + low)
                        b = (2 + i, i)
                    else:
                        a = (1 - high, high)
                        b = (1 - x, x)
                    gone, kept = [p + late * (q - p) for p, q in zip(a, b)]
                    sends[stage][slot, chunk, i] = add(
                        old[slot, chunk, gone], loaded[chunk, gone]
                    )
                    new[slot, chunk, i] = add(old[slot, chunk, kept], loaded[chunk, kept])
                    return carry

                if stage < 4:
                    lax.fori_loop(0, blocks // 2, one, 0)
                else:
                    sends[4][slot, chunk] = add(old[slot, chunk, 0], loaded[chunk, 0])
                    out_copy(pair, chunk).start()
                stage_copy(stage + 1, pair, chunk).start()

    def small_copy(stage):
        return remote(
            small_sum.at[stage],
            small_came.at[stage],
            small_send.at[stage],
            small_recv.at[stage],
            partners[stage],
        )

    small_sum[0] = small[...]
    small_copy(0).start()

    def turn(time, carry):
        for stage in range(len(partners)):

            @pl.when(time == stage)
            def _():
                small_copy(stage).wait_recv()
                total = small_sum[stage] + small_came[stage]
                if stage + 1 < len(partners):
                    small_sum[stage + 1] = total
                    small_copy(stage + 1).start()
                else:
                    small_out[...] = total

        for lag, work in (
            (1, add_core),
            (2, functools.partial(add_stage, 1)),
            (3, functools.partial(add_stage, 2)),
            (4, functools.partial(add_stage, 3)),
            (5, functools.partial(add_stage, 4)),
            (0, products),
        ):
            pair = time - lag

            @pl.when((pair >= 0) & (pair < pairs))
            def _():
                work(pair)

        return carry

    lax.fori_loop(0, pairs + 5, turn, 0)
    for stage in range(len(partners)):
        small_copy(stage).wait_send()
    for chunk in (0, 1):
        mine = pairs if chunk == 0 else full_pairs
        if mine == pairs:
            for side in (0, 1):
                core_copy(mine - 1, chunk, side).wait_send()
        for pair in range(max(mine - 2, 0), mine):
            out_copy(pair, chunk).wait()
            for stage in range(1, 6):
                stage_copy(stage, pair, chunk).wait_send()
        for pair in range(mine):
            stage_copy(5, pair, chunk).wait_recv()


def scatter_products(
    factors, sources, small, pairs, full_pairs, shrink_pairs, rows, width, collective_id
):
    tokens = factors[0].shape[0]
    depth = 16 * rows
    low = jnp.bfloat16

    def blocks(*lead):
        return jax.ShapeDtypeStruct((*lead, rows, width), low)

    hbm = [
        blocks(pairs, 4, 8),
        blocks(pairs, 2, 8),
        blocks(pairs, 2, 4),
        blocks(pairs, 2, 2),
        blocks(pairs, 2, 1),
        blocks(pairs, 2, 2),
    ]
    any_space = pl.BlockSpec(memory_space=pl.ANY)

    def vmem(*lead):
        return pltpu.VMEM((*lead, rows, width), low)

    dma = pltpu.SemaphoreType.DMA
    whole = pl.BlockSpec(memory_space=pltpu.VMEM)
    *_, out, total = pl.pallas_call(
        functools.partial(
            scatter_kernel, pairs, full_pairs, shrink_pairs, (), sources, len(factors)
        ),
        out_shape=hbm + [jax.ShapeDtypeStruct(small.shape, small.dtype)],
        in_specs=[any_space] * len(factors) + [whole],
        out_specs=[any_space] * len(hbm) + [whole],
        scratch_shapes=[
            pltpu.VMEM((2, tokens, width), low),
            pltpu.VMEM((2, tokens, width), low),
            pltpu.VMEM((depth, width), jnp.float32),
            vmem(2, 4, 8),
            vmem(2, 8),
            vmem(2, 2, 8),
            vmem(2, 2, 4),
            vmem(2, 2, 2),
            vmem(2, 2, 1),
            vmem(2, 2),
            vmem(2, 2, 8),
            vmem(2, 2, 4),
            vmem(2, 2, 2),
            vmem(2, 2, 1),
            dma((2, 2)),
            dma((2,)),
            dma((2, 2)),
            dma((4,)),
            dma((pairs, 4)),
            dma((5, 2, 2)),
            dma((5, pairs, 2)),
            pltpu.VMEM((5, *small.shape), small.dtype),
            pltpu.VMEM((5, *small.shape), small.dtype),
            dma((5,)),
            dma((5,)),
        ],
        compiler_params=pltpu.CompilerParams(
            collective_id=collective_id, has_side_effects=True, vmem_limit_bytes=58 << 20
        ),
        cost_estimate=pl.CostEstimate(
            flops=2 * len(sources) * depth * tokens * width,
            bytes_accessed=16 * len(sources) * depth * width,
            transcendentals=0,
        ),
    )(*factors, small)
    return out, total


BESIDE = ((1, "shrink"), )


def token_rows(gradients):
    return gradients.reshape(-1, gradients.shape[-1])


def scatter_all(terms, small):
    size = lax.axis_size("sp")
    if size != 16 or lax.axis_size("seq") != 2:
        links = {}
        flags = [(False, False), (True, True), (False, False), (False, True)]
        blocks = [
            [scatter_grad(*pair, *flag, links) for pair, flag in zip(block, flags)]
            for block in terms[:2]
        ]
        last = [scatter_grad(*pair, False, False, links) for pair in terms[2]]
        return blocks[0], blocks[1], last, lax.psum(small, ("seq", "sp"))
    factors, sources = [], []

    def add_factors(pair):
        factors.extend(token_rows(member) for member in pair)
        return len(factors) - 2, len(factors) - 1

    names = ("expand", "shrink", "qkv", "out")
    results = [dict(), dict()]
    shrink_pairs, homes = [], []

    def beside(block, name):
        left, right = [token_rows(member) for member in terms[block][names.index(name)]]
        product = lax.dot_general(
            left, right, (((0,), (0,)), ((), ())), preferred_element_type=jnp.float32
        ).astype(jnp.bfloat16)
        return lax.psum_scatter(product, "sp", scatter_dimension=0, tiled=True)

    early = [beside(block, name) for block, name in BESIDE]
    for block in (1, 0):
        expand, shrink, qkv, out = terms[block]
        if (block, "shrink") not in BESIDE:
            shrink_pairs.append(len(homes))
            homes.append((block, "shrink"))
            left, right = add_factors(shrink)
            sources += [((left, j * D), (right, 0)) for j in range(4)]
        if (block, "expand") not in BESIDE:
            homes.append((block, "expand"))
            left, right = add_factors(expand)
            sources += [((left, 0), (right, j * D)) for j in range(4)]
        homes.append((block, "qkv"))
        left, right = add_factors(qkv)
        sources += [((left, 0), (right, j * D)) for j in range(3)]
        left, right = add_factors(out)
        sources.append(((left, 0), (right, 0)))
    for pair in terms[2]:
        left, right = add_factors(pair)
        sources.append(((left, 0), (right, 0)))
    pairs = len(homes) + 1
    if early:
        small, first = lax.optimization_barrier((small, early[0]))
        early[0] = first
    done, total = scatter_products(
        factors, sources, small, pairs, pairs - 1, tuple(shrink_pairs), D // size, D, 1
    )
    done = done.astype(jnp.float32)

    def quarter(pair, k):
        return done[pair, k // 2, k % 2]

    for pair, (block, name) in enumerate(homes):
        parts = [quarter(pair, k) for k in range(4)]
        if name == "qkv":
            results[block]["out"] = parts.pop()
        results[block][name] = jnp.concatenate(parts, axis=0 if name == "shrink" else 1)
    for (block, name), part in zip(BESIDE, early):
        results[block][name] = sum_seq(part)
    last = [quarter(pairs - 1, k) for k in range(2)]
    ordered = [[found[name] for name in names] for found in results]
    return ordered[0], ordered[1], last, total


def halve(members, bit_value, bit, links):
    parts = [split_blocks(member, bit_value) for member in members]
    sent = low_sum(*[part[0] for part in parts])
    return (low_sum(*[part[1] for part in parts]), swap_sp(sent, bit, links))


def sum_seq(values):
    mine = values.astype(jnp.bfloat16)
    return mine.astype(jnp.float32) + swap_seq(mine, {}).astype(jnp.float32)


def triple_bias(query_bias, value_bias):
    head_query = query_bias.reshape(HEADS, 1, HEAD_DIM)
    head_value = value_bias.reshape(HEADS, 1, HEAD_DIM)
    return jnp.concatenate([head_query, jnp.zeros_like(head_query), head_value], axis=1).reshape(
        3 * D
    )


def pair_bias(value_bias):
    head_value = value_bias.reshape(HEADS, 1, HEAD_DIM)
    return jnp.concatenate([jnp.zeros_like(head_value), head_value], axis=1).reshape(2 * D)


def triple_bias_grad(totals):
    split_rows = totals.reshape(HEADS, 3, HEAD_DIM)
    return (split_rows[:, 0].reshape(D), split_rows[:, 2].reshape(D))


def frame_modulation(segment_ids, timesteps):
    onehot = (segment_ids[:, :, None] == jnp.arange(CLIPS)[None, None, :]).astype(jnp.float32)
    features = time_features(timesteps)
    return jnp.einsum("sfc,scz->sfz", onehot, features, precision=lax.Precision.HIGHEST)


def block_pieces(table_rows, frame_mod):
    modulation = table_rows[None, None] + frame_mod
    return [modulation[:, :, number][:, :, None, :] for number in range(6)]


def gated_back(grad_out, gating, branch):
    branch_grad = (gating * grad_out).astype(jnp.bfloat16)
    gate_grad = jnp.sum(grad_out * branch, axis=2, keepdims=True)
    return (branch_grad, gate_grad)


def to_pairs(values):
    groups, frames, patches, head_count, columns = values.shape
    reordered = jnp.transpose(values, (0, 1, 3, 2, 4))
    return reordered.reshape(lax.axis_size("sp"), -1, patches, columns)


def from_pairs(values, groups, frames):
    devices, pair_count, patches, columns = values.shape
    reordered = values.reshape(groups, frames, -1, patches, columns)
    return jnp.transpose(reordered, (0, 1, 3, 2, 4))


def pair_scores(triple):
    queries = triple[..., :HEAD_DIM]
    key_rows = triple[..., HEAD_DIM : 2 * HEAD_DIM]
    scores = jnp.einsum(
        "zkqe,zkre->zkqr", queries, key_rows, preferred_element_type=jnp.float32
    ) * HEAD_DIM ** (-0.5)
    return jax.nn.softmax(scores, axis=-1)


def attend_pairs(triple):
    attention = pair_scores(triple).astype(jnp.bfloat16)
    mixture = jnp.einsum(
        "zkqr,zkre->zkqe",
        attention,
        triple[..., 2 * HEAD_DIM :],
        preferred_element_type=jnp.float32,
    ).astype(jnp.bfloat16)
    return lax.all_to_all(mixture, "sp", split_axis=2, concat_axis=0, tiled=True)


def pair_backward(members):
    triple, out_grad = members
    queries = triple[..., :HEAD_DIM]
    key_rows = triple[..., HEAD_DIM : 2 * HEAD_DIM]
    value_rows = triple[..., 2 * HEAD_DIM :]
    attention = pair_scores(triple)
    rounded = attention.astype(jnp.bfloat16)
    prob_grad = jnp.einsum(
        "zkqe,zkre->zkqr", out_grad, value_rows, preferred_element_type=jnp.float32
    )
    centre = jnp.sum(prob_grad * attention, axis=-1, keepdims=True)
    score_grad = (attention * (prob_grad - centre)).astype(jnp.bfloat16)
    scaling = HEAD_DIM ** (-0.5)
    query_grad = (
        jnp.einsum("zkqr,zkre->zkqe", score_grad, key_rows, preferred_element_type=jnp.float32)
        * scaling
    )
    key_grad = (
        jnp.einsum("zkqr,zkqe->zkre", score_grad, queries, preferred_element_type=jnp.float32)
        * scaling
    )
    value_grad = jnp.einsum(
        "zkqr,zkqe->zkre", rounded, out_grad, preferred_element_type=jnp.float32
    )
    gradients = jnp.concatenate([query_grad, key_grad, value_grad], axis=-1).astype(jnp.bfloat16)
    return lax.all_to_all(gradients, "sp", split_axis=2, concat_axis=0, tiled=True)


def pair_attention(triple):
    groups, frames, patches = triple.shape[:3]
    shaped = triple.reshape(groups, frames, patches, HEADS, 3 * HEAD_DIM)
    pairs = lax.all_to_all(to_pairs(shaped), "sp", split_axis=0, concat_axis=2, tiled=True)
    exchanged = attend_pairs(pairs)
    return from_pairs(exchanged, groups, frames).reshape(groups, frames, patches, D), pairs


def pair_attention_back(pairs, mixture_grad):
    groups, frames, patches = mixture_grad.shape[:3]
    grad_shaped = mixture_grad.reshape(groups, frames, patches, HEADS, HEAD_DIM)
    returned = pair_backward(
        (
            pairs,
            lax.all_to_all(to_pairs(grad_shaped), "sp", split_axis=0, concat_axis=2, tiled=True),
        )
    )
    return from_pairs(returned, groups, frames).reshape(groups, frames, patches, 3 * D)


def feed_forward(residual, offset, scaling, gating, expand, shrink, vectors, start_row):
    hidden = modulate(residual, offset, scaling).astype(jnp.bfloat16)
    inner_sum = project(hidden, expand) + vectors[start_row : start_row + 4].reshape(FF)
    active = gelu_tanh(inner_sum).astype(jnp.bfloat16)
    branch = project(active, shrink) + vectors[3]
    return ((hidden, inner_sum, active, branch), residual + gating * branch)


def feed_backward(grad_out, residual, offset, scaling, gating, stored, expand, shrink):
    hidden, inner_sum, active, branch = stored
    branch_grad, gate_grad = gated_back(grad_out, gating, branch)
    shrink_grad = (active, branch_grad)
    active_grad = input_grad(branch_grad, shrink)
    gelu_value, gelu_back = jax.vjp(gelu_tanh, inner_sum)
    inner_grad = gelu_back(active_grad)[0].astype(jnp.bfloat16)
    expand_grad = (hidden, inner_grad)
    hidden_grad = input_grad(inner_grad, expand)
    norm_value, norm_back = jax.vjp(modulate, residual, offset, scaling)
    residual_grad, offset_grad, scaling_grad = norm_back(hidden_grad)
    return (
        grad_out + residual_grad,
        [offset_grad, scaling_grad, gate_grad],
        (expand_grad, shrink_grad, column_sum(inner_grad), column_sum(branch_grad)),
    )


def table_sums(members):
    return jnp.stack([jnp.sum(member, axis=(0, 1, 2)) for member in members])


def spatial_forward(residual, weights, frame_mod):
    qkv_weight, out_weight, expand, shrink, vectors = weights
    vectors_f = as_float(vectors)
    pieces = block_pieces(vectors_f[4:10], frame_mod)
    hidden = modulate(residual, pieces[0], pieces[1]).astype(jnp.bfloat16)
    triple = (project(hidden, qkv_weight) + triple_bias(vectors_f[0], vectors_f[1])).astype(
        jnp.bfloat16
    )
    mixture, pairs = pair_attention(triple)
    branch = project(mixture, out_weight) + vectors_f[2]
    middle = residual + pieces[2] * branch
    stored_ffn, result = feed_forward(
        middle, pieces[3], pieces[4], pieces[5], expand, shrink, vectors_f, 10
    )
    return (result, (hidden, pairs, mixture, branch, middle, stored_ffn))


def spatial_backward(grad_out, residual, weights, frame_mod, stored):
    qkv_weight, out_weight, expand, shrink, vectors = weights
    pieces = block_pieces(as_float(vectors)[4:10], frame_mod)
    hidden, pairs, mixture, branch, middle, stored_ffn = stored
    middle_grad, ffn_table, ffn_grads = feed_backward(
        grad_out, middle, pieces[3], pieces[4], pieces[5], stored_ffn, expand, shrink
    )
    branch_grad, gate_grad = gated_back(middle_grad, pieces[2], branch)
    out_weight_grad = (mixture, branch_grad)
    out_bias = column_sum(branch_grad)
    mixture_grad = input_grad(branch_grad, out_weight).astype(jnp.bfloat16)
    triple_grad = pair_attention_back(pairs, mixture_grad)
    qkv_grad = (hidden, triple_grad)
    query_bias, value_bias = triple_bias_grad(column_sum(triple_grad))
    hidden_grad = input_grad(triple_grad, qkv_weight)
    norm_value, norm_back = jax.vjp(modulate, residual, pieces[0], pieces[1])
    residual_grad, offset_grad, scaling_grad = norm_back(hidden_grad)
    table_grad = table_sums([offset_grad, scaling_grad, gate_grad] + ffn_table)
    vector_grad = jnp.concatenate(
        [
            jnp.stack([query_bias, value_bias, out_bias, ffn_grads[3]]),
            table_grad,
            ffn_grads[2].reshape(4, D),
        ],
        axis=0,
    )
    return (
        middle_grad + residual_grad,
        (qkv_grad, out_weight_grad, ffn_grads[0], ffn_grads[1], vector_grad),
    )


def temporal_scores(triple, same_clip):
    scores = jnp.einsum(
        "sfphe,sgphe->sphfg",
        triple[..., :HEAD_DIM],
        triple[..., HEAD_DIM : 2 * HEAD_DIM],
        preferred_element_type=jnp.float32,
    ) * HEAD_DIM ** (-0.5)
    return jax.nn.softmax(jnp.where(same_clip, scores, masked_score), axis=-1)


def caption_scores(queries, keyval, allowed):
    scores = jnp.einsum(
        "sfphe,srhe->sfphr", queries, keyval[..., :HEAD_DIM], preferred_element_type=jnp.float32
    ) * HEAD_DIM ** (-0.5)
    return jax.nn.softmax(jnp.where(allowed, scores, masked_score), axis=-1)


def temporal_forward(residual, weights, frame_mod, same_clip, allowed, context):
    qkv_weight, out_weight, expand, shrink, query_weight, keyval_weight, cross_weight, vectors = (
        weights
    )
    vectors_f = as_float(vectors)
    pieces = block_pieces(vectors_f[8:14], frame_mod)
    groups, frames, patches = residual.shape[:3]
    hidden = modulate(residual, pieces[0], pieces[1]).astype(jnp.bfloat16)
    triple = (project(hidden, qkv_weight) + triple_bias(vectors_f[0], vectors_f[1])).astype(
        jnp.bfloat16
    )
    triple = triple.reshape(groups, frames, patches, HEADS, 3 * HEAD_DIM)
    attention = temporal_scores(triple, same_clip).astype(jnp.bfloat16)
    mixture = (
        jnp.einsum(
            "sphfg,sgphe->sfphe",
            attention,
            triple[..., 2 * HEAD_DIM :],
            preferred_element_type=jnp.float32,
        )
        .astype(jnp.bfloat16)
        .reshape(groups, frames, patches, D)
    )
    branch = project(mixture, out_weight) + vectors_f[2]
    middle = residual + pieces[2] * branch
    lowered = middle.astype(jnp.bfloat16)
    queries = (project(lowered, query_weight) + vectors_f[4]).astype(jnp.bfloat16)
    queries = queries.reshape(groups, frames, patches, HEADS, HEAD_DIM)
    keyval = (project(context, keyval_weight) + pair_bias(vectors_f[5])).astype(jnp.bfloat16)
    keyval = keyval.reshape(groups, -1, HEADS, 2 * HEAD_DIM)
    cross_probs = caption_scores(queries, keyval, allowed).astype(jnp.bfloat16)
    cross_mix = (
        jnp.einsum(
            "sfphr,srhe->sfphe",
            cross_probs,
            keyval[..., HEAD_DIM:],
            preferred_element_type=jnp.float32,
        )
        .astype(jnp.bfloat16)
        .reshape(groups, frames, patches, D)
    )
    crossed = middle + project(cross_mix, cross_weight) + vectors_f[6]
    stored_ffn, result = feed_forward(
        crossed, pieces[3], pieces[4], pieces[5], expand, shrink, vectors_f, 14
    )
    return (
        result,
        (
            hidden,
            triple,
            mixture,
            branch,
            middle,
            lowered,
            queries,
            keyval,
            cross_mix,
            crossed,
            stored_ffn,
        ),
    )


def temporal_backward(grad_out, residual, weights, frame_mod, same_clip, allowed, stored):
    qkv_weight, out_weight, expand, shrink, query_weight, keyval_weight, cross_weight, vectors = (
        weights
    )
    pieces = block_pieces(as_float(vectors)[8:14], frame_mod)
    (
        hidden,
        triple,
        mixture,
        branch,
        middle,
        lowered,
        queries,
        keyval,
        cross_mix,
        crossed,
        stored_ffn,
    ) = stored
    groups, frames, patches = residual.shape[:3]
    scaling = HEAD_DIM ** (-0.5)
    crossed_grad, ffn_table, ffn_grads = feed_backward(
        grad_out, crossed, pieces[3], pieces[4], pieces[5], stored_ffn, expand, shrink
    )
    cross_branch_grad = crossed_grad.astype(jnp.bfloat16)
    cross_weight_grad = (cross_mix, cross_branch_grad)
    cross_bias = column_sum(cross_branch_grad)
    mix_grad = input_grad(cross_branch_grad, cross_weight).astype(jnp.bfloat16)
    mix_grad = mix_grad.reshape(groups, frames, patches, HEADS, HEAD_DIM)
    cross_probs = caption_scores(queries, keyval, allowed)
    rounded = cross_probs.astype(jnp.bfloat16)
    prob_grad = jnp.einsum(
        "sfphe,srhe->sfphr", mix_grad, keyval[..., HEAD_DIM:], preferred_element_type=jnp.float32
    )
    centre = jnp.sum(prob_grad * cross_probs, axis=-1, keepdims=True)
    score_grad = (cross_probs * (prob_grad - centre)).astype(jnp.bfloat16)
    query_grad = (
        jnp.einsum(
            "sfphr,srhe->sfphe",
            score_grad,
            keyval[..., :HEAD_DIM],
            preferred_element_type=jnp.float32,
        )
        * scaling
    )
    query_grad = query_grad.astype(jnp.bfloat16).reshape(groups, frames, patches, D)
    key_grad = (
        jnp.einsum("sfphr,sfphe->srhe", score_grad, queries, preferred_element_type=jnp.float32)
        * scaling
    )
    value_grad = jnp.einsum(
        "sfphr,sfphe->srhe", rounded, mix_grad, preferred_element_type=jnp.float32
    )
    keyval_grad = jnp.concatenate([key_grad, value_grad], axis=-1).reshape(groups, -1, 2 * D)
    keyval_grad = lax.psum(keyval_grad.astype(jnp.bfloat16), "sp")
    query_weight_grad = (lowered, query_grad)
    cross_query_bias = column_sum(query_grad)
    middle_grad = crossed_grad + input_grad(query_grad, query_weight)
    branch_grad, gate_grad = gated_back(middle_grad, pieces[2], branch)
    out_weight_grad = (mixture, branch_grad)
    out_bias = column_sum(branch_grad)
    mixture_grad = input_grad(branch_grad, out_weight).astype(jnp.bfloat16)
    mixture_grad = mixture_grad.reshape(groups, frames, patches, HEADS, HEAD_DIM)
    attention = temporal_scores(triple, same_clip)
    rounded_t = attention.astype(jnp.bfloat16)
    prob_grad_t = jnp.einsum(
        "sfphe,sgphe->sphfg",
        mixture_grad,
        triple[..., 2 * HEAD_DIM :],
        preferred_element_type=jnp.float32,
    )
    centre_t = jnp.sum(prob_grad_t * attention, axis=-1, keepdims=True)
    score_grad_t = (attention * (prob_grad_t - centre_t)).astype(jnp.bfloat16)
    query_part = (
        jnp.einsum(
            "sphfg,sgphe->sfphe",
            score_grad_t,
            triple[..., HEAD_DIM : 2 * HEAD_DIM],
            preferred_element_type=jnp.float32,
        )
        * scaling
    )
    key_part = (
        jnp.einsum(
            "sphfg,sfphe->sgphe",
            score_grad_t,
            triple[..., :HEAD_DIM],
            preferred_element_type=jnp.float32,
        )
        * scaling
    )
    value_part = jnp.einsum(
        "sphfg,sfphe->sgphe", rounded_t, mixture_grad, preferred_element_type=jnp.float32
    )
    triple_grad = jnp.concatenate([query_part, key_part, value_part], axis=-1).astype(jnp.bfloat16)
    triple_grad = triple_grad.reshape(groups, frames, patches, 3 * D)
    qkv_grad = (hidden, triple_grad)
    query_bias, value_bias = triple_bias_grad(column_sum(triple_grad))
    hidden_grad = input_grad(triple_grad, qkv_weight)
    norm_value, norm_back = jax.vjp(modulate, residual, pieces[0], pieces[1])
    residual_grad, offset_grad, scaling_grad = norm_back(hidden_grad)
    table_grad = table_sums([offset_grad, scaling_grad, gate_grad] + ffn_table)
    zero_row = jnp.zeros((D,), jnp.float32)
    vector_grad = jnp.concatenate(
        [
            jnp.stack(
                [
                    query_bias,
                    value_bias,
                    out_bias,
                    ffn_grads[3],
                    cross_query_bias,
                    zero_row,
                    cross_bias,
                    zero_row,
                ]
            ),
            table_grad,
            ffn_grads[2].reshape(4, D),
        ],
        axis=0,
    )
    terms = (
        qkv_grad,
        out_weight_grad,
        ffn_grads[0],
        ffn_grads[1],
        query_weight_grad,
        cross_weight_grad,
        vector_grad,
    )
    return (middle_grad + residual_grad, terms, keyval_grad)


def on_device(
    video,
    segment_ids,
    timesteps,
    drop_mask,
    captions,
    null_caption,
    caption_weight,
    spatial_qkv,
    spatial_out,
    spatial_expand,
    spatial_shrink,
    spatial_vectors,
    temporal_qkv,
    temporal_out,
    temporal_expand,
    temporal_shrink,
    cross_query,
    cross_keyval,
    cross_out,
    temporal_vectors,
    cotangent,
):
    groups, frames, patches = video.shape[:3]
    size = lax.axis_size("sp")
    third = D
    wide = [
        spatial_qkv,
        spatial_out,
        spatial_expand,
        temporal_qkv,
        temporal_out,
        cross_query,
        cross_keyval,
        cross_out,
    ]

    def rounds_of(rows):
        cut = 512

        def block_round(qkv, out, start, width):
            return columns_round(
                (qkv, start, width),
                (qkv, third + start, width),
                (qkv, 2 * third + start, width),
                (out, start, width),
            )

        def expand_round(weight, late=False):
            quarter = FF // 4
            return columns_round(*[(weight, k * quarter, quarter) for k in range(4)], late=late)

        return [
            block_round(0, 1, 0, cut),
            block_round(0, 1, cut, third - cut),
            expand_round(2),
            rows_round(8, rows),
            columns_round((5, 0, third), (6, 0, third), (6, third, third), (7, 0, third)),
            block_round(3, 4, 0, cut),
            block_round(3, 4, cut, third - cut),
        ]

    (
        full_sqkv,
        full_sout,
        full_sexp,
        full_tqkv,
        full_tout,
        full_cq,
        full_ckv,
        full_cout,
        full_sshr,
        all_vectors,
    ) = gather_all(
        [spatial_shrink],
        wide,
        jnp.concatenate([spatial_vectors, temporal_vectors], axis=0),
        rounds_of,
        0,
    )
    full_sqkv, expand_shard, shrink_shard = lax.optimization_barrier(
        (full_sqkv, temporal_expand, temporal_shrink)
    )
    full_texp = lax.all_gather(expand_shard, "sp", axis=0, tiled=True)
    full_tshr = lax.all_gather(shrink_shard, "sp", axis=0, tiled=True)
    n_spatial = spatial_vectors.shape[0]
    spatial = (full_sqkv, full_sout, full_sexp, full_sshr, all_vectors[:n_spatial])
    temporal = (
        full_tqkv,
        full_tout,
        full_texp,
        full_tshr,
        full_cq,
        full_ckv,
        full_cout,
        all_vectors[n_spatial:],
    )
    dropped = (drop_mask > 0).astype(jnp.float32)
    text_local = jnp.where(drop_mask[:, :, None, None] > 0, null_caption[None, None], captions)
    text_rows = text_local.reshape(groups, CLIPS * CAP, -1)
    caption_sum = lax.psum(project(text_rows, caption_weight).astype(jnp.float32), "sp")
    caption_sum, first = lax.optimization_barrier((caption_sum, spatial[0]))
    spatial = (first, *spatial[1:])
    frame_mod = frame_modulation(segment_ids, timesteps).reshape(groups, frames, 6, D)
    same_clip = (segment_ids[:, :, None] == segment_ids[:, None, :])[:, None, None]
    row_clip = jnp.arange(CLIPS * CAP) // CAP
    allowed = (segment_ids[:, :, None] == row_clip[None, None, :])[:, :, None, None, :]
    residual = video.astype(jnp.float32)
    middle, spatial_kept = spatial_forward(residual, spatial, frame_mod)
    context = (caption_sum + as_float(temporal[7])[7]).astype(jnp.bfloat16)
    result, temporal_kept = temporal_forward(
        middle, temporal, frame_mod, same_clip, allowed, context
    )
    output = result.astype(jnp.bfloat16)
    middle_grad, temporal_terms, keyval_grad = temporal_backward(
        cotangent.astype(jnp.float32),
        middle,
        temporal,
        frame_mod,
        same_clip,
        allowed,
        temporal_kept,
    )
    shard_rows = D // lax.axis_size("sp")
    first_row = lax.axis_index("sp") * shard_rows
    video_grad, spatial_terms = spatial_backward(
        middle_grad, residual, spatial, frame_mod, spatial_kept
    )
    spatial_sums, temporal_sums, cross_sums, vector_total = scatter_all(
        (
            (spatial_terms[2], spatial_terms[3], spatial_terms[0], spatial_terms[1]),
            (temporal_terms[2], temporal_terms[3], temporal_terms[0], temporal_terms[1]),
            (temporal_terms[4], temporal_terms[5]),
        ),
        jnp.concatenate([spatial_terms[4], temporal_terms[6]], axis=0),
    )
    vector_total = lax.dynamic_slice_in_dim(vector_total, first_row, shard_rows, 1)
    keyval_grad, vector_total = lax.optimization_barrier((keyval_grad, vector_total))
    context_grad = input_grad(keyval_grad, temporal[5]).astype(jnp.bfloat16)
    local_context = lax.dynamic_slice_in_dim(context, first_row, shard_rows, 2)
    keyval_weight_grad = weight_grad(local_context, keyval_grad)
    value_bias_full = column_sum(keyval_grad).reshape(HEADS, 2, HEAD_DIM)[:, 1].reshape(D)
    caption_bias_full = column_sum(context_grad)
    caption_weight_grad = weight_grad(text_rows, context_grad)
    text_grad = input_grad(context_grad, caption_weight).reshape(groups, CLIPS, CAP, -1)
    null_grad = jnp.sum(text_grad * dropped[:, :, None, None], axis=(0, 1))
    own_rows = [
        lax.dynamic_slice_in_dim(row, first_row, shard_rows, 0)
        for row in (value_bias_full, caption_bias_full)
    ]
    width = null_grad.shape[1]
    flat = jnp.stack([jnp.pad(row, (0, width - shard_rows)) for row in own_rows])
    small_total = sum_seq(jnp.concatenate([null_grad, flat], axis=0))
    null_total = small_total[: null_grad.shape[0]]
    bias_total = small_total[null_grad.shape[0] :, :shard_rows]
    vector_total = vector_total.at[n_spatial + 5].add(bias_total[0])
    vector_total = vector_total.at[n_spatial + 7].add(bias_total[1])
    return (
        output,
        video_grad.astype(jnp.bfloat16),
        null_total,
        sum_seq(caption_weight_grad),
        spatial_sums[2],
        spatial_sums[3],
        spatial_sums[0],
        spatial_sums[1],
        vector_total[:n_spatial],
        temporal_sums[2],
        temporal_sums[3],
        temporal_sums[0],
        temporal_sums[1],
        cross_sums[0],
        sum_seq(keyval_weight_grad),
        cross_sums[1],
        vector_total[n_spatial:],
    )


def solution(mesh):
    return jax.shard_map(
        on_device,
        mesh=mesh,
        in_specs=(
            P("seq", None, "sp", None),
            P("seq", None),
            P("seq", None),
            P("seq", None),
            P("seq", None, None, "sp"),
            P(None, "sp"),
            P("sp", None),
            P("sp", None),
            P("sp", None),
            P("sp", None),
            P("sp", None),
            P(None, "sp"),
            P("sp", None),
            P("sp", None),
            P("sp", None),
            P("sp", None),
            P("sp", None),
            P("sp", None),
            P("sp", None),
            P(None, "sp"),
            P("seq", None, "sp", None),
        ),
        out_specs=(
            P("seq", None, "sp", None),
            P("seq", None, "sp", None),
            P(None, "sp"),
            P("sp", None),
            P("sp", None),
            P("sp", None),
            P("sp", None),
            P("sp", None),
            P(None, "sp"),
            P("sp", None),
            P("sp", None),
            P("sp", None),
            P("sp", None),
            P("sp", None),
            P("sp", None),
            P("sp", None),
            P(None, "sp"),
        ),
        check_vma=False,
    )
```

```python
import functools
import math

import jax
import jax.numpy as jnp
from jax import lax
from jax.experimental import pallas as pl
from jax.experimental.pallas import tpu as pltpu
from jax.sharding import PartitionSpec as P

D = 1152
HEADS = 16
HEAD_DIM = 72
FF = 4608
CAP = 120
CLIPS = 2


norm_eps = 1e-06
masked_score = -1e30


def time_features(timestep):
    half_width = 3 * D
    frequency = jnp.exp(
        jnp.arange(half_width, dtype=jnp.float32) * (-math.log(10000.0) / half_width)
    )
    angles = timestep.astype(jnp.float32)[..., None] * frequency
    return 0.5 * jnp.concatenate([jnp.cos(angles), jnp.sin(angles)], axis=-1)


def layer_norm(residual):
    center = residual - jnp.mean(residual, axis=-1, keepdims=True)
    return center * lax.rsqrt(jnp.mean(center * center, axis=-1, keepdims=True) + norm_eps)


def modulate(residual, offset, scaling):
    return layer_norm(residual) * (1.0 + scaling) + offset


def gelu_tanh(inner_sum):
    return jax.nn.gelu(inner_sum, approximate=True)


def as_float(member):
    return member.astype(jnp.float32)


def project(inputs, weight):
    return jnp.dot(inputs, weight, preferred_element_type=jnp.float32)


def weight_grad(inputs, gradients):
    left_rows = inputs.reshape(-1, inputs.shape[-1])
    right_rows = gradients.reshape(-1, gradients.shape[-1])
    return lax.dot_general(
        left_rows, right_rows, (((0,), (0,)), ((), ())), preferred_element_type=jnp.float32
    )


def input_grad(gradients, weight):
    return lax.dot_general(
        gradients,
        weight,
        (((gradients.ndim - 1,), (1,)), ((), ())),
        preferred_element_type=jnp.float32,
    )


def column_sum(gradients):
    return jnp.sum(gradients.astype(jnp.float32).reshape(-1, gradients.shape[-1]), axis=0)


def index_bits():
    return lax.axis_size("sp").bit_length() - 1


def after(values, earlier):
    if not earlier:
        return values
    return lax.optimization_barrier((values, tuple(earlier)))[0]


def in_turn(links, key, values, exchange):
    last = links.get(key)
    result = exchange(values if last is None else after(values, [last]))
    links[key] = result
    return result


def swap_sp(values, bit, links):
    size = lax.axis_size("sp")
    pairs = [(i, i ^ (1 << bit)) for i in range(size)]
    return in_turn(links, min(bit, 2), values, lambda v: lax.ppermute(v, "sp", pairs))


def swap_seq(values, links, key="seq"):
    return in_turn(links, key, values, lambda v: lax.ppermute(v, "seq", [(0, 1), (1, 0)]))


def gather_kernel(rounds, n_in, n_out, *refs):
    shards, outs = refs[:n_in], refs[n_in : n_in + n_out]
    local_sem, send_sem, recv_sem, small_local, small_send, small_recv = refs[n_in + n_out :]
    me = lax.axis_index("sp")
    plane = lax.axis_index("seq")
    count = index_bits()
    place = [(me // (1 << (count - 1 - d))) % 2 for d in range(count)]

    def flip(bit):
        mine = (me // (1 << bit)) % 2
        return (plane, me + (1 << bit) * (1 - 2 * mine))

    across = (1 - plane, me)
    partners = [flip(bit) for bit in range(count)] + [across]
    barrier = pltpu.get_barrier_semaphore()
    for partner in partners:
        pl.semaphore_signal(
            barrier, inc=1, device_id=partner, device_id_type=pl.DeviceIdType.MESH
        )
    pl.semaphore_wait(barrier, len(partners))

    def part(ref, lead, piece):
        weight, rows, columns = piece
        if rows is None:
            return ref.at[(*lead, slice(None), pl.ds(*columns))]
        half, first, size = rows
        return ref.at[(*lead, half, pl.ds(first, size), slice(None))]

    def stage_places(stage):
        return tuple(
            slice(None) if d < stage else place[d] for d in range(count)
        )

    for own_half in (0, 1):

        @pl.when(plane == own_half)
        def _():
            started = []

            def send(number, stage, slot, source, target, partner):
                copy = pltpu.make_async_remote_copy(
                    src_ref=source,
                    dst_ref=target,
                    send_sem=send_sem.at[number, stage, slot],
                    recv_sem=recv_sem.at[number, stage, slot],
                    device_id=partner,
                    device_id_type=pl.DeviceIdType.MESH,
                )
                copy.start()
                return copy

            def own(chunk):
                return chunk[own_half]

            def other(chunk):
                return chunk[1 - own_half]

            def step(number, stage):
                (first, second), late = rounds[number]
                lead = stage_places(min(stage, count - 2))
                four = [piece for chunk in (first, second) for piece in (own(chunk), other(chunk))]
                if late and stage < count:
                    partner = [flip(1), across, *[flip(bit) for bit in range(count - 1, 1, -1)]][stage]
                    moves = [(piece, partner) for piece in (four if stage > 1 else four[::2])]
                    lead = tuple(
                        slice(None) if d < stage - 2 or (d == count - 2 and stage) else place[d]
                        for d in range(count)
                    )
                elif stage < count - 2:
                    moves = [(own(first), flip(count - 1 - stage)), (own(second), flip(count - 1 - stage))]
                elif stage == count - 2:
                    moves = [(own(first), flip(1)), (own(second), across)]
                elif stage == count - 1:
                    moves = [
                        (own(first), across),
                        (own(second), flip(1)),
                        (other(second), flip(1)),
                    ]
                else:
                    moves = [(piece, flip(0)) for piece in four]
                copies = []
                for slot, (piece, partner) in enumerate(moves):
                    places = lead
                    if not late and stage == count - 1 and partner is across or stage == count:
                        places = stage_places(count - 1)
                    target = part(outs[piece[0]], places, piece)
                    source = target
                    if stage == 0:
                        source = part(shards[piece[0]], (), piece)
                    copies.append(send(number, stage, slot, source, target, partner))
                return copies

            def small_step(stage):
                target = outs[-1].at[stage_places(stage)]
                copy = pltpu.make_async_remote_copy(
                    src_ref=target if stage else shards[-1],
                    dst_ref=target,
                    send_sem=small_send.at[stage],
                    recv_sem=small_recv.at[stage],
                    device_id=flip(count - 1 - stage),
                    device_id_type=pl.DeviceIdType.MESH,
                )
                copy.start()
                return copy

            copies = {}
            small = [small_step(0)]
            local = [
                pltpu.make_async_copy(shards[-1], outs[-1].at[stage_places(0)], small_local)
            ]
            local[0].start()
            for number, (pair, late) in enumerate(rounds):
                for slot, chunk in enumerate(pair):
                    piece = own(chunk)
                    copy = pltpu.make_async_copy(
                        part(shards[piece[0]], (), piece),
                        part(outs[piece[0]], stage_places(0), piece),
                        local_sem.at[number, slot],
                    )
                    copy.start()
                    local.append(copy)
            lags = {
                False: [*range(count), count + 1],
                True: [*range(count - 1), count, count + 2],
            }
            for time in range(len(rounds) + count + 2):
                if time == 1:
                    for copy in local:
                        copy.wait()
                if 0 < time < count:
                    small[-1].wait_recv()
                    small.append(small_step(time))
                for stage in range(count + 1):
                    for number, (_, late) in enumerate(rounds):
                        if number != time - lags[late][stage]:
                            continue
                        if stage:
                            for copy in copies[number, stage - 1]:
                                copy.wait_recv()
                        copies[number, stage] = step(number, stage)
            small[-1].wait_recv()
            for copy in small:
                copy.wait_send()
            for number in range(len(rounds)):
                for copy in copies[number, count]:
                    copy.wait_recv()
                for stage in range(count + 1):
                    for copy in copies[number, stage]:
                        copy.wait_send()


def gather_weights(shards, rounds, collective_id):
    size = lax.axis_size("sp")
    lead = (2,) * index_bits()
    shapes = [lead + shard.shape for shard in shards]
    total = sum(2 * math.prod(shape) for shape in shapes)
    stages = index_bits() + 1
    placed = pl.pallas_call(
        functools.partial(gather_kernel, rounds, len(shards), len(shards)),
        out_shape=[jax.ShapeDtypeStruct(shape, jnp.bfloat16) for shape in shapes],
        in_specs=[pl.BlockSpec(memory_space=pltpu.VMEM)] * len(shards),
        out_specs=[pl.BlockSpec(memory_space=pl.ANY)] * len(shards),
        scratch_shapes=[
            pltpu.SemaphoreType.DMA((len(rounds), 2)),
            pltpu.SemaphoreType.DMA((len(rounds), stages, 4)),
            pltpu.SemaphoreType.DMA((len(rounds), stages, 4)),
            pltpu.SemaphoreType.DMA,
            pltpu.SemaphoreType.DMA((index_bits(),)),
            pltpu.SemaphoreType.DMA((index_bits(),)),
        ],
        compiler_params=pltpu.CompilerParams(
            collective_id=collective_id, has_side_effects=True, vmem_limit_bytes=32 << 20
        ),
        cost_estimate=pl.CostEstimate(flops=0, bytes_accessed=total, transcendentals=0),
    )(*shards)
    *large, small = placed
    full = [member.reshape(size * math.prod(member.shape[index_bits() : -1]), -1) for member in large]
    small = jnp.swapaxes(small.reshape(size, *small.shape[-2:]), 0, 1)
    return full + [small.reshape(small.shape[0], -1)]


def columns_round(*quarters, late=False):
    pieces = [(weight, None, (first, width)) for weight, first, width in quarters]
    return ((pieces[0], pieces[2]), (pieces[1], pieces[3])), late


def rows_round(weight, rows):
    cut = rows // 32 * 16 + (rows // 16 % 2) * 16
    return (
        ((weight, (0, 0, cut), None), (weight, (1, 0, cut), None)),
        ((weight, (0, cut, rows - cut), None), (weight, (1, cut, rows - cut), None)),
    ), False


def gather_all(tall, wide, small, rounds_of, collective_id):
    if wide[0].shape[0] % 8 or lax.axis_size("seq") != 2:
        full = [lax.all_gather(shard, "sp", axis=0, tiled=True) for shard in wide + tall]
        return full + [lax.all_gather(small, "sp", axis=1, tiled=True)]
    shards = list(wide) + [
        shard.reshape(2, shard.shape[0] // 2, shard.shape[1]) for shard in tall
    ]
    shards.append(small)
    return gather_weights(shards, rounds_of(tall[0].shape[0] // 2), collective_id)


def pick_half(first, second):
    return jnp.where(lax.axis_index("seq") == 0, first, second)


def low_sum(*members):
    total = members[0].astype(jnp.float32)
    for member in members[1:]:
        total = total + member.astype(jnp.float32)
    return total.astype(jnp.bfloat16)


def pick(values, index, axis):
    return lax.dynamic_index_in_dim(values, index, axis, keepdims=False)


def split_blocks(values, bit_value):
    paired = values.reshape(values.shape[0] // 2, 2, *values.shape[1:])
    return pick(paired, 1 - bit_value, 1), pick(paired, bit_value, 1)


def scatter_grad(inputs, gradients, by_rows, seq_first, links):
    size = lax.axis_size("sp")
    me = lax.axis_index("sp")
    plane = lax.axis_index("seq")
    bits = [(me // (1 << b)) % 2 for b in range(index_bits())]
    left = inputs.reshape(-1, inputs.shape[-1])
    right = gradients.reshape(-1, gradients.shape[-1])
    depth = left.shape[1]
    columns = right.shape[1]
    rows = depth // size
    half = (rows if by_rows else columns) // 2
    if not by_rows:
        padded = -(-half // 128) * 128
        fill = ((0, 0), (0, padded - half))
        right = jnp.concatenate(
            [
                jnp.pad(pick_half(right[:, :half], right[:, half:]), fill),
                jnp.pad(pick_half(right[:, half:], right[:, :half]), fill),
            ],
            axis=1,
        )
    total = lax.dot_general(
        left, right, (((0,), (0,)), ((), ())), preferred_element_type=jnp.float32
    ).astype(jnp.bfloat16)
    if by_rows:
        total = total.reshape(size, 2, half, columns)
    else:
        total = total.reshape(size, rows, 2 * padded)
    sent, kept = split_blocks(total, bits[0])
    came = swap_sp(sent, 0, links)
    if by_rows:
        own, other = [
            (pick(kept, which, 1), pick(came, which, 1)) for which in (plane, 1 - plane)
        ]
    else:
        own = (kept[:, :, :padded], came[:, :, :padded])
        other = (kept[:, :, padded:], came[:, :, padded:])
    if seq_first:
        current = (*own, swap_seq(low_sum(*other), links))
        current = halve(current, bits[1], 1, links)
    else:
        own = halve(own, bits[1], 1, links)
        other = halve(other, bits[1], 1, links)
        current = (*own, swap_seq(low_sum(*other), links))
    for bit in range(2, index_bits()):
        current = halve(current, bits[bit], bit, links)
    mine = low_sum(*current)[0]
    theirs = swap_seq(mine, links, "last")
    if not by_rows:
        mine, theirs = mine[:, :half], theirs[:, :half]
    axis = 0 if by_rows else 1
    return pick_half(
        jnp.concatenate([mine, theirs], axis=axis), jnp.concatenate([theirs, mine], axis=axis)
    ).astype(jnp.float32)


def scatter_kernel(pairs, full_pairs, shrink_pairs, late_pairs, sources, n_in, *refs):
    factors, small = refs[:n_in], refs[n_in]
    refs = refs[n_in + 1 :]
    came, out, small_out = refs[:5], refs[5], refs[6]
    scratch = refs[7:]
    left_in, right_in, product, core_both, loaded = scratch[:5]
    sends, keeps = scratch[5:10], scratch[10:14]
    in_sem, load_sem, out_sem, core_send_sem, core_recv_sem, send_sem, recv_sem = scratch[14:21]
    small_sum, small_came, small_send, small_recv = scratch[21:]
    core_own, core_send = core_both.at[0], core_both.at[1]
    me = lax.axis_index("sp")
    plane = lax.axis_index("seq")

    def bit_of(bit):
        return (me // (1 << bit)) % 2

    def flip(bit):
        return (plane, me + (1 << bit) * (1 - 2 * bit_of(bit)))

    across = (1 - plane, me)
    core = bit_of(0)
    rows = out.shape[3]
    barrier = pltpu.get_barrier_semaphore()
    partners = [flip(bit) for bit in range(4)] + [across]
    for partner in partners:
        pl.semaphore_signal(
            barrier, inc=1, device_id=partner, device_id_type=pl.DeviceIdType.MESH
        )
    pl.semaphore_wait(barrier, len(partners))

    def among(pair, chosen):
        return sum([1 // (1 + (pair - p) * (pair - p)) for p in chosen], 0 * pair)

    def remote(source, target, send, recv, partner):
        return pltpu.make_async_remote_copy(
            src_ref=source,
            dst_ref=target,
            send_sem=send,
            recv_sem=recv,
            device_id=partner,
            device_id_type=pl.DeviceIdType.MESH,
        )

    def half_of(side):
        return plane if side == 0 else 1 - plane

    def core_copy(pair, chunk, side):
        number = 2 * chunk + side
        return remote(
            core_send.at[number],
            came[0].at[pair, number],
            core_send_sem.at[number],
            core_recv_sem.at[pair, number],
            flip(0),
        )

    def is_late(pair):
        return among(pair, late_pairs)

    def is_second(pair, chunk):
        return 0 * pair + 1 if chunk == 1 else among(pair, (pairs - 1,))

    def stage_partner(stage, chunk, pair):
        second = is_second(pair, chunk)
        if stage < 3:
            usual = (across, flip(1)) if stage == 1 else (flip(1), across)
            usual = tuple(a + second * (b - a) for a, b in zip(*usual))
        else:
            usual = flip(2) if stage == 3 else flip(3) if stage == 4 else across
        swapped = (flip(2), flip(3), across, flip(1), across)[stage - 1]
        late = is_late(pair)
        return tuple(a + late * (b - a) for a, b in zip(usual, swapped))

    def stage_copy(stage, pair, chunk):
        source = sends[stage - 1].at[pair % 2, chunk]
        target = out.at[pair, chunk, plane] if stage == 5 else came[stage].at[pair, chunk]
        return remote(
            source,
            target,
            send_sem.at[stage - 1, pair % 2, chunk],
            recv_sem.at[stage - 1, pair, chunk],
            stage_partner(stage, chunk, pair),
        )

    def out_copy(pair, chunk):
        return pltpu.make_async_copy(
            sends[4].at[pair % 2, chunk], out.at[pair, chunk, plane], out_sem.at[pair % 2, chunk]
        )

    def has(pair, chunk):
        return pair < (pairs if chunk == 0 else full_pairs)

    width = out.shape[4]

    def start_inputs(q, slot):
        for number, source in enumerate(sources):

            @pl.when(q == number)
            def _():
                for place, target, k in ((source[0], left_in, 0), (source[1], right_in, 1)):
                    pltpu.make_async_copy(
                        factors[place[0]].at[:, pl.ds(place[1], width)],
                        target.at[slot],
                        in_sem.at[slot, k],
                    ).start()

    def wait_inputs(slot):
        for target, k in ((left_in, 0), (right_in, 1)):
            pltpu.make_async_copy(
                factors[0].at[:, pl.ds(0, width)], target.at[slot], in_sem.at[slot, k]
            ).wait()

    def products(pair):
        start_inputs(4 * pair, 0)
        for chunk in (0, 1):

            @pl.when((pair > 0) & has(pair - 1, chunk))
            def _():
                for side in (0, 1):
                    core_copy(pair - 1, chunk, side).wait_send()

        last = pair // full_pairs
        shrink = among(pair, shrink_pairs)

        def one(j, carry):
            slot = j % 2

            @pl.when(j + 1 < 4 - 2 * last)
            def _():
                start_inputs(4 * pair + j + 1, 1 - slot)

            wait_inputs(slot)
            product[...] = lax.dot_general(
                left_in[slot],
                right_in[slot],
                (((0,), (0,)), ((), ())),
                preferred_element_type=jnp.float32,
            )

            def store(i, carry):
                owner = shrink * (4 * j + i // 4) + (1 - shrink) * i
                quarter = shrink * (i % 4) + (1 - shrink) * j
                number = quarter // 2 * 2 + (quarter % 2 + plane) % 2
                first = pl.multiple_of(i * rows, 8)
                core_both[(owner + core) % 2, number, owner // 2] = product[
                    pl.ds(first, rows), :
                ].astype(jnp.bfloat16)
                return carry

            lax.fori_loop(0, 16, store, 0)
            return carry

        lax.fori_loop(0, 4 - 2 * last, one, 0)
        for chunk in (0, 1):

            @pl.when(has(pair, chunk))
            def _():
                for side in (0, 1):
                    core_copy(pair, chunk, side).start()

    def add(a, b):
        return (a.astype(jnp.float32) + b.astype(jnp.float32)).astype(jnp.bfloat16)

    def load(source, slot, blocks):
        return pltpu.make_async_copy(
            source, loaded.at[slot, pl.ds(0, blocks)], load_sem.at[slot]
        )

    def free_send(stage, pair, chunk):
        @pl.when(pair >= 2)
        def _():
            stage_copy(stage, pair, chunk).wait_send()

    def add_core(pair):
        slot = pair % 2
        x = bit_of(1)
        for chunk in (0, 1):

            @pl.when(has(pair, chunk))
            def _():
                for side in (1, 0):
                    core_copy(pair, chunk, side).wait_recv()
                    load(came[0].at[pair, 2 * chunk + side], side, 8).start()
                free_send(1, pair, chunk)
                for side in (1, 0):
                    number = 2 * chunk + side
                    load(came[0].at[pair, number], side, 8).wait()
                    late = is_late(pair)

                    def both():
                        target = sends[0] if side == 1 else keeps[0]

                        def one(block, carry):
                            target[slot, chunk, block] = add(
                                core_own[number, block], loaded[side, block]
                            )
                            return carry

                        lax.fori_loop(0, 8, one, 0)
                        if side == 1:
                            stage_copy(1, pair, chunk).start()

                    def split():
                        def one(i, carry):
                            usual = 2 * i
                            other = 4 * (i // 2) + i % 2
                            low = bit_of(2)
                            for target, a, b in (
                                (sends[0], usual + 1 - x, other + 2 * (1 - low)),
                                (keeps[0], usual + x, other + 2 * low),
                            ):
                                block = a + late * (b - a)
                                target[slot, chunk, 4 * side + i] = add(
                                    core_own[number, block], loaded[side, block]
                                )
                            return carry

                        lax.fori_loop(0, 4, one, 0)
                        if side == 0:
                            stage_copy(1, pair, chunk).start()

                    if chunk == 0:
                        apart = late + is_second(pair, chunk)
                        pl.when(apart == 0)(both)
                        pl.when(apart == 1)(split)
                    else:
                        split()

    def add_stage(stage, pair):
        slot = pair % 2
        blocks = 16 >> stage
        for chunk in (0, 1):

            @pl.when(has(pair, chunk))
            def _():
                stage_copy(stage, pair, chunk).wait_recv()
                load(came[stage].at[pair, chunk], chunk, blocks).start()
        for chunk in (0, 1):

            @pl.when(has(pair, chunk))
            def _():
                free_send(stage + 1, pair, chunk)
                if stage == 4:

                    @pl.when(pair >= 2)
                    def _():
                        out_copy(pair, chunk).wait()

                load(came[stage].at[pair, chunk], chunk, blocks).wait()
                old, new = keeps[stage - 1], keeps[stage] if stage < 4 else None

                def one(i, carry):
                    late = is_late(pair)
                    x, low, high = bit_of(1), bit_of(2), bit_of(3)
                    if stage == 1:
                        second = is_second(pair, chunk)
                        a = (
                            2 * i + 1 - x + second * (3 + x - i),
                            2 * i + x + second * (-x - i),
                        )
                        start = 4 * (i // 2) + i % 2
                        b = (start + 2 * (1 - high), start + 2 * high)
                    elif stage == 2:
                        a = (2 * i + 1 - low, 2 * i + low)
                        b = (2 + i, i)
                    else:
                        a = (1 - high, high)
                        b = (1 - x, x)
                    gone, kept = [p + late * (q - p) for p, q in zip(a, b)]
                    sends[stage][slot, chunk, i] = add(
                        old[slot, chunk, gone], loaded[chunk, gone]
                    )
                    new[slot, chunk, i] = add(old[slot, chunk, kept], loaded[chunk, kept])
                    return carry

                if stage < 4:
                    lax.fori_loop(0, blocks // 2, one, 0)
                else:
                    sends[4][slot, chunk] = add(old[slot, chunk, 0], loaded[chunk, 0])
                    out_copy(pair, chunk).start()
                stage_copy(stage + 1, pair, chunk).start()

    def small_copy(stage):
        return remote(
            small_sum.at[stage],
            small_came.at[stage],
            small_send.at[stage],
            small_recv.at[stage],
            partners[stage],
        )

    small_sum[0] = small[...]
    small_copy(0).start()

    def turn(time, carry):
        for stage in range(len(partners)):

            @pl.when(time == stage)
            def _():
                small_copy(stage).wait_recv()
                total = small_sum[stage] + small_came[stage]
                if stage + 1 < len(partners):
                    small_sum[stage + 1] = total
                    small_copy(stage + 1).start()
                else:
                    small_out[...] = total

        for lag, work in (
            (1, add_core),
            (2, functools.partial(add_stage, 1)),
            (3, functools.partial(add_stage, 2)),
            (4, functools.partial(add_stage, 3)),
            (5, functools.partial(add_stage, 4)),
            (0, products),
        ):
            pair = time - lag

            @pl.when((pair >= 0) & (pair < pairs))
            def _():
                work(pair)

        return carry

    lax.fori_loop(0, pairs + 5, turn, 0)
    for stage in range(len(partners)):
        small_copy(stage).wait_send()
    for chunk in (0, 1):
        mine = pairs if chunk == 0 else full_pairs
        if mine == pairs:
            for side in (0, 1):
                core_copy(mine - 1, chunk, side).wait_send()
        for pair in range(max(mine - 2, 0), mine):
            out_copy(pair, chunk).wait()
            for stage in range(1, 6):
                stage_copy(stage, pair, chunk).wait_send()
        for pair in range(mine):
            stage_copy(5, pair, chunk).wait_recv()


def scatter_products(
    factors, sources, small, pairs, full_pairs, shrink_pairs, rows, width, collective_id
):
    tokens = factors[0].shape[0]
    depth = 16 * rows
    low = jnp.bfloat16

    def blocks(*lead):
        return jax.ShapeDtypeStruct((*lead, rows, width), low)

    hbm = [
        blocks(pairs, 4, 8),
        blocks(pairs, 2, 8),
        blocks(pairs, 2, 4),
        blocks(pairs, 2, 2),
        blocks(pairs, 2, 1),
        blocks(pairs, 2, 2),
    ]
    any_space = pl.BlockSpec(memory_space=pl.ANY)

    def vmem(*lead):
        return pltpu.VMEM((*lead, rows, width), low)

    dma = pltpu.SemaphoreType.DMA
    whole = pl.BlockSpec(memory_space=pltpu.VMEM)
    *_, out, total = pl.pallas_call(
        functools.partial(
            scatter_kernel, pairs, full_pairs, shrink_pairs, (), sources, len(factors)
        ),
        out_shape=hbm + [jax.ShapeDtypeStruct(small.shape, small.dtype)],
        in_specs=[any_space] * len(factors) + [whole],
        out_specs=[any_space] * len(hbm) + [whole],
        scratch_shapes=[
            pltpu.VMEM((2, tokens, width), low),
            pltpu.VMEM((2, tokens, width), low),
            pltpu.VMEM((depth, width), jnp.float32),
            vmem(2, 4, 8),
            vmem(2, 8),
            vmem(2, 2, 8),
            vmem(2, 2, 4),
            vmem(2, 2, 2),
            vmem(2, 2, 1),
            vmem(2, 2),
            vmem(2, 2, 8),
            vmem(2, 2, 4),
            vmem(2, 2, 2),
            vmem(2, 2, 1),
            dma((2, 2)),
            dma((2,)),
            dma((2, 2)),
            dma((4,)),
            dma((pairs, 4)),
            dma((5, 2, 2)),
            dma((5, pairs, 2)),
            pltpu.VMEM((5, *small.shape), small.dtype),
            pltpu.VMEM((5, *small.shape), small.dtype),
            dma((5,)),
            dma((5,)),
        ],
        compiler_params=pltpu.CompilerParams(
            collective_id=collective_id, has_side_effects=True, vmem_limit_bytes=58 << 20
        ),
        cost_estimate=pl.CostEstimate(
            flops=2 * len(sources) * depth * tokens * width,
            bytes_accessed=16 * len(sources) * depth * width,
            transcendentals=0,
        ),
    )(*factors, small)
    return out, total


BESIDE = ((1, "shrink"), )


def token_rows(gradients):
    return gradients.reshape(-1, gradients.shape[-1])


def scatter_all(terms, small):
    size = lax.axis_size("sp")
    if size != 16 or lax.axis_size("seq") != 2:
        links = {}
        flags = [(False, False), (True, True), (False, False), (False, True)]
        blocks = [
            [scatter_grad(*pair, *flag, links) for pair, flag in zip(block, flags)]
            for block in terms[:2]
        ]
        last = [scatter_grad(*pair, False, False, links) for pair in terms[2]]
        return blocks[0], blocks[1], last, lax.psum(small, ("seq", "sp"))
    factors, sources = [], []

    def add_factors(pair):
        factors.extend(token_rows(member) for member in pair)
        return len(factors) - 2, len(factors) - 1

    names = ("expand", "shrink", "qkv", "out")
    results = [dict(), dict()]
    shrink_pairs, homes = [], []

    def beside(block, name):
        left, right = [token_rows(member) for member in terms[block][names.index(name)]]
        product = lax.dot_general(
            left, right, (((0,), (0,)), ((), ())), preferred_element_type=jnp.float32
        ).astype(jnp.bfloat16)
        return lax.psum_scatter(product, "sp", scatter_dimension=0, tiled=True)

    early = [beside(block, name) for block, name in BESIDE]
    for block in (1, 0):
        expand, shrink, qkv, out = terms[block]
        if (block, "shrink") not in BESIDE:
            shrink_pairs.append(len(homes))
            homes.append((block, "shrink"))
            left, right = add_factors(shrink)
            sources += [((left, j * D), (right, 0)) for j in range(4)]
        if (block, "expand") not in BESIDE:
            homes.append((block, "expand"))
            left, right = add_factors(expand)
            sources += [((left, 0), (right, j * D)) for j in range(4)]
        homes.append((block, "qkv"))
        left, right = add_factors(qkv)
        sources += [((left, 0), (right, j * D)) for j in range(3)]
        left, right = add_factors(out)
        sources.append(((left, 0), (right, 0)))
    for pair in terms[2]:
        left, right = add_factors(pair)
        sources.append(((left, 0), (right, 0)))
    pairs = len(homes) + 1
    if early:
        small, first = lax.optimization_barrier((small, early[0]))
        early[0] = first
    done, total = scatter_products(
        factors, sources, small, pairs, pairs - 1, tuple(shrink_pairs), D // size, D, 1
    )
    done = done.astype(jnp.float32)

    def quarter(pair, k):
        return done[pair, k // 2, k % 2]

    for pair, (block, name) in enumerate(homes):
        parts = [quarter(pair, k) for k in range(4)]
        if name == "qkv":
            results[block]["out"] = parts.pop()
        results[block][name] = jnp.concatenate(parts, axis=0 if name == "shrink" else 1)
    for (block, name), part in zip(BESIDE, early):
        results[block][name] = sum_seq(part)
    last = [quarter(pairs - 1, k) for k in range(2)]
    ordered = [[found[name] for name in names] for found in results]
    return ordered[0], ordered[1], last, total


def halve(members, bit_value, bit, links):
    parts = [split_blocks(member, bit_value) for member in members]
    sent = low_sum(*[part[0] for part in parts])
    return (low_sum(*[part[1] for part in parts]), swap_sp(sent, bit, links))


def sum_seq(values):
    mine = values.astype(jnp.bfloat16)
    return mine.astype(jnp.float32) + swap_seq(mine, {}).astype(jnp.float32)


def triple_bias(query_bias, value_bias):
    head_query = query_bias.reshape(HEADS, 1, HEAD_DIM)
    head_value = value_bias.reshape(HEADS, 1, HEAD_DIM)
    return jnp.concatenate([head_query, jnp.zeros_like(head_query), head_value], axis=1).reshape(
        3 * D
    )


def pair_bias(value_bias):
    head_value = value_bias.reshape(HEADS, 1, HEAD_DIM)
    return jnp.concatenate([jnp.zeros_like(head_value), head_value], axis=1).reshape(2 * D)


def triple_bias_grad(totals):
    split_rows = totals.reshape(HEADS, 3, HEAD_DIM)
    return (split_rows[:, 0].reshape(D), split_rows[:, 2].reshape(D))


def frame_modulation(segment_ids, timesteps):
    onehot = (segment_ids[:, :, None] == jnp.arange(CLIPS)[None, None, :]).astype(jnp.float32)
    features = time_features(timesteps)
    return jnp.einsum("sfc,scz->sfz", onehot, features, precision=lax.Precision.HIGHEST)


def block_pieces(table_rows, frame_mod):
    modulation = table_rows[None, None] + frame_mod
    return [modulation[:, :, number][:, :, None, :] for number in range(6)]


def gated_back(grad_out, gating, branch):
    branch_grad = (gating * grad_out).astype(jnp.bfloat16)
    gate_grad = jnp.sum(grad_out * branch, axis=2, keepdims=True)
    return (branch_grad, gate_grad)


def split_kernel(width, source, target):
    for head in range(HEADS):
        target[:, head] = source[:, :, head * width : (head + 1) * width]


def merge_kernel(width, source, target):
    for head in range(HEADS):
        target[:, :, head * width : (head + 1) * width] = source[:, head]


def move_heads(kernel, values, width, shape):
    step = 8

    def block(dims):
        return pl.BlockSpec((step, *dims[1:]), lambda i: (i, *[0] * (len(dims) - 1)))

    return pl.pallas_call(
        functools.partial(kernel, width),
        grid=(shape[0] // step,),
        in_specs=[block(values.shape)],
        out_specs=block(shape),
        out_shape=jax.ShapeDtypeStruct(shape, values.dtype),
        compiler_params=pltpu.CompilerParams(vmem_limit_bytes=32 << 20),
        cost_estimate=pl.CostEstimate(
            flops=0, bytes_accessed=4 * values.size, transcendentals=0
        ),
    )(values)


def to_pairs(values):
    groups, frames, patches, columns = values.shape
    width = columns // HEADS
    flat = values.reshape(groups * frames, patches, columns)
    shape = (groups * frames, HEADS, patches, width)
    return move_heads(split_kernel, flat, width, shape).reshape(
        lax.axis_size("sp"), -1, patches, width
    )


def from_pairs(values, groups, frames):
    devices, pair_count, patches, width = values.shape
    pairs = values.reshape(groups * frames, HEADS, patches, width)
    shape = (groups * frames, patches, HEADS * width)
    return move_heads(merge_kernel, pairs, width, shape)


def pair_scores(triple):
    queries = triple[..., :HEAD_DIM]
    key_rows = triple[..., HEAD_DIM : 2 * HEAD_DIM]
    scores = jnp.einsum(
        "zkqe,zkre->zkqr", queries, key_rows, preferred_element_type=jnp.float32
    ) * HEAD_DIM ** (-0.5)
    return jax.nn.softmax(scores, axis=-1)


def attend_pairs(triple):
    attention = pair_scores(triple).astype(jnp.bfloat16)
    mixture = jnp.einsum(
        "zkqr,zkre->zkqe",
        attention,
        triple[..., 2 * HEAD_DIM :],
        preferred_element_type=jnp.float32,
    ).astype(jnp.bfloat16)
    return lax.all_to_all(mixture, "sp", split_axis=2, concat_axis=0, tiled=True)


def pair_backward(members):
    triple, out_grad = members
    queries = triple[..., :HEAD_DIM]
    key_rows = triple[..., HEAD_DIM : 2 * HEAD_DIM]
    value_rows = triple[..., 2 * HEAD_DIM :]
    attention = pair_scores(triple)
    rounded = attention.astype(jnp.bfloat16)
    prob_grad = jnp.einsum(
        "zkqe,zkre->zkqr", out_grad, value_rows, preferred_element_type=jnp.float32
    )
    centre = jnp.sum(prob_grad * attention, axis=-1, keepdims=True)
    score_grad = (attention * (prob_grad - centre)).astype(jnp.bfloat16)
    scaling = HEAD_DIM ** (-0.5)
    query_grad = (
        jnp.einsum("zkqr,zkre->zkqe", score_grad, key_rows, preferred_element_type=jnp.float32)
        * scaling
    )
    key_grad = (
        jnp.einsum("zkqr,zkqe->zkre", score_grad, queries, preferred_element_type=jnp.float32)
        * scaling
    )
    value_grad = jnp.einsum(
        "zkqr,zkqe->zkre", rounded, out_grad, preferred_element_type=jnp.float32
    )
    gradients = jnp.concatenate([query_grad, key_grad, value_grad], axis=-1).astype(jnp.bfloat16)
    return lax.all_to_all(gradients, "sp", split_axis=2, concat_axis=0, tiled=True)


def pair_attention(triple):
    groups, frames, patches = triple.shape[:3]
    pairs = lax.all_to_all(to_pairs(triple), "sp", split_axis=0, concat_axis=2, tiled=True)
    exchanged = attend_pairs(pairs)
    return from_pairs(exchanged, groups, frames).reshape(groups, frames, patches, D), pairs


def pair_attention_back(pairs, mixture_grad):
    groups, frames, patches = mixture_grad.shape[:3]
    returned = pair_backward(
        (
            pairs,
            lax.all_to_all(to_pairs(mixture_grad), "sp", split_axis=0, concat_axis=2, tiled=True),
        )
    )
    return from_pairs(returned, groups, frames).reshape(groups, frames, patches, 3 * D)


def feed_forward(residual, offset, scaling, gating, expand, shrink, vectors, start_row):
    hidden = modulate(residual, offset, scaling).astype(jnp.bfloat16)
    inner_sum = project(hidden, expand) + vectors[start_row : start_row + 4].reshape(FF)
    active = gelu_tanh(inner_sum).astype(jnp.bfloat16)
    branch = project(active, shrink) + vectors[3]
    return ((hidden, inner_sum, active, branch), residual + gating * branch)


def feed_backward(grad_out, residual, offset, scaling, gating, stored, expand, shrink):
    hidden, inner_sum, active, branch = stored
    branch_grad, gate_grad = gated_back(grad_out, gating, branch)
    shrink_grad = (active, branch_grad)
    active_grad = input_grad(branch_grad, shrink)
    gelu_value, gelu_back = jax.vjp(gelu_tanh, inner_sum)
    inner_grad = gelu_back(active_grad)[0].astype(jnp.bfloat16)
    expand_grad = (hidden, inner_grad)
    hidden_grad = input_grad(inner_grad, expand)
    norm_value, norm_back = jax.vjp(modulate, residual, offset, scaling)
    residual_grad, offset_grad, scaling_grad = norm_back(hidden_grad)
    return (
        grad_out + residual_grad,
        [offset_grad, scaling_grad, gate_grad],
        (expand_grad, shrink_grad, column_sum(inner_grad), column_sum(branch_grad)),
    )


def table_sums(members):
    return jnp.stack([jnp.sum(member, axis=(0, 1, 2)) for member in members])


def spatial_forward(residual, weights, frame_mod):
    qkv_weight, out_weight, expand, shrink, vectors = weights
    vectors_f = as_float(vectors)
    pieces = block_pieces(vectors_f[4:10], frame_mod)
    hidden = modulate(residual, pieces[0], pieces[1]).astype(jnp.bfloat16)
    triple = (project(hidden, qkv_weight) + triple_bias(vectors_f[0], vectors_f[1])).astype(
        jnp.bfloat16
    )
    mixture, pairs = pair_attention(triple)
    branch = project(mixture, out_weight) + vectors_f[2]
    middle = residual + pieces[2] * branch
    stored_ffn, result = feed_forward(
        middle, pieces[3], pieces[4], pieces[5], expand, shrink, vectors_f, 10
    )
    return (result, (hidden, pairs, mixture, branch, middle, stored_ffn))


def spatial_backward(grad_out, residual, weights, frame_mod, stored):
    qkv_weight, out_weight, expand, shrink, vectors = weights
    pieces = block_pieces(as_float(vectors)[4:10], frame_mod)
    hidden, pairs, mixture, branch, middle, stored_ffn = stored
    middle_grad, ffn_table, ffn_grads = feed_backward(
        grad_out, middle, pieces[3], pieces[4], pieces[5], stored_ffn, expand, shrink
    )
    branch_grad, gate_grad = gated_back(middle_grad, pieces[2], branch)
    out_weight_grad = (mixture, branch_grad)
    out_bias = column_sum(branch_grad)
    mixture_grad = input_grad(branch_grad, out_weight).astype(jnp.bfloat16)
    triple_grad = pair_attention_back(pairs, mixture_grad)
    qkv_grad = (hidden, triple_grad)
    query_bias, value_bias = triple_bias_grad(column_sum(triple_grad))
    hidden_grad = input_grad(triple_grad, qkv_weight)
    norm_value, norm_back = jax.vjp(modulate, residual, pieces[0], pieces[1])
    residual_grad, offset_grad, scaling_grad = norm_back(hidden_grad)
    table_grad = table_sums([offset_grad, scaling_grad, gate_grad] + ffn_table)
    vector_grad = jnp.concatenate(
        [
            jnp.stack([query_bias, value_bias, out_bias, ffn_grads[3]]),
            table_grad,
            ffn_grads[2].reshape(4, D),
        ],
        axis=0,
    )
    return (
        middle_grad + residual_grad,
        (qkv_grad, out_weight_grad, ffn_grads[0], ffn_grads[1], vector_grad),
    )


def temporal_scores(triple, same_clip):
    scores = jnp.einsum(
        "sfphe,sgphe->sphfg",
        triple[..., :HEAD_DIM],
        triple[..., HEAD_DIM : 2 * HEAD_DIM],
        preferred_element_type=jnp.float32,
    ) * HEAD_DIM ** (-0.5)
    return jax.nn.softmax(jnp.where(same_clip, scores, masked_score), axis=-1)


def caption_scores(queries, keyval, allowed):
    scores = jnp.einsum(
        "sfphe,srhe->sfphr", queries, keyval[..., :HEAD_DIM], preferred_element_type=jnp.float32
    ) * HEAD_DIM ** (-0.5)
    return jax.nn.softmax(jnp.where(allowed, scores, masked_score), axis=-1)


def temporal_forward(residual, weights, frame_mod, same_clip, allowed, context):
    qkv_weight, out_weight, expand, shrink, query_weight, keyval_weight, cross_weight, vectors = (
        weights
    )
    vectors_f = as_float(vectors)
    pieces = block_pieces(vectors_f[8:14], frame_mod)
    groups, frames, patches = residual.shape[:3]
    hidden = modulate(residual, pieces[0], pieces[1]).astype(jnp.bfloat16)
    triple = (project(hidden, qkv_weight) + triple_bias(vectors_f[0], vectors_f[1])).astype(
        jnp.bfloat16
    )
    triple = triple.reshape(groups, frames, patches, HEADS, 3 * HEAD_DIM)
    attention = temporal_scores(triple, same_clip).astype(jnp.bfloat16)
    mixture = (
        jnp.einsum(
            "sphfg,sgphe->sfphe",
            attention,
            triple[..., 2 * HEAD_DIM :],
            preferred_element_type=jnp.float32,
        )
        .astype(jnp.bfloat16)
        .reshape(groups, frames, patches, D)
    )
    branch = project(mixture, out_weight) + vectors_f[2]
    middle = residual + pieces[2] * branch
    lowered = middle.astype(jnp.bfloat16)
    queries = (project(lowered, query_weight) + vectors_f[4]).astype(jnp.bfloat16)
    queries = queries.reshape(groups, frames, patches, HEADS, HEAD_DIM)
    keyval = (project(context, keyval_weight) + pair_bias(vectors_f[5])).astype(jnp.bfloat16)
    keyval = keyval.reshape(groups, -1, HEADS, 2 * HEAD_DIM)
    cross_probs = caption_scores(queries, keyval, allowed).astype(jnp.bfloat16)
    cross_mix = (
        jnp.einsum(
            "sfphr,srhe->sfphe",
            cross_probs,
            keyval[..., HEAD_DIM:],
            preferred_element_type=jnp.float32,
        )
        .astype(jnp.bfloat16)
        .reshape(groups, frames, patches, D)
    )
    crossed = middle + project(cross_mix, cross_weight) + vectors_f[6]
    stored_ffn, result = feed_forward(
        crossed, pieces[3], pieces[4], pieces[5], expand, shrink, vectors_f, 14
    )
    return (
        result,
        (
            hidden,
            triple,
            mixture,
            branch,
            middle,
            lowered,
            queries,
            keyval,
            cross_mix,
            crossed,
            stored_ffn,
        ),
    )


def temporal_backward(grad_out, residual, weights, frame_mod, same_clip, allowed, stored):
    qkv_weight, out_weight, expand, shrink, query_weight, keyval_weight, cross_weight, vectors = (
        weights
    )
    pieces = block_pieces(as_float(vectors)[8:14], frame_mod)
    (
        hidden,
        triple,
        mixture,
        branch,
        middle,
        lowered,
        queries,
        keyval,
        cross_mix,
        crossed,
        stored_ffn,
    ) = stored
    groups, frames, patches = residual.shape[:3]
    scaling = HEAD_DIM ** (-0.5)
    crossed_grad, ffn_table, ffn_grads = feed_backward(
        grad_out, crossed, pieces[3], pieces[4], pieces[5], stored_ffn, expand, shrink
    )
    cross_branch_grad = crossed_grad.astype(jnp.bfloat16)
    cross_weight_grad = (cross_mix, cross_branch_grad)
    cross_bias = column_sum(cross_branch_grad)
    mix_grad = input_grad(cross_branch_grad, cross_weight).astype(jnp.bfloat16)
    mix_grad = mix_grad.reshape(groups, frames, patches, HEADS, HEAD_DIM)
    cross_probs = caption_scores(queries, keyval, allowed)
    rounded = cross_probs.astype(jnp.bfloat16)
    prob_grad = jnp.einsum(
        "sfphe,srhe->sfphr", mix_grad, keyval[..., HEAD_DIM:], preferred_element_type=jnp.float32
    )
    centre = jnp.sum(prob_grad * cross_probs, axis=-1, keepdims=True)
    score_grad = (cross_probs * (prob_grad - centre)).astype(jnp.bfloat16)
    query_grad = (
        jnp.einsum(
            "sfphr,srhe->sfphe",
            score_grad,
            keyval[..., :HEAD_DIM],
            preferred_element_type=jnp.float32,
        )
        * scaling
    )
    query_grad = query_grad.astype(jnp.bfloat16).reshape(groups, frames, patches, D)
    key_grad = (
        jnp.einsum("sfphr,sfphe->srhe", score_grad, queries, preferred_element_type=jnp.float32)
        * scaling
    )
    value_grad = jnp.einsum(
        "sfphr,sfphe->srhe", rounded, mix_grad, preferred_element_type=jnp.float32
    )
    keyval_grad = jnp.concatenate([key_grad, value_grad], axis=-1).reshape(groups, -1, 2 * D)
    keyval_grad = lax.psum(keyval_grad.astype(jnp.bfloat16), "sp")
    query_weight_grad = (lowered, query_grad)
    cross_query_bias = column_sum(query_grad)
    middle_grad = crossed_grad + input_grad(query_grad, query_weight)
    branch_grad, gate_grad = gated_back(middle_grad, pieces[2], branch)
    out_weight_grad = (mixture, branch_grad)
    out_bias = column_sum(branch_grad)
    mixture_grad = input_grad(branch_grad, out_weight).astype(jnp.bfloat16)
    mixture_grad = mixture_grad.reshape(groups, frames, patches, HEADS, HEAD_DIM)
    attention = temporal_scores(triple, same_clip)
    rounded_t = attention.astype(jnp.bfloat16)
    prob_grad_t = jnp.einsum(
        "sfphe,sgphe->sphfg",
        mixture_grad,
        triple[..., 2 * HEAD_DIM :],
        preferred_element_type=jnp.float32,
    )
    centre_t = jnp.sum(prob_grad_t * attention, axis=-1, keepdims=True)
    score_grad_t = (attention * (prob_grad_t - centre_t)).astype(jnp.bfloat16)
    query_part = (
        jnp.einsum(
            "sphfg,sgphe->sfphe",
            score_grad_t,
            triple[..., HEAD_DIM : 2 * HEAD_DIM],
            preferred_element_type=jnp.float32,
        )
        * scaling
    )
    key_part = (
        jnp.einsum(
            "sphfg,sfphe->sgphe",
            score_grad_t,
            triple[..., :HEAD_DIM],
            preferred_element_type=jnp.float32,
        )
        * scaling
    )
    value_part = jnp.einsum(
        "sphfg,sfphe->sgphe", rounded_t, mixture_grad, preferred_element_type=jnp.float32
    )
    triple_grad = jnp.concatenate([query_part, key_part, value_part], axis=-1).astype(jnp.bfloat16)
    triple_grad = triple_grad.reshape(groups, frames, patches, 3 * D)
    qkv_grad = (hidden, triple_grad)
    query_bias, value_bias = triple_bias_grad(column_sum(triple_grad))
    hidden_grad = input_grad(triple_grad, qkv_weight)
    norm_value, norm_back = jax.vjp(modulate, residual, pieces[0], pieces[1])
    residual_grad, offset_grad, scaling_grad = norm_back(hidden_grad)
    table_grad = table_sums([offset_grad, scaling_grad, gate_grad] + ffn_table)
    zero_row = jnp.zeros((D,), jnp.float32)
    vector_grad = jnp.concatenate(
        [
            jnp.stack(
                [
                    query_bias,
                    value_bias,
                    out_bias,
                    ffn_grads[3],
                    cross_query_bias,
                    zero_row,
                    cross_bias,
                    zero_row,
                ]
            ),
            table_grad,
            ffn_grads[2].reshape(4, D),
        ],
        axis=0,
    )
    terms = (
        qkv_grad,
        out_weight_grad,
        ffn_grads[0],
        ffn_grads[1],
        query_weight_grad,
        cross_weight_grad,
        vector_grad,
    )
    return (middle_grad + residual_grad, terms, keyval_grad)


def on_device(
    video,
    segment_ids,
    timesteps,
    drop_mask,
    captions,
    null_caption,
    caption_weight,
    spatial_qkv,
    spatial_out,
    spatial_expand,
    spatial_shrink,
    spatial_vectors,
    temporal_qkv,
    temporal_out,
    temporal_expand,
    temporal_shrink,
    cross_query,
    cross_keyval,
    cross_out,
    temporal_vectors,
    cotangent,
):
    groups, frames, patches = video.shape[:3]
    size = lax.axis_size("sp")
    third = D
    wide = [
        spatial_qkv,
        spatial_out,
        spatial_expand,
        temporal_qkv,
        temporal_out,
        cross_query,
        cross_keyval,
        cross_out,
    ]

    def rounds_of(rows):
        cut = 512

        def block_round(qkv, out, start, width):
            return columns_round(
                (qkv, start, width),
                (qkv, third + start, width),
                (qkv, 2 * third + start, width),
                (out, start, width),
            )

        def expand_round(weight, late=False):
            quarter = FF // 4
            return columns_round(*[(weight, k * quarter, quarter) for k in range(4)], late=late)

        return [
            block_round(0, 1, 0, cut),
            block_round(0, 1, cut, third - cut),
            expand_round(2),
            rows_round(8, rows),
            columns_round((5, 0, third), (6, 0, third), (6, third, third), (7, 0, third)),
            block_round(3, 4, 0, cut),
            block_round(3, 4, cut, third - cut),
        ]

    (
        full_sqkv,
        full_sout,
        full_sexp,
        full_tqkv,
        full_tout,
        full_cq,
        full_ckv,
        full_cout,
        full_sshr,
        all_vectors,
    ) = gather_all(
        [spatial_shrink],
        wide,
        jnp.concatenate([spatial_vectors, temporal_vectors], axis=0),
        rounds_of,
        0,
    )
    full_sqkv, expand_shard, shrink_shard = lax.optimization_barrier(
        (full_sqkv, temporal_expand, temporal_shrink)
    )
    full_texp = lax.all_gather(expand_shard, "sp", axis=0, tiled=True)
    full_tshr = lax.all_gather(shrink_shard, "sp", axis=0, tiled=True)
    n_spatial = spatial_vectors.shape[0]
    spatial = (full_sqkv, full_sout, full_sexp, full_sshr, all_vectors[:n_spatial])
    temporal = (
        full_tqkv,
        full_tout,
        full_texp,
        full_tshr,
        full_cq,
        full_ckv,
        full_cout,
        all_vectors[n_spatial:],
    )
    dropped = (drop_mask > 0).astype(jnp.float32)
    text_local = jnp.where(drop_mask[:, :, None, None] > 0, null_caption[None, None], captions)
    text_rows = text_local.reshape(groups, CLIPS * CAP, -1)
    caption_sum = lax.psum(project(text_rows, caption_weight).astype(jnp.float32), "sp")
    caption_sum, first = lax.optimization_barrier((caption_sum, spatial[0]))
    spatial = (first, *spatial[1:])
    frame_mod = frame_modulation(segment_ids, timesteps).reshape(groups, frames, 6, D)
    same_clip = (segment_ids[:, :, None] == segment_ids[:, None, :])[:, None, None]
    row_clip = jnp.arange(CLIPS * CAP) // CAP
    allowed = (segment_ids[:, :, None] == row_clip[None, None, :])[:, :, None, None, :]
    residual = video.astype(jnp.float32)
    middle, spatial_kept = spatial_forward(residual, spatial, frame_mod)
    context = (caption_sum + as_float(temporal[7])[7]).astype(jnp.bfloat16)
    result, temporal_kept = temporal_forward(
        middle, temporal, frame_mod, same_clip, allowed, context
    )
    output = result.astype(jnp.bfloat16)
    middle_grad, temporal_terms, keyval_grad = temporal_backward(
        cotangent.astype(jnp.float32),
        middle,
        temporal,
        frame_mod,
        same_clip,
        allowed,
        temporal_kept,
    )
    shard_rows = D // lax.axis_size("sp")
    first_row = lax.axis_index("sp") * shard_rows
    video_grad, spatial_terms = spatial_backward(
        middle_grad, residual, spatial, frame_mod, spatial_kept
    )
    spatial_sums, temporal_sums, cross_sums, vector_total = scatter_all(
        (
            (spatial_terms[2], spatial_terms[3], spatial_terms[0], spatial_terms[1]),
            (temporal_terms[2], temporal_terms[3], temporal_terms[0], temporal_terms[1]),
            (temporal_terms[4], temporal_terms[5]),
        ),
        jnp.concatenate([spatial_terms[4], temporal_terms[6]], axis=0),
    )
    vector_total = lax.dynamic_slice_in_dim(vector_total, first_row, shard_rows, 1)
    keyval_grad, vector_total = lax.optimization_barrier((keyval_grad, vector_total))
    context_grad = input_grad(keyval_grad, temporal[5]).astype(jnp.bfloat16)
    local_context = lax.dynamic_slice_in_dim(context, first_row, shard_rows, 2)
    keyval_weight_grad = weight_grad(local_context, keyval_grad)
    value_bias_full = column_sum(keyval_grad).reshape(HEADS, 2, HEAD_DIM)[:, 1].reshape(D)
    caption_bias_full = column_sum(context_grad)
    caption_weight_grad = weight_grad(text_rows, context_grad)
    text_grad = input_grad(context_grad, caption_weight).reshape(groups, CLIPS, CAP, -1)
    null_grad = jnp.sum(text_grad * dropped[:, :, None, None], axis=(0, 1))
    own_rows = [
        lax.dynamic_slice_in_dim(row, first_row, shard_rows, 0)
        for row in (value_bias_full, caption_bias_full)
    ]
    width = null_grad.shape[1]
    flat = jnp.stack([jnp.pad(row, (0, width - shard_rows)) for row in own_rows])
    small_total = sum_seq(jnp.concatenate([null_grad, flat], axis=0))
    null_total = small_total[: null_grad.shape[0]]
    bias_total = small_total[null_grad.shape[0] :, :shard_rows]
    vector_total = vector_total.at[n_spatial + 5].add(bias_total[0])
    vector_total = vector_total.at[n_spatial + 7].add(bias_total[1])
    return (
        output,
        video_grad.astype(jnp.bfloat16),
        null_total,
        sum_seq(caption_weight_grad),
        spatial_sums[2],
        spatial_sums[3],
        spatial_sums[0],
        spatial_sums[1],
        vector_total[:n_spatial],
        temporal_sums[2],
        temporal_sums[3],
        temporal_sums[0],
        temporal_sums[1],
        cross_sums[0],
        sum_seq(keyval_weight_grad),
        cross_sums[1],
        vector_total[n_spatial:],
    )


def solution(mesh):
    return jax.shard_map(
        on_device,
        mesh=mesh,
        in_specs=(
            P("seq", None, "sp", None),
            P("seq", None),
            P("seq", None),
            P("seq", None),
            P("seq", None, None, "sp"),
            P(None, "sp"),
            P("sp", None),
            P("sp", None),
            P("sp", None),
            P("sp", None),
            P("sp", None),
            P(None, "sp"),
            P("sp", None),
            P("sp", None),
            P("sp", None),
            P("sp", None),
            P("sp", None),
            P("sp", None),
            P("sp", None),
            P(None, "sp"),
            P("seq", None, "sp", None),
        ),
        out_specs=(
            P("seq", None, "sp", None),
            P("seq", None, "sp", None),
            P(None, "sp"),
            P("sp", None),
            P("sp", None),
            P("sp", None),
            P("sp", None),
            P("sp", None),
            P(None, "sp"),
            P("sp", None),
            P("sp", None),
            P("sp", None),
            P("sp", None),
            P("sp", None),
            P("sp", None),
            P("sp", None),
            P(None, "sp"),
        ),
        check_vma=False,
    )
```

```python
import functools
import math

import jax
import jax.numpy as jnp
from jax import lax
from jax.experimental import pallas as pl
from jax.experimental.pallas import tpu as pltpu
from jax.sharding import PartitionSpec as P

D = 1152
HEADS = 16
HEAD_DIM = 72
FF = 4608
CAP = 120
CLIPS = 2


norm_eps = 1e-06
masked_score = -1e30


def time_features(timestep):
    half_width = 3 * D
    frequency = jnp.exp(
        jnp.arange(half_width, dtype=jnp.float32) * (-math.log(10000.0) / half_width)
    )
    angles = timestep.astype(jnp.float32)[..., None] * frequency
    return 0.5 * jnp.concatenate([jnp.cos(angles), jnp.sin(angles)], axis=-1)


def layer_norm(residual):
    center = residual - jnp.mean(residual, axis=-1, keepdims=True)
    return center * lax.rsqrt(jnp.mean(center * center, axis=-1, keepdims=True) + norm_eps)


def modulate(residual, offset, scaling):
    return layer_norm(residual) * (1.0 + scaling) + offset


def gelu_tanh(inner_sum):
    return jax.nn.gelu(inner_sum, approximate=True)


def as_float(member):
    return member.astype(jnp.float32)


def project(inputs, weight):
    return jnp.dot(inputs, weight, preferred_element_type=jnp.float32)


def weight_grad(inputs, gradients):
    left_rows = inputs.reshape(-1, inputs.shape[-1])
    right_rows = gradients.reshape(-1, gradients.shape[-1])
    return lax.dot_general(
        left_rows, right_rows, (((0,), (0,)), ((), ())), preferred_element_type=jnp.float32
    )


def input_grad(gradients, weight):
    return lax.dot_general(
        gradients,
        weight,
        (((gradients.ndim - 1,), (1,)), ((), ())),
        preferred_element_type=jnp.float32,
    )


def column_sum(gradients):
    return jnp.sum(gradients.astype(jnp.float32).reshape(-1, gradients.shape[-1]), axis=0)


def index_bits():
    return lax.axis_size("sp").bit_length() - 1


def after(values, earlier):
    if not earlier:
        return values
    return lax.optimization_barrier((values, tuple(earlier)))[0]


def in_turn(links, key, values, exchange):
    last = links.get(key)
    result = exchange(values if last is None else after(values, [last]))
    links[key] = result
    return result


def swap_sp(values, bit, links):
    size = lax.axis_size("sp")
    pairs = [(i, i ^ (1 << bit)) for i in range(size)]
    return in_turn(links, min(bit, 2), values, lambda v: lax.ppermute(v, "sp", pairs))


def swap_seq(values, links, key="seq"):
    return in_turn(links, key, values, lambda v: lax.ppermute(v, "seq", [(0, 1), (1, 0)]))


def gather_kernel(rounds, n_in, n_out, *refs):
    shards, outs = refs[:n_in], refs[n_in : n_in + n_out]
    local_sem, send_sem, recv_sem, small_local, small_send, small_recv = refs[n_in + n_out :]
    me = lax.axis_index("sp")
    plane = lax.axis_index("seq")
    count = index_bits()
    place = [(me // (1 << (count - 1 - d))) % 2 for d in range(count)]

    def flip(bit):
        mine = (me // (1 << bit)) % 2
        return (plane, me + (1 << bit) * (1 - 2 * mine))

    across = (1 - plane, me)
    partners = [flip(bit) for bit in range(count)] + [across]
    barrier = pltpu.get_barrier_semaphore()
    for partner in partners:
        pl.semaphore_signal(
            barrier, inc=1, device_id=partner, device_id_type=pl.DeviceIdType.MESH
        )
    pl.semaphore_wait(barrier, len(partners))

    def part(ref, lead, piece):
        weight, rows, columns = piece
        if rows is None:
            return ref.at[(*lead, slice(None), pl.ds(*columns))]
        half, first, size = rows
        return ref.at[(*lead, half, pl.ds(first, size), slice(None))]

    def stage_places(stage):
        return tuple(
            slice(None) if d < stage else place[d] for d in range(count)
        )

    for own_half in (0, 1):

        @pl.when(plane == own_half)
        def _():
            started = []

            def send(number, stage, slot, source, target, partner):
                copy = pltpu.make_async_remote_copy(
                    src_ref=source,
                    dst_ref=target,
                    send_sem=send_sem.at[number, stage, slot],
                    recv_sem=recv_sem.at[number, stage, slot],
                    device_id=partner,
                    device_id_type=pl.DeviceIdType.MESH,
                )
                copy.start()
                return copy

            def own(chunk):
                return chunk[own_half]

            def other(chunk):
                return chunk[1 - own_half]

            def step(number, stage):
                (first, second), late = rounds[number]
                lead = stage_places(min(stage, count - 2))
                four = [piece for chunk in (first, second) for piece in (own(chunk), other(chunk))]
                if late and stage < count:
                    partner = [flip(1), across, *[flip(bit) for bit in range(count - 1, 1, -1)]][stage]
                    moves = [(piece, partner) for piece in (four if stage > 1 else four[::2])]
                    lead = tuple(
                        slice(None) if d < stage - 2 or (d == count - 2 and stage) else place[d]
                        for d in range(count)
                    )
                elif stage < count - 2:
                    moves = [(own(first), flip(count - 1 - stage)), (own(second), flip(count - 1 - stage))]
                elif stage == count - 2:
                    moves = [(own(first), flip(1)), (own(second), across)]
                elif stage == count - 1:
                    moves = [
                        (own(first), across),
                        (own(second), flip(1)),
                        (other(second), flip(1)),
                    ]
                else:
                    moves = [(piece, flip(0)) for piece in four]
                copies = []
                for slot, (piece, partner) in enumerate(moves):
                    places = lead
                    if not late and stage == count - 1 and partner is across or stage == count:
                        places = stage_places(count - 1)
                    target = part(outs[piece[0]], places, piece)
                    source = target
                    if stage == 0:
                        source = part(shards[piece[0]], (), piece)
                    copies.append(send(number, stage, slot, source, target, partner))
                return copies

            def small_step(stage):
                target = outs[-1].at[stage_places(stage)]
                copy = pltpu.make_async_remote_copy(
                    src_ref=target if stage else shards[-1],
                    dst_ref=target,
                    send_sem=small_send.at[stage],
                    recv_sem=small_recv.at[stage],
                    device_id=flip(count - 1 - stage),
                    device_id_type=pl.DeviceIdType.MESH,
                )
                copy.start()
                return copy

            copies = {}
            small = [small_step(0)]
            local = [
                pltpu.make_async_copy(shards[-1], outs[-1].at[stage_places(0)], small_local)
            ]
            local[0].start()
            for number, (pair, late) in enumerate(rounds):
                for slot, chunk in enumerate(pair):
                    piece = own(chunk)
                    copy = pltpu.make_async_copy(
                        part(shards[piece[0]], (), piece),
                        part(outs[piece[0]], stage_places(0), piece),
                        local_sem.at[number, slot],
                    )
                    copy.start()
                    local.append(copy)
            lags = {
                False: [*range(count), count + 1],
                True: [*range(count - 1), count, count + 2],
            }
            for time in range(len(rounds) + count + 2):
                if time == 1:
                    for copy in local:
                        copy.wait()
                if 0 < time < count:
                    small[-1].wait_recv()
                    small.append(small_step(time))
                for stage in range(count + 1):
                    for number, (_, late) in enumerate(rounds):
                        if number != time - lags[late][stage]:
                            continue
                        if stage:
                            for copy in copies[number, stage - 1]:
                                copy.wait_recv()
                        copies[number, stage] = step(number, stage)
            small[-1].wait_recv()
            for copy in small:
                copy.wait_send()
            for number in range(len(rounds)):
                for copy in copies[number, count]:
                    copy.wait_recv()
                for stage in range(count + 1):
                    for copy in copies[number, stage]:
                        copy.wait_send()


def gather_weights(shards, rounds, collective_id):
    size = lax.axis_size("sp")
    lead = (2,) * index_bits()
    shapes = [lead + shard.shape for shard in shards]
    total = sum(2 * math.prod(shape) for shape in shapes)
    stages = index_bits() + 1
    placed = pl.pallas_call(
        functools.partial(gather_kernel, rounds, len(shards), len(shards)),
        out_shape=[jax.ShapeDtypeStruct(shape, jnp.bfloat16) for shape in shapes],
        in_specs=[pl.BlockSpec(memory_space=pltpu.VMEM)] * len(shards),
        out_specs=[pl.BlockSpec(memory_space=pl.ANY)] * len(shards),
        scratch_shapes=[
            pltpu.SemaphoreType.DMA((len(rounds), 2)),
            pltpu.SemaphoreType.DMA((len(rounds), stages, 4)),
            pltpu.SemaphoreType.DMA((len(rounds), stages, 4)),
            pltpu.SemaphoreType.DMA,
            pltpu.SemaphoreType.DMA((index_bits(),)),
            pltpu.SemaphoreType.DMA((index_bits(),)),
        ],
        compiler_params=pltpu.CompilerParams(
            collective_id=collective_id, has_side_effects=True, vmem_limit_bytes=32 << 20
        ),
        cost_estimate=pl.CostEstimate(flops=0, bytes_accessed=total, transcendentals=0),
    )(*shards)
    *large, small = placed
    full = [member.reshape(size * math.prod(member.shape[index_bits() : -1]), -1) for member in large]
    small = jnp.swapaxes(small.reshape(size, *small.shape[-2:]), 0, 1)
    return full + [small.reshape(small.shape[0], -1)]


def columns_round(*quarters, late=False):
    pieces = [(weight, None, (first, width)) for weight, first, width in quarters]
    return ((pieces[0], pieces[2]), (pieces[1], pieces[3])), late


def rows_round(weight, rows):
    cut = rows // 32 * 16 + (rows // 16 % 2) * 16
    return (
        ((weight, (0, 0, cut), None), (weight, (1, 0, cut), None)),
        ((weight, (0, cut, rows - cut), None), (weight, (1, cut, rows - cut), None)),
    ), False


def gather_all(tall, wide, small, rounds_of, collective_id):
    if wide[0].shape[0] % 8 or lax.axis_size("seq") != 2:
        full = [lax.all_gather(shard, "sp", axis=0, tiled=True) for shard in wide + tall]
        return full + [lax.all_gather(small, "sp", axis=1, tiled=True)]
    shards = list(wide) + [
        shard.reshape(2, shard.shape[0] // 2, shard.shape[1]) for shard in tall
    ]
    shards.append(small)
    return gather_weights(shards, rounds_of(tall[0].shape[0] // 2), collective_id)


def pick_half(first, second):
    return jnp.where(lax.axis_index("seq") == 0, first, second)


def low_sum(*members):
    total = members[0].astype(jnp.float32)
    for member in members[1:]:
        total = total + member.astype(jnp.float32)
    return total.astype(jnp.bfloat16)


def pick(values, index, axis):
    return lax.dynamic_index_in_dim(values, index, axis, keepdims=False)


def split_blocks(values, bit_value):
    paired = values.reshape(values.shape[0] // 2, 2, *values.shape[1:])
    return pick(paired, 1 - bit_value, 1), pick(paired, bit_value, 1)


def scatter_grad(inputs, gradients, by_rows, seq_first, links):
    size = lax.axis_size("sp")
    me = lax.axis_index("sp")
    plane = lax.axis_index("seq")
    bits = [(me // (1 << b)) % 2 for b in range(index_bits())]
    left = inputs.reshape(-1, inputs.shape[-1])
    right = gradients.reshape(-1, gradients.shape[-1])
    depth = left.shape[1]
    columns = right.shape[1]
    rows = depth // size
    half = (rows if by_rows else columns) // 2
    if not by_rows:
        padded = -(-half // 128) * 128
        fill = ((0, 0), (0, padded - half))
        right = jnp.concatenate(
            [
                jnp.pad(pick_half(right[:, :half], right[:, half:]), fill),
                jnp.pad(pick_half(right[:, half:], right[:, :half]), fill),
            ],
            axis=1,
        )
    total = lax.dot_general(
        left, right, (((0,), (0,)), ((), ())), preferred_element_type=jnp.float32
    ).astype(jnp.bfloat16)
    if by_rows:
        total = total.reshape(size, 2, half, columns)
    else:
        total = total.reshape(size, rows, 2 * padded)
    sent, kept = split_blocks(total, bits[0])
    came = swap_sp(sent, 0, links)
    if by_rows:
        own, other = [
            (pick(kept, which, 1), pick(came, which, 1)) for which in (plane, 1 - plane)
        ]
    else:
        own = (kept[:, :, :padded], came[:, :, :padded])
        other = (kept[:, :, padded:], came[:, :, padded:])
    if seq_first:
        current = (*own, swap_seq(low_sum(*other), links))
        current = halve(current, bits[1], 1, links)
    else:
        own = halve(own, bits[1], 1, links)
        other = halve(other, bits[1], 1, links)
        current = (*own, swap_seq(low_sum(*other), links))
    for bit in range(2, index_bits()):
        current = halve(current, bits[bit], bit, links)
    mine = low_sum(*current)[0]
    theirs = swap_seq(mine, links, "last")
    if not by_rows:
        mine, theirs = mine[:, :half], theirs[:, :half]
    axis = 0 if by_rows else 1
    return pick_half(
        jnp.concatenate([mine, theirs], axis=axis), jnp.concatenate([theirs, mine], axis=axis)
    ).astype(jnp.float32)


def scatter_kernel(pairs, full_pairs, shrink_pairs, late_pairs, sources, n_in, *refs):
    factors, small = refs[:n_in], refs[n_in]
    refs = refs[n_in + 1 :]
    came, out, small_out = refs[:5], refs[5], refs[6]
    scratch = refs[7:]
    left_in, right_in, product, core_both, loaded = scratch[:5]
    sends, keeps = scratch[5:10], scratch[10:14]
    in_sem, load_sem, out_sem, core_send_sem, core_recv_sem, send_sem, recv_sem = scratch[14:21]
    small_sum, small_came, small_send, small_recv = scratch[21:]
    core_own, core_send = core_both.at[0], core_both.at[1]
    me = lax.axis_index("sp")
    plane = lax.axis_index("seq")

    def bit_of(bit):
        return (me // (1 << bit)) % 2

    def flip(bit):
        return (plane, me + (1 << bit) * (1 - 2 * bit_of(bit)))

    across = (1 - plane, me)
    core = bit_of(0)
    rows = out.shape[3]
    barrier = pltpu.get_barrier_semaphore()
    partners = [flip(bit) for bit in range(4)] + [across]
    for partner in partners:
        pl.semaphore_signal(
            barrier, inc=1, device_id=partner, device_id_type=pl.DeviceIdType.MESH
        )
    pl.semaphore_wait(barrier, len(partners))

    def among(pair, chosen):
        return sum([1 // (1 + (pair - p) * (pair - p)) for p in chosen], 0 * pair)

    def remote(source, target, send, recv, partner):
        return pltpu.make_async_remote_copy(
            src_ref=source,
            dst_ref=target,
            send_sem=send,
            recv_sem=recv,
            device_id=partner,
            device_id_type=pl.DeviceIdType.MESH,
        )

    def half_of(side):
        return plane if side == 0 else 1 - plane

    def core_copy(pair, chunk, side):
        number = 2 * chunk + side
        return remote(
            core_send.at[number],
            came[0].at[pair, number],
            core_send_sem.at[number],
            core_recv_sem.at[pair, number],
            flip(0),
        )

    def is_late(pair):
        return among(pair, late_pairs)

    def is_second(pair, chunk):
        return 0 * pair + 1 if chunk == 1 else among(pair, (pairs - 1,))

    def stage_partner(stage, chunk, pair):
        second = is_second(pair, chunk)
        if stage < 3:
            usual = (across, flip(1)) if stage == 1 else (flip(1), across)
            usual = tuple(a + second * (b - a) for a, b in zip(*usual))
        else:
            usual = flip(2) if stage == 3 else flip(3) if stage == 4 else across
        swapped = (flip(2), flip(3), across, flip(1), across)[stage - 1]
        late = is_late(pair)
        return tuple(a + late * (b - a) for a, b in zip(usual, swapped))

    def stage_copy(stage, pair, chunk):
        source = sends[stage - 1].at[pair % 2, chunk]
        target = out.at[pair, chunk, plane] if stage == 5 else came[stage].at[pair, chunk]
        return remote(
            source,
            target,
            send_sem.at[stage - 1, pair % 2, chunk],
            recv_sem.at[stage - 1, pair, chunk],
            stage_partner(stage, chunk, pair),
        )

    def out_copy(pair, chunk):
        return pltpu.make_async_copy(
            sends[4].at[pair % 2, chunk], out.at[pair, chunk, plane], out_sem.at[pair % 2, chunk]
        )

    def has(pair, chunk):
        return pair < (pairs if chunk == 0 else full_pairs)

    width = out.shape[4]

    def start_inputs(q, slot):
        for number, source in enumerate(sources):

            @pl.when(q == number)
            def _():
                for place, target, k in ((source[0], left_in, 0), (source[1], right_in, 1)):
                    pltpu.make_async_copy(
                        factors[place[0]].at[:, pl.ds(place[1], width)],
                        target.at[slot],
                        in_sem.at[slot, k],
                    ).start()

    def wait_inputs(slot):
        for target, k in ((left_in, 0), (right_in, 1)):
            pltpu.make_async_copy(
                factors[0].at[:, pl.ds(0, width)], target.at[slot], in_sem.at[slot, k]
            ).wait()

    def products(pair):
        start_inputs(4 * pair, 0)
        for chunk in (0, 1):

            @pl.when((pair > 0) & has(pair - 1, chunk))
            def _():
                for side in (0, 1):
                    core_copy(pair - 1, chunk, side).wait_send()

        last = pair // full_pairs
        shrink = among(pair, shrink_pairs)

        def one(j, carry):
            slot = j % 2

            @pl.when(j + 1 < 4 - 2 * last)
            def _():
                start_inputs(4 * pair + j + 1, 1 - slot)

            wait_inputs(slot)
            product[...] = lax.dot_general(
                left_in[slot],
                right_in[slot],
                (((0,), (0,)), ((), ())),
                preferred_element_type=jnp.float32,
            )

            def store(i, carry):
                owner = shrink * (4 * j + i // 4) + (1 - shrink) * i
                quarter = shrink * (i % 4) + (1 - shrink) * j
                number = quarter // 2 * 2 + (quarter % 2 + plane) % 2
                first = pl.multiple_of(i * rows, 8)
                core_both[(owner + core) % 2, number, owner // 2] = product[
                    pl.ds(first, rows), :
                ].astype(jnp.bfloat16)
                return carry

            lax.fori_loop(0, 16, store, 0)

            @pl.when((j == 1) & (shrink == 0))
            def _():
                for side in (0, 1):
                    core_copy(pair, 0, side).start()

            return carry

        lax.fori_loop(0, 4 - 2 * last, one, 0)

        @pl.when(shrink == 1)
        def _():
            for side in (0, 1):
                core_copy(pair, 0, side).start()

        @pl.when(has(pair, 1))
        def _():
            for side in (0, 1):
                core_copy(pair, 1, side).start()

    def add(a, b):
        return (a.astype(jnp.float32) + b.astype(jnp.float32)).astype(jnp.bfloat16)

    def load(source, slot, blocks):
        return pltpu.make_async_copy(
            source, loaded.at[slot, pl.ds(0, blocks)], load_sem.at[slot]
        )

    def free_send(stage, pair, chunk):
        @pl.when(pair >= 2)
        def _():
            stage_copy(stage, pair, chunk).wait_send()

    def add_core(pair):
        slot = pair % 2
        x = bit_of(1)
        for chunk in (0, 1):

            @pl.when(has(pair, chunk))
            def _():
                for side in (1, 0):
                    core_copy(pair, chunk, side).wait_recv()
                    load(came[0].at[pair, 2 * chunk + side], side, 8).start()
                free_send(1, pair, chunk)
                for side in (1, 0):
                    number = 2 * chunk + side
                    load(came[0].at[pair, number], side, 8).wait()
                    late = is_late(pair)

                    def both():
                        target = sends[0] if side == 1 else keeps[0]

                        def one(block, carry):
                            target[slot, chunk, block] = add(
                                core_own[number, block], loaded[side, block]
                            )
                            return carry

                        lax.fori_loop(0, 8, one, 0)
                        if side == 1:
                            stage_copy(1, pair, chunk).start()

                    def split():
                        def one(i, carry):
                            usual = 2 * i
                            other = 4 * (i // 2) + i % 2
                            low = bit_of(2)
                            for target, a, b in (
                                (sends[0], usual + 1 - x, other + 2 * (1 - low)),
                                (keeps[0], usual + x, other + 2 * low),
                            ):
                                block = a + late * (b - a)
                                target[slot, chunk, 4 * side + i] = add(
                                    core_own[number, block], loaded[side, block]
                                )
                            return carry

                        lax.fori_loop(0, 4, one, 0)
                        if side == 0:
                            stage_copy(1, pair, chunk).start()

                    if chunk == 0:
                        apart = late + is_second(pair, chunk)
                        pl.when(apart == 0)(both)
                        pl.when(apart == 1)(split)
                    else:
                        split()

    def add_stage(stage, pair):
        slot = pair % 2
        blocks = 16 >> stage
        for chunk in (0, 1):

            @pl.when(has(pair, chunk))
            def _():
                stage_copy(stage, pair, chunk).wait_recv()
                load(came[stage].at[pair, chunk], chunk, blocks).start()
        for chunk in (0, 1):

            @pl.when(has(pair, chunk))
            def _():
                free_send(stage + 1, pair, chunk)
                if stage == 4:

                    @pl.when(pair >= 2)
                    def _():
                        out_copy(pair, chunk).wait()

                load(came[stage].at[pair, chunk], chunk, blocks).wait()
                old, new = keeps[stage - 1], keeps[stage] if stage < 4 else None

                def one(i, carry):
                    late = is_late(pair)
                    x, low, high = bit_of(1), bit_of(2), bit_of(3)
                    if stage == 1:
                        second = is_second(pair, chunk)
                        a = (
                            2 * i + 1 - x + second * (3 + x - i),
                            2 * i + x + second * (-x - i),
                        )
                        start = 4 * (i // 2) + i % 2
                        b = (start + 2 * (1 - high), start + 2 * high)
                    elif stage == 2:
                        a = (2 * i + 1 - low, 2 * i + low)
                        b = (2 + i, i)
                    else:
                        a = (1 - high, high)
                        b = (1 - x, x)
                    gone, kept = [p + late * (q - p) for p, q in zip(a, b)]
                    sends[stage][slot, chunk, i] = add(
                        old[slot, chunk, gone], loaded[chunk, gone]
                    )
                    new[slot, chunk, i] = add(old[slot, chunk, kept], loaded[chunk, kept])
                    return carry

                if stage < 4:
                    lax.fori_loop(0, blocks // 2, one, 0)
                else:
                    sends[4][slot, chunk] = add(old[slot, chunk, 0], loaded[chunk, 0])
                    out_copy(pair, chunk).start()
                stage_copy(stage + 1, pair, chunk).start()

    def small_copy(stage):
        return remote(
            small_sum.at[stage],
            small_came.at[stage],
            small_send.at[stage],
            small_recv.at[stage],
            partners[stage],
        )

    small_sum[0] = small[...]
    small_copy(0).start()

    def turn(time, carry):
        for stage in range(len(partners)):

            @pl.when(time == stage)
            def _():
                small_copy(stage).wait_recv()
                total = small_sum[stage] + small_came[stage]
                if stage + 1 < len(partners):
                    small_sum[stage + 1] = total
                    small_copy(stage + 1).start()
                else:
                    small_out[...] = total

        for lag, work in (
            (1, add_core),
            (2, functools.partial(add_stage, 1)),
            (3, functools.partial(add_stage, 2)),
            (4, functools.partial(add_stage, 3)),
            (5, functools.partial(add_stage, 4)),
            (0, products),
        ):
            pair = time - lag

            @pl.when((pair >= 0) & (pair < pairs))
            def _():
                work(pair)

        return carry

    lax.fori_loop(0, pairs + 5, turn, 0)
    for stage in range(len(partners)):
        small_copy(stage).wait_send()
    for chunk in (0, 1):
        mine = pairs if chunk == 0 else full_pairs
        if mine == pairs:
            for side in (0, 1):
                core_copy(mine - 1, chunk, side).wait_send()
        for pair in range(max(mine - 2, 0), mine):
            out_copy(pair, chunk).wait()
            for stage in range(1, 6):
                stage_copy(stage, pair, chunk).wait_send()
        for pair in range(mine):
            stage_copy(5, pair, chunk).wait_recv()


def scatter_products(
    factors, sources, small, pairs, full_pairs, shrink_pairs, rows, width, collective_id
):
    tokens = factors[0].shape[0]
    depth = 16 * rows
    low = jnp.bfloat16

    def blocks(*lead):
        return jax.ShapeDtypeStruct((*lead, rows, width), low)

    hbm = [
        blocks(pairs, 4, 8),
        blocks(pairs, 2, 8),
        blocks(pairs, 2, 4),
        blocks(pairs, 2, 2),
        blocks(pairs, 2, 1),
        blocks(pairs, 2, 2),
    ]
    any_space = pl.BlockSpec(memory_space=pl.ANY)

    def vmem(*lead):
        return pltpu.VMEM((*lead, rows, width), low)

    dma = pltpu.SemaphoreType.DMA
    whole = pl.BlockSpec(memory_space=pltpu.VMEM)
    *_, out, total = pl.pallas_call(
        functools.partial(
            scatter_kernel, pairs, full_pairs, shrink_pairs, (), sources, len(factors)
        ),
        out_shape=hbm + [jax.ShapeDtypeStruct(small.shape, small.dtype)],
        in_specs=[any_space] * len(factors) + [whole],
        out_specs=[any_space] * len(hbm) + [whole],
        scratch_shapes=[
            pltpu.VMEM((2, tokens, width), low),
            pltpu.VMEM((2, tokens, width), low),
            pltpu.VMEM((depth, width), jnp.float32),
            vmem(2, 4, 8),
            vmem(2, 8),
            vmem(2, 2, 8),
            vmem(2, 2, 4),
            vmem(2, 2, 2),
            vmem(2, 2, 1),
            vmem(2, 2),
            vmem(2, 2, 8),
            vmem(2, 2, 4),
            vmem(2, 2, 2),
            vmem(2, 2, 1),
            dma((2, 2)),
            dma((2,)),
            dma((2, 2)),
            dma((4,)),
            dma((pairs, 4)),
            dma((5, 2, 2)),
            dma((5, pairs, 2)),
            pltpu.VMEM((5, *small.shape), small.dtype),
            pltpu.VMEM((5, *small.shape), small.dtype),
            dma((5,)),
            dma((5,)),
        ],
        compiler_params=pltpu.CompilerParams(
            collective_id=collective_id, has_side_effects=True, vmem_limit_bytes=58 << 20
        ),
        cost_estimate=pl.CostEstimate(
            flops=2 * len(sources) * depth * tokens * width,
            bytes_accessed=16 * len(sources) * depth * width,
            transcendentals=0,
        ),
    )(*factors, small)
    return out, total


BESIDE = ((1, "shrink"), )


def token_rows(gradients):
    return gradients.reshape(-1, gradients.shape[-1])


def scatter_all(terms, small):
    size = lax.axis_size("sp")
    if size != 16 or lax.axis_size("seq") != 2:
        links = {}
        flags = [(False, False), (True, True), (False, False), (False, True)]
        blocks = [
            [scatter_grad(*pair, *flag, links) for pair, flag in zip(block, flags)]
            for block in terms[:2]
        ]
        last = [scatter_grad(*pair, False, False, links) for pair in terms[2]]
        return blocks[0], blocks[1], last, lax.psum(small, ("seq", "sp"))
    factors, sources = [], []

    def add_factors(pair):
        factors.extend(token_rows(member) for member in pair)
        return len(factors) - 2, len(factors) - 1

    names = ("expand", "shrink", "qkv", "out")
    results = [dict(), dict()]
    shrink_pairs, homes = [], []

    def beside(block, name):
        left, right = [token_rows(member) for member in terms[block][names.index(name)]]
        product = lax.dot_general(
            left, right, (((0,), (0,)), ((), ())), preferred_element_type=jnp.float32
        ).astype(jnp.bfloat16)
        return lax.psum_scatter(product, "sp", scatter_dimension=0, tiled=True)

    early = [beside(block, name) for block, name in BESIDE]
    for block in (1, 0):
        expand, shrink, qkv, out = terms[block]
        if (block, "shrink") not in BESIDE:
            shrink_pairs.append(len(homes))
            homes.append((block, "shrink"))
            left, right = add_factors(shrink)
            sources += [((left, j * D), (right, 0)) for j in range(4)]
        if (block, "expand") not in BESIDE:
            homes.append((block, "expand"))
            left, right = add_factors(expand)
            sources += [((left, 0), (right, j * D)) for j in range(4)]
        homes.append((block, "qkv"))
        left, right = add_factors(qkv)
        sources += [((left, 0), (right, j * D)) for j in range(3)]
        left, right = add_factors(out)
        sources.append(((left, 0), (right, 0)))
    for pair in terms[2]:
        left, right = add_factors(pair)
        sources.append(((left, 0), (right, 0)))
    pairs = len(homes) + 1
    if early:
        small, first = lax.optimization_barrier((small, early[0]))
        early[0] = first
    done, total = scatter_products(
        factors, sources, small, pairs, pairs - 1, tuple(shrink_pairs), D // size, D, 1
    )
    done = done.astype(jnp.float32)

    def quarter(pair, k):
        return done[pair, k // 2, k % 2]

    for pair, (block, name) in enumerate(homes):
        parts = [quarter(pair, k) for k in range(4)]
        if name == "qkv":
            results[block]["out"] = parts.pop()
        results[block][name] = jnp.concatenate(parts, axis=0 if name == "shrink" else 1)
    for (block, name), part in zip(BESIDE, early):
        results[block][name] = sum_seq(part)
    last = [quarter(pairs - 1, k) for k in range(2)]
    ordered = [[found[name] for name in names] for found in results]
    return ordered[0], ordered[1], last, total


def halve(members, bit_value, bit, links):
    parts = [split_blocks(member, bit_value) for member in members]
    sent = low_sum(*[part[0] for part in parts])
    return (low_sum(*[part[1] for part in parts]), swap_sp(sent, bit, links))


def sum_seq(values):
    mine = values.astype(jnp.bfloat16)
    return mine.astype(jnp.float32) + swap_seq(mine, {}).astype(jnp.float32)


def triple_bias(query_bias, value_bias):
    head_query = query_bias.reshape(HEADS, 1, HEAD_DIM)
    head_value = value_bias.reshape(HEADS, 1, HEAD_DIM)
    return jnp.concatenate([head_query, jnp.zeros_like(head_query), head_value], axis=1).reshape(
        3 * D
    )


def pair_bias(value_bias):
    head_value = value_bias.reshape(HEADS, 1, HEAD_DIM)
    return jnp.concatenate([jnp.zeros_like(head_value), head_value], axis=1).reshape(2 * D)


def triple_bias_grad(totals):
    split_rows = totals.reshape(HEADS, 3, HEAD_DIM)
    return (split_rows[:, 0].reshape(D), split_rows[:, 2].reshape(D))


def frame_modulation(segment_ids, timesteps):
    onehot = (segment_ids[:, :, None] == jnp.arange(CLIPS)[None, None, :]).astype(jnp.float32)
    features = time_features(timesteps)
    return jnp.einsum("sfc,scz->sfz", onehot, features, precision=lax.Precision.HIGHEST)


def block_pieces(table_rows, frame_mod):
    modulation = table_rows[None, None] + frame_mod
    return [modulation[:, :, number][:, :, None, :] for number in range(6)]


def gated_back(grad_out, gating, branch):
    branch_grad = (gating * grad_out).astype(jnp.bfloat16)
    gate_grad = jnp.sum(grad_out * branch, axis=2, keepdims=True)
    return (branch_grad, gate_grad)


def split_kernel(width, source, target):
    for head in range(HEADS):
        target[:, head] = source[:, :, head * width : (head + 1) * width]


def merge_kernel(width, source, target):
    for head in range(HEADS):
        target[:, :, head * width : (head + 1) * width] = source[:, head]


def move_heads(kernel, values, width, shape):
    step = 8

    def block(dims):
        return pl.BlockSpec((step, *dims[1:]), lambda i: (i, *[0] * (len(dims) - 1)))

    return pl.pallas_call(
        functools.partial(kernel, width),
        grid=(shape[0] // step,),
        in_specs=[block(values.shape)],
        out_specs=block(shape),
        out_shape=jax.ShapeDtypeStruct(shape, values.dtype),
        compiler_params=pltpu.CompilerParams(vmem_limit_bytes=32 << 20),
        cost_estimate=pl.CostEstimate(
            flops=0, bytes_accessed=4 * values.size, transcendentals=0
        ),
    )(values)


def to_pairs(values):
    groups, frames, patches, columns = values.shape
    width = columns // HEADS
    flat = values.reshape(groups * frames, patches, columns)
    shape = (groups * frames, HEADS, patches, width)
    return move_heads(split_kernel, flat, width, shape).reshape(
        lax.axis_size("sp"), -1, patches, width
    )


def from_pairs(values, groups, frames):
    devices, pair_count, patches, width = values.shape
    pairs = values.reshape(groups * frames, HEADS, patches, width)
    shape = (groups * frames, patches, HEADS * width)
    return move_heads(merge_kernel, pairs, width, shape)


def pair_scores(triple):
    queries = triple[..., :HEAD_DIM]
    key_rows = triple[..., HEAD_DIM : 2 * HEAD_DIM]
    scores = jnp.einsum(
        "zkqe,zkre->zkqr", queries, key_rows, preferred_element_type=jnp.float32
    ) * HEAD_DIM ** (-0.5)
    return jax.nn.softmax(scores, axis=-1)


def attend_pairs(triple):
    attention = pair_scores(triple).astype(jnp.bfloat16)
    mixture = jnp.einsum(
        "zkqr,zkre->zkqe",
        attention,
        triple[..., 2 * HEAD_DIM :],
        preferred_element_type=jnp.float32,
    ).astype(jnp.bfloat16)
    return lax.all_to_all(mixture, "sp", split_axis=2, concat_axis=0, tiled=True)


def pair_backward(members):
    triple, out_grad = members
    queries = triple[..., :HEAD_DIM]
    key_rows = triple[..., HEAD_DIM : 2 * HEAD_DIM]
    value_rows = triple[..., 2 * HEAD_DIM :]
    attention = pair_scores(triple)
    rounded = attention.astype(jnp.bfloat16)
    prob_grad = jnp.einsum(
        "zkqe,zkre->zkqr", out_grad, value_rows, preferred_element_type=jnp.float32
    )
    centre = jnp.sum(prob_grad * attention, axis=-1, keepdims=True)
    score_grad = (attention * (prob_grad - centre)).astype(jnp.bfloat16)
    scaling = HEAD_DIM ** (-0.5)
    query_grad = (
        jnp.einsum("zkqr,zkre->zkqe", score_grad, key_rows, preferred_element_type=jnp.float32)
        * scaling
    )
    key_grad = (
        jnp.einsum("zkqr,zkqe->zkre", score_grad, queries, preferred_element_type=jnp.float32)
        * scaling
    )
    value_grad = jnp.einsum(
        "zkqr,zkqe->zkre", rounded, out_grad, preferred_element_type=jnp.float32
    )
    gradients = jnp.concatenate([query_grad, key_grad, value_grad], axis=-1).astype(jnp.bfloat16)
    return lax.all_to_all(gradients, "sp", split_axis=2, concat_axis=0, tiled=True)


def pair_attention(triple):
    groups, frames, patches = triple.shape[:3]
    pairs = lax.all_to_all(to_pairs(triple), "sp", split_axis=0, concat_axis=2, tiled=True)
    exchanged = attend_pairs(pairs)
    return from_pairs(exchanged, groups, frames).reshape(groups, frames, patches, D), pairs


def pair_attention_back(pairs, mixture_grad):
    groups, frames, patches = mixture_grad.shape[:3]
    returned = pair_backward(
        (
            pairs,
            lax.all_to_all(to_pairs(mixture_grad), "sp", split_axis=0, concat_axis=2, tiled=True),
        )
    )
    return from_pairs(returned, groups, frames).reshape(groups, frames, patches, 3 * D)


def feed_forward(residual, offset, scaling, gating, expand, shrink, vectors, start_row):
    hidden = modulate(residual, offset, scaling).astype(jnp.bfloat16)
    inner_sum = project(hidden, expand) + vectors[start_row : start_row + 4].reshape(FF)
    active = gelu_tanh(inner_sum).astype(jnp.bfloat16)
    branch = project(active, shrink) + vectors[3]
    return ((hidden, inner_sum, active, branch), residual + gating * branch)


def feed_backward(grad_out, residual, offset, scaling, gating, stored, expand, shrink):
    hidden, inner_sum, active, branch = stored
    branch_grad, gate_grad = gated_back(grad_out, gating, branch)
    shrink_grad = (active, branch_grad)
    active_grad = input_grad(branch_grad, shrink)
    gelu_value, gelu_back = jax.vjp(gelu_tanh, inner_sum)
    inner_grad = gelu_back(active_grad)[0].astype(jnp.bfloat16)
    expand_grad = (hidden, inner_grad)
    hidden_grad = input_grad(inner_grad, expand)
    norm_value, norm_back = jax.vjp(modulate, residual, offset, scaling)
    residual_grad, offset_grad, scaling_grad = norm_back(hidden_grad)
    return (
        grad_out + residual_grad,
        [offset_grad, scaling_grad, gate_grad],
        (expand_grad, shrink_grad, column_sum(inner_grad), column_sum(branch_grad)),
    )


def table_sums(members):
    return jnp.stack([jnp.sum(member, axis=(0, 1, 2)) for member in members])


def spatial_forward(residual, weights, frame_mod):
    qkv_weight, out_weight, expand, shrink, vectors = weights
    vectors_f = as_float(vectors)
    pieces = block_pieces(vectors_f[4:10], frame_mod)
    hidden = modulate(residual, pieces[0], pieces[1]).astype(jnp.bfloat16)
    triple = (project(hidden, qkv_weight) + triple_bias(vectors_f[0], vectors_f[1])).astype(
        jnp.bfloat16
    )
    mixture, pairs = pair_attention(triple)
    branch = project(mixture, out_weight) + vectors_f[2]
    middle = residual + pieces[2] * branch
    stored_ffn, result = feed_forward(
        middle, pieces[3], pieces[4], pieces[5], expand, shrink, vectors_f, 10
    )
    return (result, (hidden, pairs, mixture, branch, middle, stored_ffn))


def spatial_backward(grad_out, residual, weights, frame_mod, stored):
    qkv_weight, out_weight, expand, shrink, vectors = weights
    pieces = block_pieces(as_float(vectors)[4:10], frame_mod)
    hidden, pairs, mixture, branch, middle, stored_ffn = stored
    middle_grad, ffn_table, ffn_grads = feed_backward(
        grad_out, middle, pieces[3], pieces[4], pieces[5], stored_ffn, expand, shrink
    )
    branch_grad, gate_grad = gated_back(middle_grad, pieces[2], branch)
    out_weight_grad = (mixture, branch_grad)
    out_bias = column_sum(branch_grad)
    mixture_grad = input_grad(branch_grad, out_weight).astype(jnp.bfloat16)
    triple_grad = pair_attention_back(pairs, mixture_grad)
    qkv_grad = (hidden, triple_grad)
    query_bias, value_bias = triple_bias_grad(column_sum(triple_grad))
    hidden_grad = input_grad(triple_grad, qkv_weight)
    norm_value, norm_back = jax.vjp(modulate, residual, pieces[0], pieces[1])
    residual_grad, offset_grad, scaling_grad = norm_back(hidden_grad)
    table_grad = table_sums([offset_grad, scaling_grad, gate_grad] + ffn_table)
    vector_grad = jnp.concatenate(
        [
            jnp.stack([query_bias, value_bias, out_bias, ffn_grads[3]]),
            table_grad,
            ffn_grads[2].reshape(4, D),
        ],
        axis=0,
    )
    return (
        middle_grad + residual_grad,
        (qkv_grad, out_weight_grad, ffn_grads[0], ffn_grads[1], vector_grad),
    )


def temporal_scores(triple, same_clip):
    scores = jnp.einsum(
        "sfphe,sgphe->sphfg",
        triple[..., :HEAD_DIM],
        triple[..., HEAD_DIM : 2 * HEAD_DIM],
        preferred_element_type=jnp.float32,
    ) * HEAD_DIM ** (-0.5)
    return jax.nn.softmax(jnp.where(same_clip, scores, masked_score), axis=-1)


def caption_scores(queries, keyval, allowed):
    scores = jnp.einsum(
        "sfphe,srhe->sfphr", queries, keyval[..., :HEAD_DIM], preferred_element_type=jnp.float32
    ) * HEAD_DIM ** (-0.5)
    return jax.nn.softmax(jnp.where(allowed, scores, masked_score), axis=-1)


def temporal_forward(residual, weights, frame_mod, same_clip, allowed, context):
    qkv_weight, out_weight, expand, shrink, query_weight, keyval_weight, cross_weight, vectors = (
        weights
    )
    vectors_f = as_float(vectors)
    pieces = block_pieces(vectors_f[8:14], frame_mod)
    groups, frames, patches = residual.shape[:3]
    hidden = modulate(residual, pieces[0], pieces[1]).astype(jnp.bfloat16)
    triple = (project(hidden, qkv_weight) + triple_bias(vectors_f[0], vectors_f[1])).astype(
        jnp.bfloat16
    )
    triple = triple.reshape(groups, frames, patches, HEADS, 3 * HEAD_DIM)
    attention = temporal_scores(triple, same_clip).astype(jnp.bfloat16)
    mixture = (
        jnp.einsum(
            "sphfg,sgphe->sfphe",
            attention,
            triple[..., 2 * HEAD_DIM :],
            preferred_element_type=jnp.float32,
        )
        .astype(jnp.bfloat16)
        .reshape(groups, frames, patches, D)
    )
    branch = project(mixture, out_weight) + vectors_f[2]
    middle = residual + pieces[2] * branch
    lowered = middle.astype(jnp.bfloat16)
    queries = (project(lowered, query_weight) + vectors_f[4]).astype(jnp.bfloat16)
    queries = queries.reshape(groups, frames, patches, HEADS, HEAD_DIM)
    keyval = (project(context, keyval_weight) + pair_bias(vectors_f[5])).astype(jnp.bfloat16)
    keyval = keyval.reshape(groups, -1, HEADS, 2 * HEAD_DIM)
    cross_probs = caption_scores(queries, keyval, allowed).astype(jnp.bfloat16)
    cross_mix = (
        jnp.einsum(
            "sfphr,srhe->sfphe",
            cross_probs,
            keyval[..., HEAD_DIM:],
            preferred_element_type=jnp.float32,
        )
        .astype(jnp.bfloat16)
        .reshape(groups, frames, patches, D)
    )
    crossed = middle + project(cross_mix, cross_weight) + vectors_f[6]
    stored_ffn, result = feed_forward(
        crossed, pieces[3], pieces[4], pieces[5], expand, shrink, vectors_f, 14
    )
    return (
        result,
        (
            hidden,
            triple,
            mixture,
            branch,
            middle,
            lowered,
            queries,
            keyval,
            cross_mix,
            crossed,
            stored_ffn,
        ),
    )


def temporal_backward(grad_out, residual, weights, frame_mod, same_clip, allowed, stored):
    qkv_weight, out_weight, expand, shrink, query_weight, keyval_weight, cross_weight, vectors = (
        weights
    )
    pieces = block_pieces(as_float(vectors)[8:14], frame_mod)
    (
        hidden,
        triple,
        mixture,
        branch,
        middle,
        lowered,
        queries,
        keyval,
        cross_mix,
        crossed,
        stored_ffn,
    ) = stored
    groups, frames, patches = residual.shape[:3]
    scaling = HEAD_DIM ** (-0.5)
    crossed_grad, ffn_table, ffn_grads = feed_backward(
        grad_out, crossed, pieces[3], pieces[4], pieces[5], stored_ffn, expand, shrink
    )
    cross_branch_grad = crossed_grad.astype(jnp.bfloat16)
    cross_weight_grad = (cross_mix, cross_branch_grad)
    cross_bias = column_sum(cross_branch_grad)
    mix_grad = input_grad(cross_branch_grad, cross_weight).astype(jnp.bfloat16)
    mix_grad = mix_grad.reshape(groups, frames, patches, HEADS, HEAD_DIM)
    cross_probs = caption_scores(queries, keyval, allowed)
    rounded = cross_probs.astype(jnp.bfloat16)
    prob_grad = jnp.einsum(
        "sfphe,srhe->sfphr", mix_grad, keyval[..., HEAD_DIM:], preferred_element_type=jnp.float32
    )
    centre = jnp.sum(prob_grad * cross_probs, axis=-1, keepdims=True)
    score_grad = (cross_probs * (prob_grad - centre)).astype(jnp.bfloat16)
    query_grad = (
        jnp.einsum(
            "sfphr,srhe->sfphe",
            score_grad,
            keyval[..., :HEAD_DIM],
            preferred_element_type=jnp.float32,
        )
        * scaling
    )
    query_grad = query_grad.astype(jnp.bfloat16).reshape(groups, frames, patches, D)
    key_grad = (
        jnp.einsum("sfphr,sfphe->srhe", score_grad, queries, preferred_element_type=jnp.float32)
        * scaling
    )
    value_grad = jnp.einsum(
        "sfphr,sfphe->srhe", rounded, mix_grad, preferred_element_type=jnp.float32
    )
    keyval_grad = jnp.concatenate([key_grad, value_grad], axis=-1).reshape(groups, -1, 2 * D)
    keyval_grad = lax.psum(keyval_grad.astype(jnp.bfloat16), "sp")
    query_weight_grad = (lowered, query_grad)
    cross_query_bias = column_sum(query_grad)
    middle_grad = crossed_grad + input_grad(query_grad, query_weight)
    branch_grad, gate_grad = gated_back(middle_grad, pieces[2], branch)
    out_weight_grad = (mixture, branch_grad)
    out_bias = column_sum(branch_grad)
    mixture_grad = input_grad(branch_grad, out_weight).astype(jnp.bfloat16)
    mixture_grad = mixture_grad.reshape(groups, frames, patches, HEADS, HEAD_DIM)
    attention = temporal_scores(triple, same_clip)
    rounded_t = attention.astype(jnp.bfloat16)
    prob_grad_t = jnp.einsum(
        "sfphe,sgphe->sphfg",
        mixture_grad,
        triple[..., 2 * HEAD_DIM :],
        preferred_element_type=jnp.float32,
    )
    centre_t = jnp.sum(prob_grad_t * attention, axis=-1, keepdims=True)
    score_grad_t = (attention * (prob_grad_t - centre_t)).astype(jnp.bfloat16)
    query_part = (
        jnp.einsum(
            "sphfg,sgphe->sfphe",
            score_grad_t,
            triple[..., HEAD_DIM : 2 * HEAD_DIM],
            preferred_element_type=jnp.float32,
        )
        * scaling
    )
    key_part = (
        jnp.einsum(
            "sphfg,sfphe->sgphe",
            score_grad_t,
            triple[..., :HEAD_DIM],
            preferred_element_type=jnp.float32,
        )
        * scaling
    )
    value_part = jnp.einsum(
        "sphfg,sfphe->sgphe", rounded_t, mixture_grad, preferred_element_type=jnp.float32
    )
    triple_grad = jnp.concatenate([query_part, key_part, value_part], axis=-1).astype(jnp.bfloat16)
    triple_grad = triple_grad.reshape(groups, frames, patches, 3 * D)
    qkv_grad = (hidden, triple_grad)
    query_bias, value_bias = triple_bias_grad(column_sum(triple_grad))
    hidden_grad = input_grad(triple_grad, qkv_weight)
    norm_value, norm_back = jax.vjp(modulate, residual, pieces[0], pieces[1])
    residual_grad, offset_grad, scaling_grad = norm_back(hidden_grad)
    table_grad = table_sums([offset_grad, scaling_grad, gate_grad] + ffn_table)
    zero_row = jnp.zeros((D,), jnp.float32)
    vector_grad = jnp.concatenate(
        [
            jnp.stack(
                [
                    query_bias,
                    value_bias,
                    out_bias,
                    ffn_grads[3],
                    cross_query_bias,
                    zero_row,
                    cross_bias,
                    zero_row,
                ]
            ),
            table_grad,
            ffn_grads[2].reshape(4, D),
        ],
        axis=0,
    )
    terms = (
        qkv_grad,
        out_weight_grad,
        ffn_grads[0],
        ffn_grads[1],
        query_weight_grad,
        cross_weight_grad,
        vector_grad,
    )
    return (middle_grad + residual_grad, terms, keyval_grad)


def on_device(
    video,
    segment_ids,
    timesteps,
    drop_mask,
    captions,
    null_caption,
    caption_weight,
    spatial_qkv,
    spatial_out,
    spatial_expand,
    spatial_shrink,
    spatial_vectors,
    temporal_qkv,
    temporal_out,
    temporal_expand,
    temporal_shrink,
    cross_query,
    cross_keyval,
    cross_out,
    temporal_vectors,
    cotangent,
):
    groups, frames, patches = video.shape[:3]
    size = lax.axis_size("sp")
    third = D
    wide = [
        spatial_qkv,
        spatial_out,
        spatial_expand,
        temporal_qkv,
        temporal_out,
        cross_query,
        cross_keyval,
        cross_out,
    ]

    def rounds_of(rows):
        cut = 512

        def block_round(qkv, out, start, width):
            return columns_round(
                (qkv, start, width),
                (qkv, third + start, width),
                (qkv, 2 * third + start, width),
                (out, start, width),
            )

        def expand_round(weight, late=False):
            quarter = FF // 4
            return columns_round(*[(weight, k * quarter, quarter) for k in range(4)], late=late)

        return [
            block_round(0, 1, 0, cut // 2),
            block_round(0, 1, cut // 2, cut // 2),
            block_round(0, 1, cut, third - cut),
            expand_round(2),
            rows_round(8, rows),
            columns_round((5, 0, third), (6, 0, third), (6, third, third), (7, 0, third)),
            block_round(3, 4, 0, third - cut),
            block_round(3, 4, third - cut, cut // 2),
            block_round(3, 4, third - cut // 2, cut // 2),
        ]

    (
        full_sqkv,
        full_sout,
        full_sexp,
        full_tqkv,
        full_tout,
        full_cq,
        full_ckv,
        full_cout,
        full_sshr,
        all_vectors,
    ) = gather_all(
        [spatial_shrink],
        wide,
        jnp.concatenate([spatial_vectors, temporal_vectors], axis=0),
        rounds_of,
        0,
    )
    full_sqkv, expand_shard, shrink_shard = lax.optimization_barrier(
        (full_sqkv, temporal_expand, temporal_shrink)
    )
    full_texp = lax.all_gather(expand_shard, "sp", axis=0, tiled=True)
    full_tshr = lax.all_gather(shrink_shard, "sp", axis=0, tiled=True)
    n_spatial = spatial_vectors.shape[0]
    spatial = (full_sqkv, full_sout, full_sexp, full_sshr, all_vectors[:n_spatial])
    temporal = (
        full_tqkv,
        full_tout,
        full_texp,
        full_tshr,
        full_cq,
        full_ckv,
        full_cout,
        all_vectors[n_spatial:],
    )
    dropped = (drop_mask > 0).astype(jnp.float32)
    text_local = jnp.where(drop_mask[:, :, None, None] > 0, null_caption[None, None], captions)
    text_rows = text_local.reshape(groups, CLIPS * CAP, -1)
    caption_sum = lax.psum(project(text_rows, caption_weight).astype(jnp.float32), "sp")
    caption_sum, first = lax.optimization_barrier((caption_sum, spatial[0]))
    spatial = (first, *spatial[1:])
    frame_mod = frame_modulation(segment_ids, timesteps).reshape(groups, frames, 6, D)
    same_clip = (segment_ids[:, :, None] == segment_ids[:, None, :])[:, None, None]
    row_clip = jnp.arange(CLIPS * CAP) // CAP
    allowed = (segment_ids[:, :, None] == row_clip[None, None, :])[:, :, None, None, :]
    residual = video.astype(jnp.float32)
    middle, spatial_kept = spatial_forward(residual, spatial, frame_mod)
    context = (caption_sum + as_float(temporal[7])[7]).astype(jnp.bfloat16)
    result, temporal_kept = temporal_forward(
        middle, temporal, frame_mod, same_clip, allowed, context
    )
    output = result.astype(jnp.bfloat16)
    middle_grad, temporal_terms, keyval_grad = temporal_backward(
        cotangent.astype(jnp.float32),
        middle,
        temporal,
        frame_mod,
        same_clip,
        allowed,
        temporal_kept,
    )
    shard_rows = D // lax.axis_size("sp")
    first_row = lax.axis_index("sp") * shard_rows
    video_grad, spatial_terms = spatial_backward(
        middle_grad, residual, spatial, frame_mod, spatial_kept
    )
    spatial_sums, temporal_sums, cross_sums, vector_total = scatter_all(
        (
            (spatial_terms[2], spatial_terms[3], spatial_terms[0], spatial_terms[1]),
            (temporal_terms[2], temporal_terms[3], temporal_terms[0], temporal_terms[1]),
            (temporal_terms[4], temporal_terms[5]),
        ),
        jnp.concatenate([spatial_terms[4], temporal_terms[6]], axis=0),
    )
    vector_total = lax.dynamic_slice_in_dim(vector_total, first_row, shard_rows, 1)
    keyval_grad, vector_total = lax.optimization_barrier((keyval_grad, vector_total))
    context_grad = input_grad(keyval_grad, temporal[5]).astype(jnp.bfloat16)
    local_context = lax.dynamic_slice_in_dim(context, first_row, shard_rows, 2)
    keyval_weight_grad = weight_grad(local_context, keyval_grad)
    value_bias_full = column_sum(keyval_grad).reshape(HEADS, 2, HEAD_DIM)[:, 1].reshape(D)
    caption_bias_full = column_sum(context_grad)
    caption_weight_grad = weight_grad(text_rows, context_grad)
    text_grad = input_grad(context_grad, caption_weight).reshape(groups, CLIPS, CAP, -1)
    null_grad = jnp.sum(text_grad * dropped[:, :, None, None], axis=(0, 1))
    own_rows = [
        lax.dynamic_slice_in_dim(row, first_row, shard_rows, 0)
        for row in (value_bias_full, caption_bias_full)
    ]
    width = null_grad.shape[1]
    flat = jnp.stack([jnp.pad(row, (0, width - shard_rows)) for row in own_rows])
    small_total = sum_seq(jnp.concatenate([null_grad, flat], axis=0))
    null_total = small_total[: null_grad.shape[0]]
    bias_total = small_total[null_grad.shape[0] :, :shard_rows]
    vector_total = vector_total.at[n_spatial + 5].add(bias_total[0])
    vector_total = vector_total.at[n_spatial + 7].add(bias_total[1])
    return (
        output,
        video_grad.astype(jnp.bfloat16),
        null_total,
        sum_seq(caption_weight_grad),
        spatial_sums[2],
        spatial_sums[3],
        spatial_sums[0],
        spatial_sums[1],
        vector_total[:n_spatial],
        temporal_sums[2],
        temporal_sums[3],
        temporal_sums[0],
        temporal_sums[1],
        cross_sums[0],
        sum_seq(keyval_weight_grad),
        cross_sums[1],
        vector_total[n_spatial:],
    )


def solution(mesh):
    return jax.shard_map(
        on_device,
        mesh=mesh,
        in_specs=(
            P("seq", None, "sp", None),
            P("seq", None),
            P("seq", None),
            P("seq", None),
            P("seq", None, None, "sp"),
            P(None, "sp"),
            P("sp", None),
            P("sp", None),
            P("sp", None),
            P("sp", None),
            P("sp", None),
            P(None, "sp"),
            P("sp", None),
            P("sp", None),
            P("sp", None),
            P("sp", None),
            P("sp", None),
            P("sp", None),
            P("sp", None),
            P(None, "sp"),
            P("seq", None, "sp", None),
        ),
        out_specs=(
            P("seq", None, "sp", None),
            P("seq", None, "sp", None),
            P(None, "sp"),
            P("sp", None),
            P("sp", None),
            P("sp", None),
            P("sp", None),
            P("sp", None),
            P(None, "sp"),
            P("sp", None),
            P("sp", None),
            P("sp", None),
            P("sp", None),
            P("sp", None),
            P("sp", None),
            P("sp", None),
            P(None, "sp"),
        ),
        check_vma=False,
    )
```
